32 devices in a mesh: blk: 16 (over z, y, x), beamk: 2 (over core).
Axes of the slice: x: 2, y: 2, z: 4, core: 2. Of those that a mesh axis runs over, the one named last changes fastest.
Arguments:
- sky: bfloat16 [32, 3072, 384], P('blk', 'beamk'), may hold values from -6 to 6
- beam: float32 [40, 2, 3072], P('beamk'), may hold values from -6 to 6
- wigner: bfloat16 [32, 40, 16, 3072], P('blk', 'beamk'), may hold values from -0.109375 to 0.109375
- m_list: int32 [32], P('blk'), may hold values from 0 to 3071, as said below
Outputs:
- cycle_coeffs: bfloat16 [16, 32, 40, 384], P('blk', None, 'beamk')
The draws below stay inside these ranges and needn't reach their ends.
Inputs may be any that keep to these rules, and one draw needn't show every extreme that they name: `m_list`: entries 2i and 2i+1 hold m and 3071-m for some m below 1536; all entries are distinct, and some slot holds 0.
All inputs are finite; a program needn't handle non-finite values.
Results may differ from the reference program's by a relative error of at most 0.0049.
Values may be sent and summed in bfloat16 or wider, within the bound.
No kernel may reach another device: no remote copies, remote signals or barrier semaphores. Data moves between devices by JAX's collectives and lax.ppermute only.
A program may use at most 64 MiB of HBM per device.

```python
import jax
import jax.numpy as jnp
from jax import lax

L = 3072
KB = 40
SIMS = 192
MW = 32
CYCLES = 16


def draw_m_list(key, part):
    perm_key, order_key = jax.random.split(key)
    pair_count = MW // 2
    others = jax.random.permutation(perm_key, L // 2 - 1)[:pair_count - 1] + 1
    chosen = jnp.concatenate([jnp.zeros((1,), jnp.int32), others.astype(jnp.int32)])
    chosen = jax.random.permutation(order_key, chosen)
    return jnp.stack([chosen, L - 1 - chosen], axis=1).reshape(-1).astype(jnp.int32)


def levels(own_key, shape, cuts, low, top_value):
    loudness = 1.0
    for axis_at, shards_of in cuts:
        heights = jax.random.uniform(jax.random.fold_in(jax.random.fold_in(own_key, 6), axis_at), (shards_of,), jnp.float32, low / len(cuts), top_value / len(cuts))
        loudness = loudness * jnp.repeat(jnp.exp(heights), shape[axis_at] // shards_of).reshape((-1,) + (1,) * (len(shape) - 1 - axis_at))
    return loudness


def centred(key, extent, spread, bound, cuts=(), kind=jnp.bfloat16):
    gain = levels(key, extent, cuts, -0.22, 0.18) if cuts else 1.0
    entries = jax.random.normal(key, extent, jnp.float32) * spread * gain
    return jnp.minimum(jnp.maximum(entries, -bound), bound).astype(kind)


def setup_inputs(seed: int = 0) -> dict:
    key_of = jax.random.split(jax.random.key(seed), 5)
    return {
        "sky": centred(key_of[0], (MW, L, 2 * SIMS), 1.0, 6.0, ((0, 16), (1, 2))),
        "beam": centred(key_of[1], (KB, 2, L), 1.0, 6.0, ((0, 2),), jnp.float32),
        "wigner": centred(key_of[2], (MW, KB, CYCLES, L), L ** -0.5, 0.109375, ((0, 16), (1, 2))),
        "m_list": draw_m_list(jax.random.fold_in(key_of[4], 71), 0),
    }


def reference(sky, beam, wigner, m_list):
    k_offset = KB // 2
    k_absolute = jnp.abs(jnp.arange(KB, dtype=jnp.int32) - k_offset)
    degrees = jnp.arange(L, dtype=jnp.int32)
    beam_re = beam[:, 0, :]
    beam_im = beam[:, 1, :]

    def one_slot(operands):
        sky_slot, wigner_slot, m_value = operands
        sky_re = sky_slot[:, :SIMS].astype(jnp.float32)
        sky_im = sky_slot[:, SIMS:].astype(jnp.float32)
        lowest = jnp.maximum(m_value, k_absolute)
        inside = degrees[None, :] >= lowest[:, None]
        prod_re = sky_re[None] * beam_re[:, :, None] - sky_im[None] * beam_im[:, :, None]
        prod_im = sky_re[None] * beam_im[:, :, None] + sky_im[None] * beam_re[:, :, None]
        product = jnp.concatenate([prod_re, prod_im], axis=-1)
        product = jnp.where(inside[:, :, None], product, jnp.zeros_like(product)).astype(jnp.bfloat16)
        summed = jnp.einsum("krl,kls->rks", wigner_slot.astype(jnp.float32), product.astype(jnp.float32))
        return summed.astype(jnp.bfloat16)

    stacked = lax.map(one_slot, (sky, wigner, m_list))
    return jnp.transpose(stacked, (1, 0, 2, 3))
```

```python
import functools

import jax
import jax.numpy as jnp
from jax import lax
from jax.experimental import pallas as pl
from jax.experimental.pallas import tpu as pltpu
from jax.sharding import PartitionSpec as P

KB = 40


def tile_of(rows):
    return max(t for t in range(128, min(rows, 512) + 1, 128) if rows % t == 0)


def combine(acc, width):
    re_rows = acc.shape[0] // 2
    first = acc[:re_rows]
    second = acc[re_rows:]
    half = width // 2
    swapped = pltpu.roll(second, half, 1)
    column = lax.broadcasted_iota(jnp.int32, swapped.shape, 1)
    return first + jnp.where(column < half, -swapped, swapped)


def kernel(tile, tiles, initial, final, meta, *refs):
    if initial:
        sky_ref, wigner_ref, beam_ref, out_ref, factor, acc = refs[:6]
        rest = refs[6:]
    else:
        sky_ref, wigner_ref, beam_ref, before_ref, out_ref, factor, acc = refs[:7]
        rest = refs[7:]
    slot, step = pl.program_id(0), pl.program_id(1)
    slots = pl.num_programs(0)
    k_local, cycles = wigner_ref.shape[1], wigner_ref.shape[2]
    rows = k_local * cycles
    m_value = meta[2 + slot]
    first_tile = meta[4 + slot]

    @pl.when(step == 0)
    def _():
        acc[...] = jnp.zeros_like(acc)

    @pl.when(step >= first_tile)
    def _():
        degrees = meta[0] + step * tile + lax.broadcasted_iota(jnp.int32, (1, tile), 1)
        for k in range(k_local):
            lowest = jnp.maximum(m_value, jnp.abs(meta[1] + k))
            inside = degrees >= lowest
            w = wigner_ref[0, k].astype(jnp.float32)
            beam_re = jnp.where(inside, beam_ref[k, 0:1, :], 0.0)
            beam_im = jnp.where(inside, beam_ref[k, 1:2, :], 0.0)
            factor[k * cycles : (k + 1) * cycles, :] = (w * beam_re).astype(jnp.bfloat16)
            factor[rows + k * cycles : rows + (k + 1) * cycles, :] = (w * beam_im).astype(jnp.bfloat16)
        acc[...] += jnp.dot(factor[...], sky_ref[0], preferred_element_type=jnp.float32)

    @pl.when(step == tiles - 1)
    def _():
        total = combine(acc[...], acc.shape[1])
        if not initial:
            total = total + before_ref[0]
        if final:
            turned = rest[0]
            for lanes in range(turned.shape[0]):
                span = slice(lanes * 128, (lanes + 1) * 128)
                for k in range(k_local):
                    turned[lanes, pl.ds(k, cycles, stride=k_local), :] = total[k * cycles : (k + 1) * cycles, span]
                out_ref[0, :, span] = turned[lanes].astype(out_ref.dtype)
        else:
            out_ref[0] = total


def add_piece(sky, wigner, beam, meta, before, final):
    slots, piece_rows, columns = sky.shape
    _, k_local, cycles, _ = wigner.shape
    rows = k_local * cycles
    tile = tile_of(piece_rows)
    tiles = piece_rows // tile

    def at(slot, step, meta):
        return jnp.minimum(jnp.maximum(step, meta[4 + slot]), tiles - 1)

    in_specs = [
        pl.BlockSpec((1, tile, columns), lambda s, t, meta: (s, at(s, t, meta), 0)),
        pl.BlockSpec((1, k_local, cycles, tile), lambda s, t, meta: (s, 0, 0, meta[6] + at(s, t, meta))),
        pl.BlockSpec((k_local, 2, tile), lambda s, t, meta: (0, 0, meta[6] + at(s, t, meta))),
    ]
    operands = [sky, wigner, beam]
    block = pl.BlockSpec((1, rows, columns), lambda s, t, meta: (s, 0, 0))
    if before is not None:
        in_specs.append(block)
        operands.append(before)
    scratch = [
        pltpu.VMEM((2 * rows, tile), jnp.bfloat16),
        pltpu.VMEM((2 * rows, columns), jnp.float32),
    ]
    if final:
        scratch.append(pltpu.VMEM((columns // 128, rows, 128), jnp.float32))
    return pl.pallas_call(
        functools.partial(kernel, tile, tiles, before is None, final),
        out_shape=jax.ShapeDtypeStruct((slots, rows, columns), jnp.bfloat16 if final else jnp.float32),
        grid_spec=pltpu.PrefetchScalarGridSpec(
            num_scalar_prefetch=1,
            grid=(slots, tiles),
            in_specs=in_specs,
            out_specs=block,
            scratch_shapes=scratch,
        ),
        compiler_params=pltpu.CompilerParams(vmem_limit_bytes=24 * 1024 * 1024),
        cost_estimate=pl.CostEstimate(
            flops=2 * slots * 2 * rows * piece_rows * columns // 2,
            bytes_accessed=2 * slots * (rows + columns) * piece_rows // 2,
            transcendentals=0,
        ),
        name="convolve_last" if final else "convolve",
    )(meta, *operands)


def local(sky, beam, wigner, m_list, *, ways):
    slots, piece_rows, columns = sky.shape
    k_local, cycles = wigner.shape[1], wigner.shape[2]
    tile = tile_of(piece_rows)
    tiles = piece_rows // tile
    me = lax.axis_index("beamk")
    first_k = me * k_local - KB // 2

    def meta_of(owner):
        first_tile = jnp.clip((m_list - owner * piece_rows) // tile, 0, tiles)
        return jnp.concatenate(
            [
                jnp.stack([owner * piece_rows, first_k]),
                m_list,
                first_tile,
                (owner * tiles)[None],
            ]
        ).astype(jnp.int32)

    pieces = [sky]
    for shift in range(1, ways):
        perm = [(c, (c + shift) % ways) for c in range(ways)]
        pieces.append(lax.ppermute(sky, "beamk", perm))
    total = None
    for shift, piece in enumerate(pieces):
        owner = lax.rem(me - shift + ways, ways)
        total = add_piece(piece, wigner, beam, meta_of(owner), total, shift == ways - 1)
    parts = total.reshape(slots, cycles, k_local, columns).transpose(1, 0, 2, 3)
    parts = parts.reshape(cycles, slots * k_local, columns)
    received = lax.all_to_all(parts, "blk", split_axis=0, concat_axis=0, tiled=True)
    return received.reshape(1, -1, k_local, columns)


def solution(mesh):
    in_specs = (
        P("blk", "beamk", None),
        P("beamk", None, None),
        P("blk", "beamk", None, None),
        P("blk"),
    )
    out_specs = P("blk", None, "beamk", None)
    body = functools.partial(local, ways=mesh.shape["beamk"])
    return jax.shard_map(body, mesh=mesh, in_specs=in_specs, out_specs=out_specs, check_vma=False)
```

```python
import functools

import jax
import jax.numpy as jnp
from jax import lax
from jax.experimental import pallas as pl
from jax.experimental.pallas import tpu as pltpu
from jax.sharding import PartitionSpec as P

KB = 40
LANES = 128
VMEM_LIMIT = 24 * 1024 * 1024


def tile_of(rows):
    return max(t for t in range(LANES, min(rows, 512) + 1, LANES) if rows % t == 0)


def whole(memory):
    return pl.BlockSpec(memory_space=memory)


def combine(acc):
    rows = acc.shape[0] // 2
    half = acc.shape[1] // 2
    swapped = pltpu.roll(acc[rows:], half, 1)
    column = lax.broadcasted_iota(jnp.int32, swapped.shape, 1)
    return acc[:rows] + jnp.where(column < half, -swapped, swapped)


def owner_of(distance, ways):
    return lax.rem(lax.axis_index("beamk") - distance + ways, ways)


def first_tile(m_value, owner, piece_rows, tile):
    return jnp.minimum(jnp.maximum(m_value - owner * piece_rows, 0) // tile, piece_rows // tile)


def first_kernel(ways, tile, m_ref, sky, wigner, beam, part, factors, sky_in, wigner_in, beam_in, own, acc, sky_sem, wigner_sem, beam_sem):
    slots, piece_rows, _ = sky.shape
    k_local, cycles = wigner.shape[1], wigner.shape[2]
    rows = k_local * cycles
    tiles = piece_rows // tile
    first_k = lax.axis_index("beamk") * k_local - KB // 2

    def beam_copy():
        return pltpu.make_async_copy(beam, beam_in, beam_sem)

    def sky_copy(slot, step):
        span = pl.ds(pl.multiple_of(step * tile, tile), tile)
        return pltpu.make_async_copy(sky.at[slot, span], sky_in.at[slot, step], sky_sem.at[slot, step])

    def wigner_copy(distance, slot, step):
        start = pl.multiple_of(owner_of(distance, ways) * piece_rows + step * tile, tile)
        return pltpu.make_async_copy(
            wigner.at[slot, :, :, pl.ds(start, tile)],
            wigner_in.at[distance, slot, step],
            wigner_sem.at[distance, slot, step],
        )

    def begin(distance, slot):
        return first_tile(m_ref[slot], owner_of(distance, ways), piece_rows, tile)

    def fill(target, distance, slot, step):
        start = pl.multiple_of(owner_of(distance, ways) * piece_rows + step * tile, tile)
        degrees = start + lax.broadcasted_iota(jnp.int32, (1, tile), 1)
        for k in range(k_local):
            lowest = jnp.maximum(m_ref[slot], jnp.abs(first_k + k))
            inside = degrees >= lowest
            values = wigner_in[distance, slot, step, k].astype(jnp.float32)
            beam_re = jnp.where(inside, beam_in[k, 0:1, pl.ds(start, tile)], 0.0)
            beam_im = jnp.where(inside, beam_in[k, 1:2, pl.ds(start, tile)], 0.0)
            target[k * cycles : (k + 1) * cycles, :] = (values * beam_re).astype(jnp.bfloat16)
            target[rows + k * cycles : rows + (k + 1) * cycles, :] = (values * beam_im).astype(jnp.bfloat16)

    beam_copy().start()
    for slot in range(slots):

        @pl.loop(begin(0, slot), tiles)
        def _(step):
            wigner_copy(0, slot, step).start()
            sky_copy(slot, step).start()

    for distance in range(1, ways):
        for slot in range(slots):

            @pl.loop(begin(distance, slot), tiles)
            def _(step):
                wigner_copy(distance, slot, step).start()

    beam_copy().wait()
    for slot in range(slots):
        acc[...] = jnp.zeros_like(acc)

        @pl.loop(begin(0, slot), tiles)
        def _(step):
            wigner_copy(0, slot, step).wait()
            fill(own, 0, slot, step)
            sky_copy(slot, step).wait()
            acc[...] += jnp.dot(own[...], sky_in[slot, step], preferred_element_type=jnp.float32)

        part[slot] = combine(acc[...])
    for distance in range(1, ways):
        for slot in range(slots):

            @pl.loop(begin(distance, slot), tiles)
            def _(step):
                wigner_copy(distance, slot, step).wait()
                fill(factors.at[distance - 1, slot, step], distance, slot, step)


def second_kernel(ways, peers, tile, m_ref, part, factors, *refs):
    pieces, refs = refs[: ways - 1], refs[ways - 1 :]
    outs, refs = refs[:peers], refs[peers:]
    acc, turned = refs
    slots, rows, columns = part.shape
    piece_rows = pieces[0].shape[1]
    tiles = piece_rows // tile
    width = outs[0].shape[0]
    k_local = width // slots
    cycles = rows // k_local
    for slot in range(slots):
        acc[...] = jnp.zeros_like(acc)
        for distance in range(1, ways):
            begin = first_tile(m_ref[slot], owner_of(distance, ways), piece_rows, tile)

            @pl.loop(begin, tiles)
            def _(step):
                span = pl.ds(pl.multiple_of(step * tile, tile), tile)
                acc[...] += jnp.dot(
                    factors[distance - 1, slot, step], pieces[distance - 1][slot, span], preferred_element_type=jnp.float32
                )

        total = part[slot] + combine(acc[...])
        for lane in range(columns // LANES):
            for k in range(k_local):
                turned[lane, pl.ds(slot * k_local + k, cycles, stride=width), :] = total[
                    k * cycles : (k + 1) * cycles, lane * LANES : (lane + 1) * LANES
                ]
    me = lax.axis_index("blk")
    for distance in range(peers):
        cycle = me ^ distance
        for lane in range(columns // LANES):
            outs[distance][:, lane * LANES : (lane + 1) * LANES] = turned[lane, pl.ds(cycle * width, width), :].astype(jnp.bfloat16)


def third_kernel(slots, peers, *refs):
    ins, (out, stage, turned) = refs[:peers], refs[peers:]
    k_local, slot_count, columns = out.shape
    me = lax.axis_index("blk")
    for distance in range(peers):
        source = me ^ distance
        for lane in range(columns // LANES):
            stage[distance, lane] = ins[distance][:, lane * LANES : (lane + 1) * LANES].astype(jnp.float32)
            for slot in range(slots):
                turned[lane, pl.ds(slots * source + slot, k_local, stride=slot_count), :] = stage[
                    distance, lane, slot * k_local : (slot + 1) * k_local
                ]
    for lane in range(columns // LANES):
        for k in range(k_local):
            out[k, :, lane * LANES : (lane + 1) * LANES] = turned[lane, k * slot_count : (k + 1) * slot_count].astype(out.dtype)


def local(sky, beam, wigner, m_list, *, ways, peers):
    slots, piece_rows, columns = sky.shape
    _, k_local, cycles, degrees = wigner.shape
    rows = k_local * cycles
    tile = tile_of(piece_rows)
    tiles = piece_rows // tile
    lane_tiles = columns // LANES
    width = slots * k_local
    params = pltpu.CompilerParams(vmem_limit_bytes=VMEM_LIMIT)

    pieces = []
    for shift in range(1, ways):
        perm = [(c, (c + shift) % ways) for c in range(ways)]
        pieces.append(pltpu.with_memory_space_constraint(lax.ppermute(sky, "beamk", perm), pltpu.VMEM))
    sky, beam, wigner, m_list = (pltpu.with_memory_space_constraint(x, pltpu.HBM) for x in (sky, beam, wigner, m_list))

    part, factors = pl.pallas_call(
        functools.partial(first_kernel, ways, tile),
        out_shape=(
            pltpu.VMEM((slots, rows, columns), jnp.float32),
            pltpu.VMEM((ways - 1, slots, tiles, 2 * rows, tile), jnp.bfloat16),
        ),
        in_specs=[whole(pltpu.SMEM), whole(pltpu.HBM), whole(pltpu.HBM), whole(pltpu.HBM)],
        out_specs=(whole(pltpu.VMEM), whole(pltpu.VMEM)),
        scratch_shapes=[
            pltpu.VMEM((slots, tiles, tile, columns), jnp.bfloat16),
            pltpu.VMEM((ways, slots, tiles, k_local, cycles, tile), jnp.bfloat16),
            pltpu.VMEM(beam.shape, jnp.float32),
            pltpu.VMEM((2 * rows, tile), jnp.bfloat16),
            pltpu.VMEM((2 * rows, columns), jnp.float32),
            pltpu.SemaphoreType.DMA((slots, tiles)),
            pltpu.SemaphoreType.DMA((ways, slots, tiles)),
            pltpu.SemaphoreType.DMA,
        ],
        compiler_params=params,
        cost_estimate=pl.CostEstimate(
            flops=4 * slots * rows * piece_rows * columns, bytes_accessed=8 * 1024 * 1024, transcendentals=0
        ),
        name="own_half",
    )(m_list, sky, wigner, beam)

    blocks = pl.pallas_call(
        functools.partial(second_kernel, ways, peers, tile),
        out_shape=[pltpu.VMEM((width, columns), jnp.bfloat16)] * peers,
        in_specs=[whole(pltpu.SMEM)] + [whole(pltpu.VMEM)] * (ways + 1),
        out_specs=[whole(pltpu.VMEM)] * peers,
        scratch_shapes=[
            pltpu.VMEM((2 * rows, columns), jnp.float32),
            pltpu.VMEM((lane_tiles, cycles * width, LANES), jnp.float32),
        ],
        compiler_params=params,
        cost_estimate=pl.CostEstimate(
            flops=4 * slots * rows * piece_rows * columns, bytes_accessed=8 * 1024 * 1024, transcendentals=0
        ),
        name="other_half",
    )(m_list, part, factors, *pieces)

    received = [blocks[0]] + [None] * (peers - 1)
    for distance in reversed(range(1, peers)):
        perm = [(b, b ^ distance) for b in range(peers)]
        received[distance] = lax.ppermute(blocks[distance], "blk", perm)

    out = pl.pallas_call(
        functools.partial(third_kernel, slots, peers),
        out_shape=jax.ShapeDtypeStruct((k_local, slots * peers, columns), jnp.bfloat16),
        in_specs=[whole(pltpu.VMEM)] * peers,
        out_specs=whole(pltpu.VMEM),
        scratch_shapes=[
            pltpu.VMEM((peers, lane_tiles, width, LANES), jnp.float32),
            pltpu.VMEM((lane_tiles, k_local * slots * peers, LANES), jnp.float32),
        ],
        compiler_params=params,
        name="place_slots",
    )(*received)
    return out.transpose(1, 0, 2)[None]


def solution(mesh):
    in_specs = (
        P("blk", "beamk", None),
        P("beamk", None, None),
        P("blk", "beamk", None, None),
        P("blk"),
    )
    out_specs = P("blk", None, "beamk", None)
    body = functools.partial(local, ways=mesh.shape["beamk"], peers=mesh.shape["blk"])
    return jax.shard_map(body, mesh=mesh, in_specs=in_specs, out_specs=out_specs, check_vma=False)
```

```python
import functools

import jax
import jax.numpy as jnp
from jax import lax
from jax.experimental import pallas as pl
from jax.experimental.pallas import tpu as pltpu
from jax.sharding import PartitionSpec as P

KB = 40
LANES = 128
VMEM_LIMIT = 24 * 1024 * 1024


def tile_of(rows):
    return max(t for t in range(LANES, min(rows, 512) + 1, LANES) if rows % t == 0)


def whole(memory):
    return pl.BlockSpec(memory_space=memory)


def combine(acc):
    rows = acc.shape[0] // 2
    half = acc.shape[1] // 2
    swapped = pltpu.roll(acc[rows:], half, 1)
    column = lax.broadcasted_iota(jnp.int32, swapped.shape, 1)
    return acc[:rows] + jnp.where(column < half, -swapped, swapped)


def owner_of(distance, ways):
    return lax.rem(lax.axis_index("beamk") - distance + ways, ways)


def first_tile(m_value, owner, piece_rows, tile):
    return jnp.minimum(jnp.maximum(m_value - owner * piece_rows, 0) // tile, piece_rows // tile)


def first_kernel(ways, tile, m_ref, sky, wigner, beam, part, factors, sky_in, wigner_in, beam_in, own, acc, sky_sem, wigner_sem, beam_sem):
    slots, piece_rows, _ = sky.shape
    k_local, cycles = wigner.shape[1], wigner.shape[2]
    rows = k_local * cycles
    tiles = piece_rows // tile
    first_k = lax.axis_index("beamk") * k_local - KB // 2

    def beam_copy():
        return pltpu.make_async_copy(beam, beam_in, beam_sem)

    def sky_copy(slot, step):
        span = pl.ds(pl.multiple_of(step * tile, tile), tile)
        return pltpu.make_async_copy(sky.at[slot, span], sky_in.at[slot, step], sky_sem.at[slot, step])

    def wigner_copy(distance, slot, step):
        start = pl.multiple_of(owner_of(distance, ways) * piece_rows + step * tile, tile)
        return pltpu.make_async_copy(
            wigner.at[slot, :, :, pl.ds(start, tile)],
            wigner_in.at[distance, slot, step],
            wigner_sem.at[distance, slot, step],
        )

    def begin(distance, slot):
        return first_tile(m_ref[slot], owner_of(distance, ways), piece_rows, tile)

    def fill(target, distance, slot, step):
        start = pl.multiple_of(owner_of(distance, ways) * piece_rows + step * tile, tile)
        degrees = start + lax.broadcasted_iota(jnp.int32, (1, tile), 1)
        for k in range(k_local):
            lowest = jnp.maximum(m_ref[slot], jnp.abs(first_k + k))
            inside = degrees >= lowest
            values = wigner_in[distance, slot, step, k].astype(jnp.float32)
            beam_re = jnp.where(inside, beam_in[k, 0:1, pl.ds(start, tile)], 0.0)
            beam_im = jnp.where(inside, beam_in[k, 1:2, pl.ds(start, tile)], 0.0)
            target[k * cycles : (k + 1) * cycles, :] = (values * beam_re).astype(jnp.bfloat16)
            target[rows + k * cycles : rows + (k + 1) * cycles, :] = (values * beam_im).astype(jnp.bfloat16)

    beam_copy().start()
    for slot in range(slots):

        @pl.loop(begin(0, slot), tiles)
        def _(step):
            wigner_copy(0, slot, step).start()
            sky_copy(slot, step).start()

    for distance in range(1, ways):
        for slot in range(slots):

            @pl.loop(begin(distance, slot), tiles)
            def _(step):
                wigner_copy(distance, slot, step).start()

    beam_copy().wait()
    for slot in range(slots):
        acc[...] = jnp.zeros_like(acc)

        @pl.loop(begin(0, slot), tiles)
        def _(step):
            wigner_copy(0, slot, step).wait()
            fill(own, 0, slot, step)
            sky_copy(slot, step).wait()
            acc[...] += jnp.dot(own[...], sky_in[slot, step], preferred_element_type=jnp.float32)

        part[slot] = combine(acc[...])
    for distance in range(1, ways):
        for slot in range(slots):

            @pl.loop(begin(distance, slot), tiles)
            def _(step):
                wigner_copy(distance, slot, step).wait()
                fill(factors.at[distance - 1, slot, step], distance, slot, step)


def second_kernel(ways, tile, m_ref, part, factors, *refs):
    pieces, (out, acc, turned) = refs[: ways - 1], refs[ways - 1 :]
    slots, rows, columns = part.shape
    piece_rows = pieces[0].shape[1]
    tiles = piece_rows // tile
    cycles, width, _ = out.shape
    k_local = width // slots
    for slot in range(slots):
        acc[...] = jnp.zeros_like(acc)
        for distance in range(1, ways):
            begin = first_tile(m_ref[slot], owner_of(distance, ways), piece_rows, tile)

            @pl.loop(begin, tiles)
            def _(step):
                span = pl.ds(pl.multiple_of(step * tile, tile), tile)
                acc[...] += jnp.dot(
                    factors[distance - 1, slot, step], pieces[distance - 1][slot, span], preferred_element_type=jnp.float32
                )

        total = part[slot] + combine(acc[...])
        for lane in range(columns // LANES):
            for k in range(k_local):
                turned[lane, pl.ds(slot * k_local + k, cycles, stride=width), :] = total[
                    k * cycles : (k + 1) * cycles, lane * LANES : (lane + 1) * LANES
                ]
    for cycle in range(cycles):
        for lane in range(columns // LANES):
            out[cycle, :, lane * LANES : (lane + 1) * LANES] = turned[lane, cycle * width : (cycle + 1) * width].astype(out.dtype)


def local(sky, beam, wigner, m_list, *, ways):
    slots, piece_rows, columns = sky.shape
    _, k_local, cycles, degrees = wigner.shape
    rows = k_local * cycles
    tile = tile_of(piece_rows)
    tiles = piece_rows // tile
    lane_tiles = columns // LANES
    width = slots * k_local
    params = pltpu.CompilerParams(vmem_limit_bytes=VMEM_LIMIT)

    pieces = []
    for shift in range(1, ways):
        perm = [(c, (c + shift) % ways) for c in range(ways)]
        pieces.append(pltpu.with_memory_space_constraint(lax.ppermute(sky, "beamk", perm), pltpu.VMEM))
    sky, beam, wigner, m_list = (pltpu.with_memory_space_constraint(x, pltpu.HBM) for x in (sky, beam, wigner, m_list))

    part, factors = pl.pallas_call(
        functools.partial(first_kernel, ways, tile),
        out_shape=(
            pltpu.VMEM((slots, rows, columns), jnp.float32),
            pltpu.VMEM((ways - 1, slots, tiles, 2 * rows, tile), jnp.bfloat16),
        ),
        in_specs=[whole(pltpu.SMEM), whole(pltpu.HBM), whole(pltpu.HBM), whole(pltpu.HBM)],
        out_specs=(whole(pltpu.VMEM), whole(pltpu.VMEM)),
        scratch_shapes=[
            pltpu.VMEM((slots, tiles, tile, columns), jnp.bfloat16),
            pltpu.VMEM((ways, slots, tiles, k_local, cycles, tile), jnp.bfloat16),
            pltpu.VMEM(beam.shape, jnp.float32),
            pltpu.VMEM((2 * rows, tile), jnp.bfloat16),
            pltpu.VMEM((2 * rows, columns), jnp.float32),
            pltpu.SemaphoreType.DMA((slots, tiles)),
            pltpu.SemaphoreType.DMA((ways, slots, tiles)),
            pltpu.SemaphoreType.DMA,
        ],
        compiler_params=params,
        cost_estimate=pl.CostEstimate(
            flops=4 * slots * rows * piece_rows * columns, bytes_accessed=8 * 1024 * 1024, transcendentals=0
        ),
        name="own_half",
    )(m_list, sky, wigner, beam)

    blocks = pl.pallas_call(
        functools.partial(second_kernel, ways, tile),
        out_shape=pltpu.VMEM((cycles, width, columns), jnp.bfloat16),
        in_specs=[whole(pltpu.SMEM)] + [whole(pltpu.VMEM)] * (ways + 1),
        out_specs=whole(pltpu.VMEM),
        scratch_shapes=[
            pltpu.VMEM((2 * rows, columns), jnp.float32),
            pltpu.VMEM((lane_tiles, cycles * width, LANES), jnp.float32),
        ],
        compiler_params=params,
        cost_estimate=pl.CostEstimate(
            flops=4 * slots * rows * piece_rows * columns, bytes_accessed=8 * 1024 * 1024, transcendentals=0
        ),
        name="other_half",
    )(m_list, part, factors, *pieces)
    received = lax.all_to_all(blocks, "blk", split_axis=0, concat_axis=0, tiled=True)
    return received.reshape(1, -1, k_local, columns)


def solution(mesh):
    in_specs = (
        P("blk", "beamk", None),
        P("beamk", None, None),
        P("blk", "beamk", None, None),
        P("blk"),
    )
    out_specs = P("blk", None, "beamk", None)
    body = functools.partial(local, ways=mesh.shape["beamk"])
    return jax.shard_map(body, mesh=mesh, in_specs=in_specs, out_specs=out_specs, check_vma=False)
```

```python
import functools

import jax
import jax.numpy as jnp
from jax import lax
from jax.experimental import pallas as pl
from jax.experimental.pallas import tpu as pltpu
from jax.sharding import PartitionSpec as P

KB = 40
LANES = 128
VMEM_LIMIT = 24 * 1024 * 1024


def tile_of(rows):
    return max(t for t in range(LANES, min(rows, 512) + 1, LANES) if rows % t == 0)


def whole(memory):
    return pl.BlockSpec(memory_space=memory)


def turn_by_i(rows):
    half = rows.shape[1] // 2
    swapped = pltpu.roll(rows, half, 1)
    column = lax.broadcasted_iota(jnp.int32, swapped.shape, 1)
    return jnp.where(column < half, -swapped, swapped)


def owner_of(distance, ways):
    return lax.rem(lax.axis_index("beamk") - distance + ways, ways)


def first_tile(m_value, owner, piece_rows, tile):
    return jnp.minimum(jnp.maximum(m_value - owner * piece_rows, 0) // tile, piece_rows // tile)


def first_kernel(ways, tile, m_ref, sky, wigner, beam, part, factors, sky_in, wigner_in, beam_in, even, odd, acc, sky_sem, wigner_sem, beam_sem):
    slots, piece_rows, columns = sky.shape
    k_local, cycles = wigner.shape[1], wigner.shape[2]
    rows = k_local * cycles
    tiles = piece_rows // tile
    all_tiles = ways * tiles
    first_k = lax.axis_index("beamk") * k_local - KB // 2

    def beam_copy(index):
        span = pl.ds(pl.multiple_of(index * tile, tile), tile)
        return pltpu.make_async_copy(beam.at[:, :, span], beam_in.at[index], beam_sem.at[index])

    def sky_copy(slot, step):
        span = pl.ds(pl.multiple_of(step * tile, tile), tile)
        return pltpu.make_async_copy(sky.at[slot, span], sky_in.at[slot, step], sky_sem.at[slot, step])

    def wigner_copy(distance, slot, step):
        start = pl.multiple_of(owner_of(distance, ways) * piece_rows + step * tile, tile)
        return pltpu.make_async_copy(
            wigner.at[slot, :, :, pl.ds(start, tile)],
            wigner_in.at[distance, slot, step],
            wigner_sem.at[distance, slot, step],
        )

    def begin(distance, slot):
        return first_tile(m_ref[slot], owner_of(distance, ways), piece_rows, tile)

    def fill(target, distance, slot, step):
        index = owner_of(distance, ways) * tiles + step
        index = jnp.where(index == m_ref[slot] // tile, all_tiles + slot, index)
        for k in range(k_local):
            values = wigner_in[distance, slot, step, k].astype(jnp.float32)
            target[k * cycles : (k + 1) * cycles, :] = (values * beam_in[index, k, 0:1, :]).astype(jnp.bfloat16)
            target[rows + k * cycles : rows + (k + 1) * cycles, :] = (values * beam_in[index, k, 1:2, :]).astype(jnp.bfloat16)

    for index in range(all_tiles):
        beam_copy(index).start()
    for slot in range(slots):

        @pl.loop(begin(0, slot), tiles)
        def _(step):
            wigner_copy(0, slot, step).start()
            sky_copy(slot, step).start()

    for distance in range(1, ways):
        for slot in range(slots):

            @pl.loop(begin(distance, slot), tiles)
            def _(step):
                wigner_copy(distance, slot, step).start()

    acc[...] = jnp.zeros_like(acc)
    for index in range(all_tiles):
        beam_copy(index).wait()
    for slot in range(slots):
        index = m_ref[slot] // tile
        degrees = index * tile + lax.broadcasted_iota(jnp.int32, (2, tile), 1)
        for k in range(k_local):
            lowest = jnp.maximum(m_ref[slot], jnp.abs(first_k + k))
            beam_in[all_tiles + slot, k] = jnp.where(degrees >= lowest, beam_in[index, k], 0.0)

    starts = [begin(0, slot) for slot in range(slots)]
    ends = []
    for slot in range(slots):
        ends.append((ends[-1] if ends else 0) + tiles - starts[slot])
    count = ends[-1]

    def place(item):
        item = jnp.minimum(item, count - 1)
        slot = jnp.int32(0)
        step = item + starts[0]
        for later in range(1, slots):
            beyond = item >= ends[later - 1]
            slot = jnp.where(beyond, later, slot)
            step = jnp.where(beyond, item - ends[later - 1] + starts[later], step)
        return slot, step

    def arrive(item):
        @pl.when(item < count)
        def _():
            slot, step = place(item)
            wigner_copy(0, slot, step).wait()
            sky_copy(slot, step).wait()

    def work(item, present, other):
        arrive(item + 1)
        slot, step = place(item)
        fill(other, 0, *place(item + 1))
        acc[slot] += jnp.dot(present[...], sky_in[slot, step], preferred_element_type=jnp.float32)

    @pl.when(count > 0)
    def _():
        arrive(jnp.int32(0))
        fill(even, 0, *place(jnp.int32(0)))

        @pl.loop(0, (count + 1) // 2)
        def _(pair):
            work(2 * pair, even, odd)

            @pl.when(2 * pair + 1 < count)
            def _():
                work(2 * pair + 1, odd, even)

    for distance in range(1, ways):
        for slot in range(slots):

            @pl.loop(begin(distance, slot), tiles)
            def _(step):
                wigner_copy(distance, slot, step).wait()
                span = pl.ds(pl.multiple_of(step * tile, tile), tile)
                fill(factors.at[distance - 1, slot, :, span], distance, slot, step)

    @pl.loop(0, slots)
    def _(slot):
        for k in range(k_local):
            span = slice(k * cycles, (k + 1) * cycles)
            part[slot, span] = acc[slot, span] + turn_by_i(acc[slot, rows + k * cycles : rows + (k + 1) * cycles])


def second_kernel(ways, tile, m_ref, part, factors, *refs):
    pieces, (out, acc, turned) = refs[: ways - 1], refs[ways - 1 :]
    slots, rows, columns = part.shape
    piece_rows = pieces[0].shape[1]
    tiles = piece_rows // tile
    cycles, width, _ = out.shape
    k_local = width // slots

    @pl.loop(0, slots)
    def _(slot):
        for distance in range(1, ways):
            missing = first_tile(m_ref[slot], owner_of(distance, ways), piece_rows, tile)
            for skipped in range(tiles):

                @pl.when(missing == skipped)
                def _():
                    span = slice(skipped * tile, piece_rows)
                    term = jnp.dot(
                        factors[distance - 1, slot, :, span],
                        pieces[distance - 1][slot, span],
                        preferred_element_type=jnp.float32,
                    )
                    acc[...] = term if distance == 1 else acc[...] + term

            if distance == 1:

                @pl.when(missing == tiles)
                def _():
                    acc[...] = jnp.zeros_like(acc)

        for k in range(k_local):
            span = slice(k * cycles, (k + 1) * cycles)
            total = part[slot, span] + acc[span] + turn_by_i(acc[rows + k * cycles : rows + (k + 1) * cycles])
            for lane in range(columns // LANES):
                turned[lane, pl.ds(slot * k_local + k, cycles, stride=width), :] = total[:, lane * LANES : (lane + 1) * LANES]

    for cycle in range(cycles):
        for lane in range(columns // LANES):
            out[cycle, :, lane * LANES : (lane + 1) * LANES] = turned[lane, cycle * width : (cycle + 1) * width].astype(out.dtype)


def local(sky, beam, wigner, m_list, *, ways):
    slots, piece_rows, columns = sky.shape
    _, k_local, cycles, degrees = wigner.shape
    rows = k_local * cycles
    tile = tile_of(piece_rows)
    tiles = piece_rows // tile
    lane_tiles = columns // LANES
    width = slots * k_local
    params = pltpu.CompilerParams(vmem_limit_bytes=VMEM_LIMIT)

    pieces = []
    for shift in range(1, ways):
        perm = [(c, (c + shift) % ways) for c in range(ways)]
        pieces.append(pltpu.with_memory_space_constraint(lax.ppermute(sky, "beamk", perm), pltpu.VMEM))
    sky, beam, wigner, m_list = (pltpu.with_memory_space_constraint(x, pltpu.HBM) for x in (sky, beam, wigner, m_list))

    part, factors = pl.pallas_call(
        functools.partial(first_kernel, ways, tile),
        out_shape=(
            pltpu.VMEM((slots, rows, columns), jnp.float32),
            pltpu.VMEM((ways - 1, slots, 2 * rows, piece_rows), jnp.bfloat16),
        ),
        in_specs=[whole(pltpu.SMEM), whole(pltpu.HBM), whole(pltpu.HBM), whole(pltpu.HBM)],
        out_specs=(whole(pltpu.VMEM), whole(pltpu.VMEM)),
        scratch_shapes=[
            pltpu.VMEM((slots, tiles, tile, columns), jnp.bfloat16),
            pltpu.VMEM((ways, slots, tiles, k_local, cycles, tile), jnp.bfloat16),
            pltpu.VMEM((ways * tiles + slots, k_local, 2, tile), jnp.float32),
            pltpu.VMEM((2 * rows, tile), jnp.bfloat16),
            pltpu.VMEM((2 * rows, tile), jnp.bfloat16),
            pltpu.VMEM((slots, 2 * rows, columns), jnp.float32),
            pltpu.SemaphoreType.DMA((slots, tiles)),
            pltpu.SemaphoreType.DMA((ways, slots, tiles)),
            pltpu.SemaphoreType.DMA((ways * tiles,)),
        ],
        compiler_params=params,
        cost_estimate=pl.CostEstimate(
            flops=4 * slots * rows * piece_rows * columns, bytes_accessed=8 * 1024 * 1024, transcendentals=0
        ),
        name="own_half",
    )(m_list, sky, wigner, beam)

    blocks = pl.pallas_call(
        functools.partial(second_kernel, ways, tile),
        out_shape=pltpu.VMEM((cycles, width, columns), jnp.bfloat16),
        in_specs=[whole(pltpu.SMEM)] + [whole(pltpu.VMEM)] * (ways + 1),
        out_specs=whole(pltpu.VMEM),
        scratch_shapes=[
            pltpu.VMEM((2 * rows, columns), jnp.float32),
            pltpu.VMEM((lane_tiles, cycles * width, LANES), jnp.float32),
        ],
        compiler_params=params,
        cost_estimate=pl.CostEstimate(
            flops=4 * slots * rows * piece_rows * columns, bytes_accessed=8 * 1024 * 1024, transcendentals=0
        ),
        name="other_half",
    )(m_list, part, factors, *pieces)
    received = lax.all_to_all(blocks, "blk", split_axis=0, concat_axis=0, tiled=True)
    return received.reshape(1, -1, k_local, columns)


def solution(mesh):
    in_specs = (
        P("blk", "beamk", None),
        P("beamk", None, None),
        P("blk", "beamk", None, None),
        P("blk"),
    )
    out_specs = P("blk", None, "beamk", None)
    body = functools.partial(local, ways=mesh.shape["beamk"])
    return jax.shard_map(body, mesh=mesh, in_specs=in_specs, out_specs=out_specs, check_vma=False)
```

```python
import functools

import jax
import jax.numpy as jnp
from jax import lax
from jax.experimental import pallas as pl
from jax.experimental.pallas import tpu as pltpu
from jax.sharding import PartitionSpec as P

KB = 40
LANES = 128
VMEM_LIMIT = 24 * 1024 * 1024


def tile_of(rows):
    return max(t for t in range(LANES, min(rows, 512) + 1, LANES) if rows % t == 0)


def whole(memory):
    return pl.BlockSpec(memory_space=memory)


def turn_by_i(rows):
    half = rows.shape[1] // 2
    swapped = pltpu.roll(rows, half, 1)
    column = lax.broadcasted_iota(jnp.int32, swapped.shape, 1)
    return jnp.where(column < half, -swapped, swapped)


def owner_of(distance, ways):
    return lax.rem(lax.axis_index("beamk") - distance + ways, ways)


def first_tile(m_value, owner, piece_rows, tile):
    return jnp.minimum(jnp.maximum(m_value - owner * piece_rows, 0) // tile, piece_rows // tile)


def first_kernel(
    ways, tile, m_list, sky, wigner, beam, part, factors, info, m_ref, sky_in, wigner_in, beam_in, own, acc, m_sem, sky_sem, wigner_sem, beam_sem
):
    slots, piece_rows, columns = sky.shape
    k_local, cycles = wigner.shape[1], wigner.shape[2]
    rows = k_local * cycles
    tiles = piece_rows // tile
    all_tiles = ways * tiles
    first_k = lax.axis_index("beamk") * k_local - KB // 2
    last = tiles - 1

    def m_copy():
        return pltpu.make_async_copy(m_list, m_ref, m_sem)

    def beam_copy(index):
        span = pl.ds(pl.multiple_of(index * tile, tile), tile)
        return pltpu.make_async_copy(beam.at[:, :, span], beam_in.at[index], beam_sem.at[index])

    def sky_copy(slot, step):
        span = pl.ds(pl.multiple_of(step * tile, tile), tile)
        return pltpu.make_async_copy(sky.at[slot, span], sky_in.at[slot, span], sky_sem.at[slot, step])

    def wigner_copy(distance, slot, step):
        start = pl.multiple_of(owner_of(distance, ways) * piece_rows + step * tile, tile)
        return pltpu.make_async_copy(
            wigner.at[slot, :, :, pl.ds(start, tile)],
            wigner_in.at[distance, slot, step],
            wigner_sem.at[distance, slot, step],
        )

    def begin(distance, slot):
        return first_tile(m_ref[slot], owner_of(distance, ways), piece_rows, tile)

    def fill(target, distance, slot, step):
        index = owner_of(distance, ways) * tiles + step
        index = jnp.where(index == m_ref[slot] // tile, all_tiles + slot, index)
        for k in range(k_local):
            values = wigner_in[distance, slot, step, k].astype(jnp.float32)
            target[k * cycles : (k + 1) * cycles, :] = (values * beam_in[index, k, 0:1, :]).astype(jnp.bfloat16)
            target[rows + k * cycles : rows + (k + 1) * cycles, :] = (values * beam_in[index, k, 1:2, :]).astype(jnp.bfloat16)

    upper = 2 * (owner_of(0, ways) + 1) > ways
    early = [jnp.bool_(True) if slot % 2 == 0 else upper for slot in range(slots)]
    m_copy().start()
    for slot in range(slots):

        @pl.when(early[slot])
        def _():
            wigner_copy(0, slot, last).start()
            sky_copy(slot, last).start()

    for index in range(all_tiles):
        beam_copy(index).start()
    m_copy().wait()
    for slot in range(slots):
        begins = begin(0, slot)

        @pl.when(jnp.logical_and(begins < tiles, jnp.logical_not(early[slot])))
        def _():
            wigner_copy(0, slot, last).start()
            sky_copy(slot, last).start()

        @pl.loop(begins + 1, tiles)
        def _(later):
            step = tiles - 1 - later + begins
            wigner_copy(0, slot, step).start()
            sky_copy(slot, step).start()

    for distance in range(1, ways):
        for slot in range(slots):

            @pl.loop(begin(distance, slot), tiles)
            def _(step):
                wigner_copy(distance, slot, step).start()

    for slot in range(slots):
        info[slot : slot + 1, :] = jnp.full((1, LANES), m_ref[slot].astype(jnp.float32))
    for index in range(all_tiles):
        beam_copy(index).wait()
    for slot in range(slots):
        index = m_ref[slot] // tile
        degrees = index * tile + lax.broadcasted_iota(jnp.int32, (2, tile), 1)
        for k in range(k_local):
            lowest = jnp.maximum(m_ref[slot], jnp.abs(first_k + k))
            beam_in[all_tiles + slot, k] = jnp.where(degrees >= lowest, beam_in[index, k], 0.0)

    @pl.loop(0, slots)
    def _(slot):
        begins = begin(0, slot)

        @pl.loop(begins, tiles)
        def _(later):
            step = tiles - 1 - later + begins
            wigner_copy(0, slot, step).wait()
            span = pl.ds(pl.multiple_of(step * tile, tile), tile)
            fill(own.at[:, span], 0, slot, step)
            sky_copy(slot, step).wait()

        for skipped in range(tiles):

            @pl.when(begins == skipped)
            def _():
                span = slice(skipped * tile, piece_rows)
                acc[...] = jnp.dot(own[:, span], sky_in[slot, span], preferred_element_type=jnp.float32)

        @pl.when(begins == tiles)
        def _():
            acc[...] = jnp.zeros_like(acc)

        for k in range(k_local):
            span = slice(k * cycles, (k + 1) * cycles)
            part[slot, span] = acc[span] + turn_by_i(acc[rows + k * cycles : rows + (k + 1) * cycles])

    for distance in range(1, ways):

        @pl.loop(0, slots)
        def _(slot):
            @pl.loop(begin(distance, slot), tiles)
            def _(step):
                wigner_copy(distance, slot, step).wait()
                span = pl.ds(pl.multiple_of(step * tile, tile), tile)
                fill(factors.at[distance - 1, slot, :, span], distance, slot, step)

    for slot in range(slots):

        @pl.when(jnp.logical_and(begin(0, slot) == tiles, early[slot]))
        def _():
            wigner_copy(0, slot, last).wait()
            sky_copy(slot, last).wait()


def second_kernel(ways, tile, info, part, factors, *refs):
    pieces, (out, acc, turned) = refs[: ways - 1], refs[ways - 1 :]
    slots, rows, columns = part.shape
    piece_rows = pieces[0].shape[1]
    tiles = piece_rows // tile
    cycles, width, _ = out.shape
    k_local = width // slots
    pitch = turned.shape[1] // cycles

    @pl.loop(0, slots)
    def _(slot):
        m_value = jnp.max(info[pl.ds(slot, 1), :]).astype(jnp.int32)
        for distance in range(1, ways):
            missing = first_tile(m_value, owner_of(distance, ways), piece_rows, tile)
            for skipped in range(tiles):

                @pl.when(missing == skipped)
                def _():
                    span = slice(skipped * tile, piece_rows)
                    term = jnp.dot(
                        factors[distance - 1, slot, :, span],
                        pieces[distance - 1][slot, span],
                        preferred_element_type=jnp.float32,
                    )
                    acc[...] = term if distance == 1 else acc[...] + term

            if distance == 1:

                @pl.when(missing == tiles)
                def _():
                    acc[...] = jnp.zeros_like(acc)

        for k in range(k_local):
            span = slice(k * cycles, (k + 1) * cycles)
            total = part[slot, span] + acc[span] + turn_by_i(acc[rows + k * cycles : rows + (k + 1) * cycles])
            for lane in range(columns // LANES):
                turned[lane, pl.ds(slot * k_local + k, cycles, stride=pitch), :] = total[:, lane * LANES : (lane + 1) * LANES]

    for cycle in range(cycles):
        for lane in range(columns // LANES):
            out[cycle, :, lane * LANES : (lane + 1) * LANES] = turned[lane, cycle * pitch : cycle * pitch + width].astype(out.dtype)


def local(sky, beam, wigner, m_list, *, ways):
    slots, piece_rows, columns = sky.shape
    _, k_local, cycles, degrees = wigner.shape
    rows = k_local * cycles
    tile = tile_of(piece_rows)
    tiles = piece_rows // tile
    lane_tiles = columns // LANES
    width = slots * k_local
    params = pltpu.CompilerParams(vmem_limit_bytes=VMEM_LIMIT)

    pieces = []
    for shift in range(1, ways):
        perm = [(c, (c + shift) % ways) for c in range(ways)]
        pieces.append(pltpu.with_memory_space_constraint(lax.ppermute(sky, "beamk", perm), pltpu.VMEM))
    sky, beam, wigner, m_list = (pltpu.with_memory_space_constraint(x, pltpu.HBM) for x in (sky, beam, wigner, m_list))

    part, factors, info = pl.pallas_call(
        functools.partial(first_kernel, ways, tile),
        out_shape=(
            pltpu.VMEM((slots, rows, columns), jnp.float32),
            pltpu.VMEM((ways - 1, slots, 2 * rows, piece_rows), jnp.bfloat16),
            pltpu.VMEM((8, LANES), jnp.float32),
        ),
        in_specs=[whole(pltpu.HBM)] * 4,
        out_specs=(whole(pltpu.VMEM),) * 3,
        scratch_shapes=[
            pltpu.SMEM(m_list.shape, jnp.int32),
            pltpu.VMEM((slots, piece_rows, columns), jnp.bfloat16),
            pltpu.VMEM((ways, slots, tiles, k_local, cycles, tile), jnp.bfloat16),
            pltpu.VMEM((ways * tiles + slots, k_local, 2, tile), jnp.float32),
            pltpu.VMEM((2 * rows, piece_rows), jnp.bfloat16),
            pltpu.VMEM((2 * rows, columns), jnp.float32),
            pltpu.SemaphoreType.DMA,
            pltpu.SemaphoreType.DMA((slots, tiles)),
            pltpu.SemaphoreType.DMA((ways, slots, tiles)),
            pltpu.SemaphoreType.DMA((ways * tiles,)),
        ],
        compiler_params=params,
        cost_estimate=pl.CostEstimate(
            flops=4 * slots * rows * piece_rows * columns, bytes_accessed=8 * 1024 * 1024, transcendentals=0
        ),
        name="own_half",
    )(m_list, sky, wigner, beam)

    blocks = pl.pallas_call(
        functools.partial(second_kernel, ways, tile),
        out_shape=pltpu.VMEM((cycles, width, columns), jnp.bfloat16),
        in_specs=[whole(pltpu.VMEM)] * (ways + 2),
        out_specs=whole(pltpu.VMEM),
        scratch_shapes=[
            pltpu.VMEM((2 * rows, columns), jnp.float32),
            pltpu.VMEM((lane_tiles, cycles * (width + 1 - width % 2), LANES), jnp.float32),
        ],
        compiler_params=params,
        cost_estimate=pl.CostEstimate(
            flops=4 * slots * rows * piece_rows * columns, bytes_accessed=8 * 1024 * 1024, transcendentals=0
        ),
        name="other_half",
    )(info, part, factors, *pieces)
    received = lax.all_to_all(blocks, "blk", split_axis=0, concat_axis=0, tiled=True)
    return received.reshape(1, -1, k_local, columns)


def solution(mesh):
    in_specs = (
        P("blk", "beamk", None),
        P("beamk", None, None),
        P("blk", "beamk", None, None),
        P("blk"),
    )
    out_specs = P("blk", None, "beamk", None)
    body = functools.partial(local, ways=mesh.shape["beamk"])
    return jax.shard_map(body, mesh=mesh, in_specs=in_specs, out_specs=out_specs, check_vma=False)
```

```python
import functools

import jax
import jax.numpy as jnp
from jax import lax
from jax.experimental import pallas as pl
from jax.experimental.pallas import tpu as pltpu
from jax.sharding import PartitionSpec as P

KB = 40
LANES = 128
VMEM_LIMIT = 24 * 1024 * 1024


def tile_of(rows):
    return max(t for t in range(LANES, min(rows, 512) + 1, LANES) if rows % t == 0)


def whole(memory):
    return pl.BlockSpec(memory_space=memory)


def turn_by_i(rows):
    half = rows.shape[1] // 2
    swapped = pltpu.roll(rows, half, 1)
    column = lax.broadcasted_iota(jnp.int32, swapped.shape, 1)
    return jnp.where(column < half, -swapped, swapped)


def owner_of(distance, ways):
    return lax.rem(lax.axis_index("beamk") - distance + ways, ways)


def first_tile(m_value, owner, piece_rows, tile):
    return jnp.minimum(jnp.maximum(m_value - owner * piece_rows, 0) // tile, piece_rows // tile)


def first_kernel(
    ways, tile, m_list, sky, wigner, beam, part, factors, info, m_ref, sky_in, wigner_in, beam_in, own, acc, m_sem, sky_sem, wigner_sem, beam_sem
):
    slots, piece_rows, columns = sky.shape
    k_local, cycles = wigner.shape[1], wigner.shape[2]
    rows = k_local * cycles
    tiles = piece_rows // tile
    all_tiles = ways * tiles
    first_k = lax.axis_index("beamk") * k_local - KB // 2
    last = tiles - 1

    def m_copy():
        return pltpu.make_async_copy(m_list, m_ref, m_sem)

    def beam_copy(index, half):
        span = pl.ds(pl.multiple_of(index * tile, tile), tile)
        return pltpu.make_async_copy(beam.at[:, half, span], beam_in.at[index, half], beam_sem.at[index, half])

    def sky_copy(slot, step):
        span = pl.ds(pl.multiple_of(step * tile, tile), tile)
        return pltpu.make_async_copy(sky.at[slot, span], sky_in.at[slot, span], sky_sem.at[slot, step])

    def wigner_copy(distance, slot, step):
        start = pl.multiple_of(owner_of(distance, ways) * piece_rows + step * tile, tile)
        return pltpu.make_async_copy(
            wigner.at[slot, :, :, pl.ds(start, tile)],
            wigner_in.at[distance, slot, step],
            wigner_sem.at[distance, slot, step],
        )

    def begin(distance, slot):
        return first_tile(m_ref[slot], owner_of(distance, ways), piece_rows, tile)

    def fill(target, distance, slot, step):
        index = owner_of(distance, ways) * tiles + step
        index = jnp.where(index == m_ref[slot] // tile, all_tiles + slot, index)
        for k in range(k_local):
            values = wigner_in[distance, slot, step, k].astype(jnp.float32)
            target[k * cycles : (k + 1) * cycles, :] = (values * beam_in[index, 0, k : k + 1, :]).astype(jnp.bfloat16)
            target[rows + k * cycles : rows + (k + 1) * cycles, :] = (values * beam_in[index, 1, k : k + 1, :]).astype(jnp.bfloat16)

    upper = 2 * (owner_of(0, ways) + 1) > ways
    early = [jnp.bool_(True) if slot % 2 == 0 else upper for slot in range(slots)]
    m_copy().start()
    for slot in range(slots):

        @pl.when(early[slot])
        def _():
            wigner_copy(0, slot, last).start()
            sky_copy(slot, last).start()

    for index in range(all_tiles):
        for half in range(2):
            beam_copy(index, half).start()
    m_copy().wait()
    for slot in range(slots):
        begins = begin(0, slot)

        @pl.when(jnp.logical_and(begins < tiles, jnp.logical_not(early[slot])))
        def _():
            wigner_copy(0, slot, last).start()
            sky_copy(slot, last).start()

        @pl.loop(begins + 1, tiles)
        def _(later):
            step = tiles - 1 - later + begins
            wigner_copy(0, slot, step).start()
            sky_copy(slot, step).start()

    for distance in range(1, ways):
        for slot in range(slots):

            @pl.loop(begin(distance, slot), tiles)
            def _(step):
                wigner_copy(distance, slot, step).start()

    for slot in range(slots):
        info[slot : slot + 1, :] = jnp.full((1, LANES), m_ref[slot].astype(jnp.float32))
    for index in range(all_tiles):
        for half in range(2):
            beam_copy(index, half).wait()
    for slot in range(slots):
        index = m_ref[slot] // tile
        degrees = index * tile + lax.broadcasted_iota(jnp.int32, (k_local, tile), 1)
        k_values = first_k + lax.broadcasted_iota(jnp.int32, (k_local, tile), 0)
        inside = degrees >= jnp.maximum(m_ref[slot], jnp.abs(k_values))
        for half in range(2):
            beam_in[all_tiles + slot, half] = jnp.where(inside, beam_in[index, half], 0.0)

    @pl.loop(0, slots)
    def _(slot):
        begins = begin(0, slot)

        @pl.loop(begins, tiles)
        def _(later):
            step = tiles - 1 - later + begins
            wigner_copy(0, slot, step).wait()
            span = pl.ds(pl.multiple_of(step * tile, tile), tile)
            fill(own.at[:, span], 0, slot, step)
            sky_copy(slot, step).wait()

        for skipped in range(tiles):

            @pl.when(begins == skipped)
            def _():
                span = slice(skipped * tile, piece_rows)
                acc[...] = jnp.dot(own[:, span], sky_in[slot, span], preferred_element_type=jnp.float32)

        @pl.when(begins == tiles)
        def _():
            acc[...] = jnp.zeros_like(acc)

        for k in range(k_local):
            span = slice(k * cycles, (k + 1) * cycles)
            part[slot, span] = acc[span] + turn_by_i(acc[rows + k * cycles : rows + (k + 1) * cycles])

    for distance in range(1, ways):

        @pl.loop(0, slots)
        def _(slot):
            @pl.loop(begin(distance, slot), tiles)
            def _(step):
                wigner_copy(distance, slot, step).wait()
                span = pl.ds(pl.multiple_of(step * tile, tile), tile)
                fill(factors.at[distance - 1, slot, :, span], distance, slot, step)

    for slot in range(slots):

        @pl.when(jnp.logical_and(begin(0, slot) == tiles, early[slot]))
        def _():
            wigner_copy(0, slot, last).wait()
            sky_copy(slot, last).wait()


def second_kernel(ways, tile, info, part, factors, *refs):
    pieces, (out, acc, turned) = refs[: ways - 1], refs[ways - 1 :]
    slots, rows, columns = part.shape
    piece_rows = pieces[0].shape[1]
    tiles = piece_rows // tile
    cycles, width, _ = out.shape
    k_local = width // slots
    pitch = turned.shape[1] // cycles

    @pl.loop(0, slots)
    def _(slot):
        m_value = jnp.max(info[pl.ds(slot, 1), :]).astype(jnp.int32)
        for distance in range(1, ways):
            missing = first_tile(m_value, owner_of(distance, ways), piece_rows, tile)
            for skipped in range(tiles):

                @pl.when(missing == skipped)
                def _():
                    span = slice(skipped * tile, piece_rows)
                    term = jnp.dot(
                        factors[distance - 1, slot, :, span],
                        pieces[distance - 1][slot, span],
                        preferred_element_type=jnp.float32,
                    )
                    acc[...] = term if distance == 1 else acc[...] + term

            if distance == 1:

                @pl.when(missing == tiles)
                def _():
                    acc[...] = jnp.zeros_like(acc)

        for k in range(k_local):
            span = slice(k * cycles, (k + 1) * cycles)
            total = part[slot, span] + acc[span] + turn_by_i(acc[rows + k * cycles : rows + (k + 1) * cycles])
            for lane in range(columns // LANES):
                turned[lane, pl.ds(slot * k_local + k, cycles, stride=pitch), :] = total[:, lane * LANES : (lane + 1) * LANES]

    for cycle in range(cycles):
        for lane in range(columns // LANES):
            out[cycle, :, lane * LANES : (lane + 1) * LANES] = turned[lane, cycle * pitch : cycle * pitch + width].astype(out.dtype)


def local(sky, beam, wigner, m_list, *, ways):
    slots, piece_rows, columns = sky.shape
    _, k_local, cycles, degrees = wigner.shape
    rows = k_local * cycles
    tile = tile_of(piece_rows)
    tiles = piece_rows // tile
    lane_tiles = columns // LANES
    width = slots * k_local
    params = pltpu.CompilerParams(vmem_limit_bytes=VMEM_LIMIT)

    pieces = []
    for shift in range(1, ways):
        perm = [(c, (c + shift) % ways) for c in range(ways)]
        pieces.append(pltpu.with_memory_space_constraint(lax.ppermute(sky, "beamk", perm), pltpu.VMEM))
    sky, beam, wigner, m_list = (pltpu.with_memory_space_constraint(x, pltpu.HBM) for x in (sky, beam, wigner, m_list))

    part, factors, info = pl.pallas_call(
        functools.partial(first_kernel, ways, tile),
        out_shape=(
            pltpu.VMEM((slots, rows, columns), jnp.float32),
            pltpu.VMEM((ways - 1, slots, 2 * rows, piece_rows), jnp.bfloat16),
            pltpu.VMEM((8, LANES), jnp.float32),
        ),
        in_specs=[whole(pltpu.HBM)] * 4,
        out_specs=(whole(pltpu.VMEM),) * 3,
        scratch_shapes=[
            pltpu.SMEM(m_list.shape, jnp.int32),
            pltpu.VMEM((slots, piece_rows, columns), jnp.bfloat16),
            pltpu.VMEM((ways, slots, tiles, k_local, cycles, tile), jnp.bfloat16),
            pltpu.VMEM((ways * tiles + slots, 2, k_local, tile), jnp.float32),
            pltpu.VMEM((2 * rows, piece_rows), jnp.bfloat16),
            pltpu.VMEM((2 * rows, columns), jnp.float32),
            pltpu.SemaphoreType.DMA,
            pltpu.SemaphoreType.DMA((slots, tiles)),
            pltpu.SemaphoreType.DMA((ways, slots, tiles)),
            pltpu.SemaphoreType.DMA((ways * tiles, 2)),
        ],
        compiler_params=params,
        cost_estimate=pl.CostEstimate(
            flops=4 * slots * rows * piece_rows * columns, bytes_accessed=8 * 1024 * 1024, transcendentals=0
        ),
        name="own_half",
    )(m_list, sky, wigner, beam)

    blocks = pl.pallas_call(
        functools.partial(second_kernel, ways, tile),
        out_shape=pltpu.VMEM((cycles, width, columns), jnp.bfloat16),
        in_specs=[whole(pltpu.VMEM)] * (ways + 2),
        out_specs=whole(pltpu.VMEM),
        scratch_shapes=[
            pltpu.VMEM((2 * rows, columns), jnp.float32),
            pltpu.VMEM((lane_tiles, cycles * (width + 1 - width % 2), LANES), jnp.float32),
        ],
        compiler_params=params,
        cost_estimate=pl.CostEstimate(
            flops=4 * slots * rows * piece_rows * columns, bytes_accessed=8 * 1024 * 1024, transcendentals=0
        ),
        name="other_half",
    )(info, part, factors, *pieces)
    received = lax.all_to_all(blocks, "blk", split_axis=0, concat_axis=0, tiled=True)
    return received.reshape(1, -1, k_local, columns)


def solution(mesh):
    in_specs = (
        P("blk", "beamk", None),
        P("beamk", None, None),
        P("blk", "beamk", None, None),
        P("blk"),
    )
    out_specs = P("blk", None, "beamk", None)
    body = functools.partial(local, ways=mesh.shape["beamk"])
    return jax.shard_map(body, mesh=mesh, in_specs=in_specs, out_specs=out_specs, check_vma=False)
```

```python
import functools

import jax
import jax.numpy as jnp
from jax import lax
from jax.experimental import pallas as pl
from jax.experimental.pallas import tpu as pltpu
from jax.sharding import PartitionSpec as P

KB = 40
LANES = 128
VMEM_LIMIT = 24 * 1024 * 1024


def tile_of(rows):
    return max(t for t in range(LANES, min(rows, 512) + 1, LANES) if rows % t == 0)


def whole(memory):
    return pl.BlockSpec(memory_space=memory)


def turn_by_i(rows):
    half = rows.shape[1] // 2
    swapped = pltpu.roll(rows, half, 1)
    column = lax.broadcasted_iota(jnp.int32, swapped.shape, 1)
    return jnp.where(column < half, -swapped, swapped)


def owner_of(distance, ways):
    return lax.rem(lax.axis_index("beamk") - distance + ways, ways)


def first_tile(m_value, owner, piece_rows, tile):
    return jnp.minimum(jnp.maximum(m_value - owner * piece_rows, 0) // tile, piece_rows // tile)


def first_kernel(
    ways, tile, m_list, sky, wigner, beam, part, factors, info, m_ref, sky_in, wigner_in, beam_in, own, m_sem, sky_sem, wigner_sem, beam_sem
):
    slots, piece_rows, columns = sky.shape
    k_local, cycles = wigner.shape[1], wigner.shape[2]
    rows = k_local * cycles
    tiles = piece_rows // tile
    all_tiles = ways * tiles
    first_k = lax.axis_index("beamk") * k_local - KB // 2
    last = tiles - 1

    def m_copy():
        return pltpu.make_async_copy(m_list, m_ref, m_sem)

    def beam_copy(distance, half):
        span = pl.ds(pl.multiple_of(owner_of(distance, ways) * piece_rows, tile), piece_rows)
        return pltpu.make_async_copy(beam.at[:, half, span], beam_in.at[half, :, span], beam_sem.at[distance, half])

    def sky_copy(slot, step):
        span = pl.ds(pl.multiple_of(step * tile, tile), tile)
        return pltpu.make_async_copy(sky.at[slot, span], sky_in.at[slot, span], sky_sem.at[slot, step])

    def wigner_copy(distance, slot, step):
        start = pl.multiple_of(owner_of(distance, ways) * piece_rows + step * tile, tile)
        return pltpu.make_async_copy(
            wigner.at[slot, :, :, pl.ds(start, tile)],
            wigner_in.at[distance, slot, step],
            wigner_sem.at[distance, slot, step],
        )

    def begin(distance, slot):
        return first_tile(m_ref[slot], owner_of(distance, ways), piece_rows, tile)

    def fill(target, distance, slot, step):
        index = owner_of(distance, ways) * tiles + step
        index = jnp.where(index == m_ref[slot] // tile, all_tiles + slot, index)
        span = pl.ds(pl.multiple_of(index * tile, tile), tile)
        for k in range(k_local):
            values = wigner_in[distance, slot, step, k]
            for half in range(2):
                factor = jnp.broadcast_to(beam_in[half, k : k + 1, span], (cycles, tile)).astype(jnp.bfloat16)
                target[half * rows + k * cycles : half * rows + (k + 1) * cycles, :] = values * factor

    def cut(slot):
        index = m_ref[slot] // tile
        degrees = index * tile + lax.broadcasted_iota(jnp.int32, (k_local, tile), 1)
        k_values = first_k + lax.broadcasted_iota(jnp.int32, (k_local, tile), 0)
        inside = degrees >= jnp.maximum(m_ref[slot], jnp.abs(k_values))
        span = pl.ds(pl.multiple_of(index * tile, tile), tile)
        for half in range(2):
            beam_in[half, :, (all_tiles + slot) * tile : (all_tiles + slot + 1) * tile] = jnp.where(inside, beam_in[half, :, span], 0.0)

    def cut_in(distance, slot):
        return m_ref[slot] // piece_rows == owner_of(distance, ways)

    upper = 2 * (owner_of(0, ways) + 1) > ways
    early = [jnp.bool_(True) if slot % 2 == 0 else upper for slot in range(slots)]
    m_copy().start()
    for slot in range(slots):

        @pl.when(early[slot])
        def _():
            wigner_copy(0, slot, last).start()
            sky_copy(slot, last).start()

        if slot == 0:
            for half in range(2):
                beam_copy(0, half).start()

    m_copy().wait()
    for slot in range(slots):
        begins = begin(0, slot)

        @pl.when(jnp.logical_and(begins < tiles, jnp.logical_not(early[slot])))
        def _():
            wigner_copy(0, slot, last).start()
            sky_copy(slot, last).start()

        @pl.loop(begins + 1, tiles)
        def _(later):
            step = tiles - 1 - later + begins
            wigner_copy(0, slot, step).start()
            sky_copy(slot, step).start()

    for distance in range(1, ways):
        for half in range(2):
            beam_copy(distance, half).start()
        for slot in range(slots):

            @pl.loop(begin(distance, slot), tiles)
            def _(step):
                wigner_copy(distance, slot, step).start()

    for slot in range(slots):
        info[slot : slot + 1, :] = jnp.full((1, LANES), m_ref[slot].astype(jnp.float32))
    def beam_arrives(distance):
        for half in range(2):
            beam_copy(distance, half).wait()
        for slot in range(slots):
            pl.when(cut_in(distance, slot))(functools.partial(cut, slot))

    beam_arrives(0)

    @pl.loop(0, slots)
    def _(slot):
        begins = begin(0, slot)

        @pl.loop(begins, tiles)
        def _(later):
            step = tiles - 1 - later + begins
            wigner_copy(0, slot, step).wait()
            span = pl.ds(pl.multiple_of(step * tile, tile), tile)
            fill(own.at[:, span], 0, slot, step)
            sky_copy(slot, step).wait()

        for skipped in range(tiles):

            @pl.when(begins == skipped)
            def _():
                span = slice(skipped * tile, piece_rows)
                part[slot] = jnp.dot(own[:, span], sky_in[slot, span], preferred_element_type=jnp.float32)

        @pl.when(begins == tiles)
        def _():
            part[slot] = jnp.zeros(part.shape[1:], part.dtype)

    for distance in range(1, ways):
        beam_arrives(distance)

        @pl.loop(0, slots)
        def _(slot):
            @pl.loop(begin(distance, slot), tiles)
            def _(step):
                wigner_copy(distance, slot, step).wait()
                span = pl.ds(pl.multiple_of(step * tile, tile), tile)
                fill(factors.at[distance - 1, slot, :, span], distance, slot, step)

    for slot in range(slots):

        @pl.when(jnp.logical_and(begin(0, slot) == tiles, early[slot]))
        def _():
            wigner_copy(0, slot, last).wait()
            sky_copy(slot, last).wait()


def second_kernel(ways, tile, info, _, factors, *refs):
    pieces, (out, acc, turned) = refs[: ways - 1], refs[ways - 1 :]
    slots, rows, columns = acc.shape
    rows = rows // 2
    piece_rows = pieces[0].shape[1]
    tiles = piece_rows // tile
    cycles, width, _ = out.shape
    k_local = width // slots
    pitch = turned.shape[1] // cycles

    @pl.loop(0, slots)
    def _(slot):
        m_value = jnp.max(info[pl.ds(slot, 1), :]).astype(jnp.int32)
        for distance in range(1, ways):
            missing = first_tile(m_value, owner_of(distance, ways), piece_rows, tile)
            for skipped in range(tiles):

                @pl.when(missing == skipped)
                def _():
                    span = slice(skipped * tile, piece_rows)
                    acc[slot] += jnp.dot(
                        factors[distance - 1, slot, :, span],
                        pieces[distance - 1][slot, span],
                        preferred_element_type=jnp.float32,
                    )

        for k in range(k_local):
            span = slice(k * cycles, (k + 1) * cycles)
            total = acc[slot, span] + turn_by_i(acc[slot, rows + k * cycles : rows + (k + 1) * cycles])
            for lane in range(columns // LANES):
                turned[lane, pl.ds(slot * k_local + k, cycles, stride=pitch), :] = total[:, lane * LANES : (lane + 1) * LANES]

    for cycle in range(cycles):
        for lane in range(columns // LANES):
            out[cycle, :, lane * LANES : (lane + 1) * LANES] = turned[lane, cycle * pitch : cycle * pitch + width].astype(out.dtype)


def local(sky, beam, wigner, m_list, *, ways):
    slots, piece_rows, columns = sky.shape
    _, k_local, cycles, degrees = wigner.shape
    rows = k_local * cycles
    tile = tile_of(piece_rows)
    tiles = piece_rows // tile
    lane_tiles = columns // LANES
    width = slots * k_local
    params = pltpu.CompilerParams(vmem_limit_bytes=VMEM_LIMIT)

    pieces = []
    for shift in range(1, ways):
        perm = [(c, (c + shift) % ways) for c in range(ways)]
        pieces.append(pltpu.with_memory_space_constraint(lax.ppermute(sky, "beamk", perm), pltpu.VMEM))
    sky, beam, wigner, m_list = (pltpu.with_memory_space_constraint(x, pltpu.HBM) for x in (sky, beam, wigner, m_list))

    part, factors, info = pl.pallas_call(
        functools.partial(first_kernel, ways, tile),
        out_shape=(
            pltpu.VMEM((slots, 2 * rows, columns), jnp.float32),
            pltpu.VMEM((ways - 1, slots, 2 * rows, piece_rows), jnp.bfloat16),
            pltpu.VMEM((8, LANES), jnp.float32),
        ),
        in_specs=[whole(pltpu.HBM)] * 4,
        out_specs=(whole(pltpu.VMEM),) * 3,
        scratch_shapes=[
            pltpu.SMEM(m_list.shape, jnp.int32),
            pltpu.VMEM((slots, piece_rows, columns), jnp.bfloat16),
            pltpu.VMEM((ways, slots, tiles, k_local, cycles, tile), jnp.bfloat16),
            pltpu.VMEM((2, k_local, degrees + slots * tile), jnp.float32),
            pltpu.VMEM((2 * rows, piece_rows), jnp.bfloat16),
            pltpu.SemaphoreType.DMA,
            pltpu.SemaphoreType.DMA((slots, tiles)),
            pltpu.SemaphoreType.DMA((ways, slots, tiles)),
            pltpu.SemaphoreType.DMA((ways, 2)),
        ],
        compiler_params=params,
        cost_estimate=pl.CostEstimate(
            flops=4 * slots * rows * piece_rows * columns, bytes_accessed=8 * 1024 * 1024, transcendentals=0
        ),
        name="own_half",
    )(m_list, sky, wigner, beam)

    blocks, _ = pl.pallas_call(
        functools.partial(second_kernel, ways, tile),
        out_shape=(pltpu.VMEM((cycles, width, columns), jnp.bfloat16), pltpu.VMEM(part.shape, part.dtype)),
        in_specs=[whole(pltpu.VMEM)] * (ways + 2),
        out_specs=(whole(pltpu.VMEM),) * 2,
        input_output_aliases={1: 1},
        scratch_shapes=[
            pltpu.VMEM((lane_tiles, cycles * (width + 1 - width % 2), LANES), jnp.float32),
        ],
        compiler_params=params,
        cost_estimate=pl.CostEstimate(
            flops=4 * slots * rows * piece_rows * columns, bytes_accessed=8 * 1024 * 1024, transcendentals=0
        ),
        name="other_half",
    )(info, part, factors, *pieces)
    received = lax.all_to_all(blocks, "blk", split_axis=0, concat_axis=0, tiled=True)
    return received.reshape(1, -1, k_local, columns)


def solution(mesh):
    in_specs = (
        P("blk", "beamk", None),
        P("beamk", None, None),
        P("blk", "beamk", None, None),
        P("blk"),
    )
    out_specs = P("blk", None, "beamk", None)
    body = functools.partial(local, ways=mesh.shape["beamk"])
    return jax.shard_map(body, mesh=mesh, in_specs=in_specs, out_specs=out_specs, check_vma=False)
```

```python
import functools

import jax
import jax.numpy as jnp
from jax import lax
from jax.experimental import pallas as pl
from jax.experimental.pallas import tpu as pltpu
from jax.sharding import PartitionSpec as P

KB = 40
LANES = 128
VMEM_LIMIT = 24 * 1024 * 1024


def tile_of(rows):
    return max(t for t in range(LANES, min(rows, 512) + 1, LANES) if rows % t == 0)


def whole(memory):
    return pl.BlockSpec(memory_space=memory)


def turn_by_i(rows):
    half = rows.shape[1] // 2
    swapped = pltpu.roll(rows, half, 1)
    column = lax.broadcasted_iota(jnp.int32, swapped.shape, 1)
    return jnp.where(column < half, -swapped, swapped)


def owner_of(distance, ways):
    return lax.rem(lax.axis_index("beamk") - distance + ways, ways)


def first_tile(m_value, owner, piece_rows, tile):
    return jnp.minimum(jnp.maximum(m_value - owner * piece_rows, 0) // tile, piece_rows // tile)


def first_kernel(
    ways, tile, m_list, sky, wigner, beam, part, factors, info, m_ref, sky_in, wigner_in, beam_in, own, m_sem, sky_sem, wigner_sem, distant_sem, beam_sem
):
    slots, piece_rows, columns = sky.shape
    k_local, cycles = wigner.shape[1], wigner.shape[2]
    rows = k_local * cycles
    tiles = piece_rows // tile
    all_tiles = ways * tiles
    first_k = lax.axis_index("beamk") * k_local - KB // 2
    last = tiles - 1

    def m_copy():
        return pltpu.make_async_copy(m_list, m_ref, m_sem)

    def beam_copy(distance, half):
        span = pl.ds(pl.multiple_of(owner_of(distance, ways) * piece_rows, tile), piece_rows)
        return pltpu.make_async_copy(beam.at[:, half, span], beam_in.at[half, :, span], beam_sem.at[distance, half])

    def sky_copy(slot, step):
        span = pl.ds(pl.multiple_of(step * tile, tile), tile)
        return pltpu.make_async_copy(sky.at[slot, span], sky_in.at[slot, span], sky_sem.at[slot, step])

    def wigner_copy(slot, step):
        start = pl.multiple_of(owner_of(0, ways) * piece_rows + step * tile, tile)
        span = pl.ds(start, tile)
        return pltpu.make_async_copy(wigner.at[slot, :, :, span], wigner_in.at[slot, :, :, span], wigner_sem.at[slot, step])

    def distant_copy(distance, slot):
        span = pl.ds(pl.multiple_of(owner_of(distance, ways) * piece_rows, tile), piece_rows)
        return pltpu.make_async_copy(wigner.at[slot, :, :, span], wigner_in.at[slot, :, :, span], distant_sem.at[distance - 1, slot])

    def begin(distance, slot):
        return first_tile(m_ref[slot], owner_of(distance, ways), piece_rows, tile)

    def fill(target, distance, slot, step):
        index = owner_of(distance, ways) * tiles + step
        rows_of = pl.ds(pl.multiple_of(index * tile, tile), tile)
        index = jnp.where(index == m_ref[slot] // tile, all_tiles + slot, index)
        span = pl.ds(pl.multiple_of(index * tile, tile), tile)
        for k in range(k_local):
            values = wigner_in[slot, k, :, rows_of]
            for half in range(2):
                factor = jnp.broadcast_to(beam_in[half, k : k + 1, span], (cycles, tile)).astype(jnp.bfloat16)
                target[half * rows + k * cycles : half * rows + (k + 1) * cycles, :] = values * factor

    def cut(slot):
        index = m_ref[slot] // tile
        degrees = index * tile + lax.broadcasted_iota(jnp.int32, (k_local, tile), 1)
        k_values = first_k + lax.broadcasted_iota(jnp.int32, (k_local, tile), 0)
        inside = degrees >= jnp.maximum(m_ref[slot], jnp.abs(k_values))
        span = pl.ds(pl.multiple_of(index * tile, tile), tile)
        for half in range(2):
            beam_in[half, :, (all_tiles + slot) * tile : (all_tiles + slot + 1) * tile] = jnp.where(inside, beam_in[half, :, span], 0.0)

    def cut_in(distance, slot):
        return m_ref[slot] // piece_rows == owner_of(distance, ways)

    def upper(distance):
        return 2 * (owner_of(distance, ways) + 1) > ways

    def where_needed(distance, slot, do):
        if slot % 2 == 0:
            do()
        else:
            pl.when(upper(distance))(do)

    m_copy().start()
    for slot in range(slots):

        def fetch(slot=slot):
            for step in reversed(range(tiles)):
                wigner_copy(slot, step).start()
                if slot == 0 and step == last:
                    for half in range(2):
                        beam_copy(0, half).start()
                sky_copy(slot, step).start()

        where_needed(0, slot, fetch)
    for distance in range(1, ways):
        for half in range(2):
            beam_copy(distance, half).start()
        for slot in range(slots):
            where_needed(distance, slot, lambda distance=distance, slot=slot: distant_copy(distance, slot).start())
    m_copy().wait()
    for slot in range(slots):
        info[slot : slot + 1, :] = jnp.full((1, LANES), m_ref[slot].astype(jnp.float32))
    def beam_arrives(distance):
        for half in range(2):
            beam_copy(distance, half).wait()
        for slot in range(slots):
            pl.when(cut_in(distance, slot))(functools.partial(cut, slot))

    beam_arrives(0)

    @pl.loop(0, slots)
    def _(slot):
        begins = begin(0, slot)

        @pl.loop(begins, tiles)
        def _(later):
            step = tiles - 1 - later + begins
            wigner_copy(slot, step).wait()
            span = pl.ds(pl.multiple_of(step * tile, tile), tile)
            fill(own.at[:, span], 0, slot, step)
            sky_copy(slot, step).wait()

        for skipped in range(tiles):

            @pl.when(begins == skipped)
            def _():
                span = slice(skipped * tile, piece_rows)
                part[slot] = jnp.dot(own[:, span], sky_in[slot, span], preferred_element_type=jnp.float32)

        @pl.when(begins == tiles)
        def _():
            part[slot] = jnp.zeros(part.shape[1:], part.dtype)

    for distance in range(1, ways):
        beam_arrives(distance)
        for slot in range(slots):
            where_needed(distance, slot, lambda distance=distance, slot=slot: distant_copy(distance, slot).wait())

        @pl.loop(0, slots)
        def _(slot):
            @pl.loop(begin(distance, slot), tiles)
            def _(step):
                span = pl.ds(pl.multiple_of(step * tile, tile), tile)
                fill(factors.at[distance - 1, slot, :, span], distance, slot, step)

    for slot in range(slots):

        def drop(slot=slot):
            @pl.loop(0, begin(0, slot))
            def _(step):
                wigner_copy(slot, step).wait()
                sky_copy(slot, step).wait()

        where_needed(0, slot, drop)


def second_kernel(ways, tile, info, _, factors, *refs):
    pieces, (out, acc, turned) = refs[: ways - 1], refs[ways - 1 :]
    slots, rows, columns = acc.shape
    rows = rows // 2
    piece_rows = pieces[0].shape[1]
    tiles = piece_rows // tile
    cycles, width, _ = out.shape
    k_local = width // slots
    pitch = turned.shape[1] // cycles

    @pl.loop(0, slots)
    def _(slot):
        m_value = jnp.max(info[pl.ds(slot, 1), :]).astype(jnp.int32)
        for distance in range(1, ways):
            missing = first_tile(m_value, owner_of(distance, ways), piece_rows, tile)
            for skipped in range(tiles):

                @pl.when(missing == skipped)
                def _():
                    span = slice(skipped * tile, piece_rows)
                    acc[slot] += jnp.dot(
                        factors[distance - 1, slot, :, span],
                        pieces[distance - 1][slot, span],
                        preferred_element_type=jnp.float32,
                    )

        for k in range(k_local):
            span = slice(k * cycles, (k + 1) * cycles)
            total = acc[slot, span] + turn_by_i(acc[slot, rows + k * cycles : rows + (k + 1) * cycles])
            for lane in range(columns // LANES):
                turned[lane, pl.ds(slot * k_local + k, cycles, stride=pitch), :] = total[:, lane * LANES : (lane + 1) * LANES]

    for cycle in range(cycles):
        for lane in range(columns // LANES):
            out[cycle, :, lane * LANES : (lane + 1) * LANES] = turned[lane, cycle * pitch : cycle * pitch + width].astype(out.dtype)


def local(sky, beam, wigner, m_list, *, ways):
    slots, piece_rows, columns = sky.shape
    _, k_local, cycles, degrees = wigner.shape
    rows = k_local * cycles
    tile = tile_of(piece_rows)
    tiles = piece_rows // tile
    lane_tiles = columns // LANES
    width = slots * k_local
    params = pltpu.CompilerParams(vmem_limit_bytes=VMEM_LIMIT)

    pieces = []
    for shift in range(1, ways):
        perm = [(c, (c + shift) % ways) for c in range(ways)]
        pieces.append(pltpu.with_memory_space_constraint(lax.ppermute(sky, "beamk", perm), pltpu.VMEM))
    sky, beam, wigner, m_list = (pltpu.with_memory_space_constraint(x, pltpu.HBM) for x in (sky, beam, wigner, m_list))

    part, factors, info = pl.pallas_call(
        functools.partial(first_kernel, ways, tile),
        out_shape=(
            pltpu.VMEM((slots, 2 * rows, columns), jnp.float32),
            pltpu.VMEM((ways - 1, slots, 2 * rows, piece_rows), jnp.bfloat16),
            pltpu.VMEM((8, LANES), jnp.float32),
        ),
        in_specs=[whole(pltpu.HBM)] * 4,
        out_specs=(whole(pltpu.VMEM),) * 3,
        scratch_shapes=[
            pltpu.SMEM(m_list.shape, jnp.int32),
            pltpu.VMEM((slots, piece_rows, columns), jnp.bfloat16),
            pltpu.VMEM(wigner.shape, jnp.bfloat16),
            pltpu.VMEM((2, k_local, degrees + slots * tile), jnp.float32),
            pltpu.VMEM((2 * rows, piece_rows), jnp.bfloat16),
            pltpu.SemaphoreType.DMA,
            pltpu.SemaphoreType.DMA((slots, tiles)),
            pltpu.SemaphoreType.DMA((slots, tiles)),
            pltpu.SemaphoreType.DMA((ways - 1, slots)),
            pltpu.SemaphoreType.DMA((ways, 2)),
        ],
        compiler_params=params,
        cost_estimate=pl.CostEstimate(
            flops=4 * slots * rows * piece_rows * columns, bytes_accessed=8 * 1024 * 1024, transcendentals=0
        ),
        name="own_half",
    )(m_list, sky, wigner, beam)

    blocks, _ = pl.pallas_call(
        functools.partial(second_kernel, ways, tile),
        out_shape=(pltpu.VMEM((cycles, width, columns), jnp.bfloat16), pltpu.VMEM(part.shape, part.dtype)),
        in_specs=[whole(pltpu.VMEM)] * (ways + 2),
        out_specs=(whole(pltpu.VMEM),) * 2,
        input_output_aliases={1: 1},
        scratch_shapes=[
            pltpu.VMEM((lane_tiles, cycles * (width + 1 - width % 2), LANES), jnp.float32),
        ],
        compiler_params=params,
        cost_estimate=pl.CostEstimate(
            flops=4 * slots * rows * piece_rows * columns, bytes_accessed=8 * 1024 * 1024, transcendentals=0
        ),
        name="other_half",
    )(info, part, factors, *pieces)
    received = lax.all_to_all(blocks, "blk", split_axis=0, concat_axis=0, tiled=True)
    return received.reshape(1, -1, k_local, columns)


def solution(mesh):
    in_specs = (
        P("blk", "beamk", None),
        P("beamk", None, None),
        P("blk", "beamk", None, None),
        P("blk"),
    )
    out_specs = P("blk", None, "beamk", None)
    body = functools.partial(local, ways=mesh.shape["beamk"])
    return jax.shard_map(body, mesh=mesh, in_specs=in_specs, out_specs=out_specs, check_vma=False)
```

```python
import functools

import jax
import jax.numpy as jnp
from jax import lax
from jax.experimental import pallas as pl
from jax.experimental.pallas import tpu as pltpu
from jax.sharding import PartitionSpec as P

KB = 40
LANES = 128
VMEM_LIMIT = 24 * 1024 * 1024


def tile_of(rows):
    return max(t for t in range(LANES, min(rows, 512) + 1, LANES) if rows % t == 0)


def groups_of(k_local):
    cut = 4 * (3 * k_local // 20)
    return [(0, cut), (cut, k_local)] if cut else [(0, k_local)]


def whole(memory):
    return pl.BlockSpec(memory_space=memory)


def turn_by_i(rows):
    half = rows.shape[1] // 2
    swapped = pltpu.roll(rows, half, 1)
    column = lax.broadcasted_iota(jnp.int32, swapped.shape, 1)
    return jnp.where(column < half, -swapped, swapped)


def owner_of(distance, ways):
    return lax.rem(lax.axis_index("beamk") - distance + ways, ways)


def first_tile(m_value, owner, piece_rows, tile):
    return jnp.minimum(jnp.maximum(m_value - owner * piece_rows, 0) // tile, piece_rows // tile)


def first_kernel(ways, tile, groups, m_list, sky, wigner, beam, *refs):
    slots, piece_rows, columns = sky.shape
    parts, refs = refs[: len(groups)], refs[len(groups) :]
    factors, info, m_ref, sky_in, wigner_in, beam_in, own, m_sem, sky_sem, wigner_sem, distant_sem, beam_sem = refs
    k_local, cycles = wigner.shape[1], wigner.shape[2]
    rows = k_local * cycles
    tiles = piece_rows // tile
    all_tiles = ways * tiles
    first_k = lax.axis_index("beamk") * k_local - KB // 2
    last = tiles - 1

    def m_copy():
        return pltpu.make_async_copy(m_list, m_ref, m_sem)

    def beam_copy(distance, half):
        span = pl.ds(pl.multiple_of(owner_of(distance, ways) * piece_rows, tile), piece_rows)
        return pltpu.make_async_copy(beam.at[:, half, span], beam_in.at[half, :, span], beam_sem.at[distance, half])

    def sky_copy(slot, step):
        span = pl.ds(pl.multiple_of(step * tile, tile), tile)
        return pltpu.make_async_copy(sky.at[slot, span], sky_in.at[slot, span], sky_sem.at[slot, step])

    def wigner_copy(slot, step):
        start = pl.multiple_of(owner_of(0, ways) * piece_rows + step * tile, tile)
        span = pl.ds(start, tile)
        return pltpu.make_async_copy(wigner.at[slot, :, :, span], wigner_in.at[slot, :, :, span], wigner_sem.at[slot, step])

    def distant_copy(distance, slot):
        span = pl.ds(pl.multiple_of(owner_of(distance, ways) * piece_rows, tile), piece_rows)
        return pltpu.make_async_copy(wigner.at[slot, :, :, span], wigner_in.at[slot, :, :, span], distant_sem.at[distance - 1, slot])

    def begin(distance, slot):
        return first_tile(m_ref[slot], owner_of(distance, ways), piece_rows, tile)

    def fill(target, distance, slot, step):
        index = owner_of(distance, ways) * tiles + step
        rows_of = pl.ds(pl.multiple_of(index * tile, tile), tile)
        index = jnp.where(index == m_ref[slot] // tile, all_tiles + slot, index)
        span = pl.ds(pl.multiple_of(index * tile, tile), tile)
        for first, end in groups:
            for k in range(first, end):
                values = wigner_in[slot, k, :, rows_of]
                for half in range(2):
                    factor = jnp.broadcast_to(beam_in[half, k : k + 1, span], (cycles, tile)).astype(jnp.bfloat16)
                    row = (first + half * (end - first) + k) * cycles
                    target[row : row + cycles, :] = values * factor

    def cut(slot):
        index = m_ref[slot] // tile
        degrees = index * tile + lax.broadcasted_iota(jnp.int32, (k_local, tile), 1)
        k_values = first_k + lax.broadcasted_iota(jnp.int32, (k_local, tile), 0)
        inside = degrees >= jnp.maximum(m_ref[slot], jnp.abs(k_values))
        span = pl.ds(pl.multiple_of(index * tile, tile), tile)
        for half in range(2):
            beam_in[half, :, (all_tiles + slot) * tile : (all_tiles + slot + 1) * tile] = jnp.where(inside, beam_in[half, :, span], 0.0)

    def cut_in(distance, slot):
        return m_ref[slot] // piece_rows == owner_of(distance, ways)

    def upper(distance):
        return 2 * (owner_of(distance, ways) + 1) > ways

    def where_needed(distance, slot, do):
        if slot % 2 == 0:
            do()
        else:
            pl.when(upper(distance))(do)

    m_copy().start()
    for slot in range(slots):

        def fetch(slot=slot):
            for step in reversed(range(tiles)):
                wigner_copy(slot, step).start()
                if slot == 0 and step == last:
                    for half in range(2):
                        beam_copy(0, half).start()
                sky_copy(slot, step).start()

        where_needed(0, slot, fetch)
    for distance in range(1, ways):
        for half in range(2):
            beam_copy(distance, half).start()
        for slot in range(slots):
            where_needed(distance, slot, lambda distance=distance, slot=slot: distant_copy(distance, slot).start())
    m_copy().wait()
    for slot in range(slots):
        info[slot : slot + 1, :] = jnp.full((1, LANES), m_ref[slot].astype(jnp.float32))
    def beam_arrives(distance):
        for half in range(2):
            beam_copy(distance, half).wait()
        for slot in range(slots):
            pl.when(cut_in(distance, slot))(functools.partial(cut, slot))

    beam_arrives(0)

    @pl.loop(0, slots)
    def _(slot):
        begins = begin(0, slot)

        @pl.loop(begins, tiles)
        def _(later):
            step = tiles - 1 - later + begins
            wigner_copy(slot, step).wait()
            span = pl.ds(pl.multiple_of(step * tile, tile), tile)
            fill(own.at[:, span], 0, slot, step)
            sky_copy(slot, step).wait()

        for skipped in range(tiles):

            @pl.when(begins == skipped)
            def _():
                span = slice(skipped * tile, piece_rows)
                sums = jnp.dot(own[:, span], sky_in[slot, span], preferred_element_type=jnp.float32)
                for part, (first, end) in zip(parts, groups):
                    part[slot] = sums[2 * first * cycles : 2 * end * cycles]

        @pl.when(begins == tiles)
        def _():
            for part in parts:
                part[slot] = jnp.zeros(part.shape[1:], part.dtype)

    for distance in range(1, ways):
        beam_arrives(distance)
        for slot in range(slots):
            where_needed(distance, slot, lambda distance=distance, slot=slot: distant_copy(distance, slot).wait())

        @pl.loop(0, slots)
        def _(slot):
            @pl.loop(begin(distance, slot), tiles)
            def _(step):
                span = pl.ds(pl.multiple_of(step * tile, tile), tile)
                fill(factors.at[distance - 1, slot, :, span], distance, slot, step)

    for slot in range(slots):

        def drop(slot=slot):
            @pl.loop(0, begin(0, slot))
            def _(step):
                wigner_copy(slot, step).wait()
                sky_copy(slot, step).wait()

        where_needed(0, slot, drop)


def second_kernel(ways, tile, first_row, info, _, factors, *refs):
    pieces, (out, acc, turned) = refs[: ways - 1], refs[ways - 1 :]
    slots, rows, columns = acc.shape
    rows = rows // 2
    piece_rows = pieces[0].shape[1]
    tiles = piece_rows // tile
    cycles, width, _ = out.shape
    k_local = width // slots
    pitch = turned.shape[1] // cycles

    @pl.loop(0, slots)
    def _(slot):
        m_value = jnp.max(info[pl.ds(slot, 1), :]).astype(jnp.int32)
        for distance in range(1, ways):
            missing = first_tile(m_value, owner_of(distance, ways), piece_rows, tile)
            for skipped in range(tiles):

                @pl.when(missing == skipped)
                def _():
                    span = slice(skipped * tile, piece_rows)
                    acc[slot] += jnp.dot(
                        factors[distance - 1, slot, first_row : first_row + 2 * rows, span],
                        pieces[distance - 1][slot, span],
                        preferred_element_type=jnp.float32,
                    )

        for k in range(k_local):
            span = slice(k * cycles, (k + 1) * cycles)
            total = acc[slot, span] + turn_by_i(acc[slot, rows + k * cycles : rows + (k + 1) * cycles])
            for lane in range(columns // LANES):
                turned[lane, pl.ds(slot * k_local + k, cycles, stride=pitch), :] = total[:, lane * LANES : (lane + 1) * LANES]

    for cycle in range(cycles):
        for lane in range(columns // LANES):
            out[cycle, :, lane * LANES : (lane + 1) * LANES] = turned[lane, cycle * pitch : cycle * pitch + width].astype(out.dtype)


def local(sky, beam, wigner, m_list, *, ways):
    slots, piece_rows, columns = sky.shape
    _, k_local, cycles, degrees = wigner.shape
    rows = k_local * cycles
    tile = tile_of(piece_rows)
    tiles = piece_rows // tile
    lane_tiles = columns // LANES
    params = pltpu.CompilerParams(vmem_limit_bytes=VMEM_LIMIT)

    pieces = []
    for shift in range(1, ways):
        perm = [(c, (c + shift) % ways) for c in range(ways)]
        pieces.append(pltpu.with_memory_space_constraint(lax.ppermute(sky, "beamk", perm), pltpu.VMEM))
    sky, beam, wigner, m_list = (pltpu.with_memory_space_constraint(x, pltpu.HBM) for x in (sky, beam, wigner, m_list))

    groups = groups_of(k_local)
    sums = [pltpu.VMEM((slots, 2 * (end - first) * cycles, columns), jnp.float32) for first, end in groups]
    *parts, factors, info = pl.pallas_call(
        functools.partial(first_kernel, ways, tile, groups),
        out_shape=(
            *sums,
            pltpu.VMEM((ways - 1, slots, 2 * rows, piece_rows), jnp.bfloat16),
            pltpu.VMEM((8, LANES), jnp.float32),
        ),
        in_specs=[whole(pltpu.HBM)] * 4,
        out_specs=(whole(pltpu.VMEM),) * (len(groups) + 2),
        scratch_shapes=[
            pltpu.SMEM(m_list.shape, jnp.int32),
            pltpu.VMEM((slots, piece_rows, columns), jnp.bfloat16),
            pltpu.VMEM(wigner.shape, jnp.bfloat16),
            pltpu.VMEM((2, k_local, degrees + slots * tile), jnp.float32),
            pltpu.VMEM((2 * rows, piece_rows), jnp.bfloat16),
            pltpu.SemaphoreType.DMA,
            pltpu.SemaphoreType.DMA((slots, tiles)),
            pltpu.SemaphoreType.DMA((slots, tiles)),
            pltpu.SemaphoreType.DMA((ways - 1, slots)),
            pltpu.SemaphoreType.DMA((ways, 2)),
        ],
        compiler_params=params,
        cost_estimate=pl.CostEstimate(
            flops=4 * slots * rows * piece_rows * columns, bytes_accessed=8 * 1024 * 1024, transcendentals=0
        ),
        name="own_half",
    )(m_list, sky, wigner, beam)

    received = []
    for part, shape, (first, end) in zip(parts, sums, groups):
        width = slots * (end - first)
        blocks, _ = pl.pallas_call(
            functools.partial(second_kernel, ways, tile, 2 * first * cycles),
            out_shape=(pltpu.VMEM((cycles, width, columns), jnp.bfloat16), shape),
            in_specs=[whole(pltpu.VMEM)] * (ways + 2),
            out_specs=(whole(pltpu.VMEM),) * 2,
            input_output_aliases={1: 1},
            scratch_shapes=[
                pltpu.VMEM((lane_tiles, cycles * (width + 1 - width % 2), LANES), jnp.float32),
            ],
            compiler_params=params,
            cost_estimate=pl.CostEstimate(
                flops=4 * slots * (end - first) * cycles * piece_rows * columns, bytes_accessed=4 * 1024 * 1024, transcendentals=0
            ),
            name="other_half",
        )(info, part, factors, *pieces)
        blocks = lax.all_to_all(blocks, "blk", split_axis=0, concat_axis=0, tiled=True)
        received.append(blocks.reshape(1, -1, end - first, columns))
    return jnp.concatenate(received, axis=2)


def solution(mesh):
    in_specs = (
        P("blk", "beamk", None),
        P("beamk", None, None),
        P("blk", "beamk", None, None),
        P("blk"),
    )
    out_specs = P("blk", None, "beamk", None)
    body = functools.partial(local, ways=mesh.shape["beamk"])
    return jax.shard_map(body, mesh=mesh, in_specs=in_specs, out_specs=out_specs, check_vma=False)
```

```python
import functools

import jax
import jax.numpy as jnp
from jax import lax
from jax.experimental import pallas as pl
from jax.experimental.pallas import tpu as pltpu
from jax.sharding import PartitionSpec as P

KB = 40
LANES = 128
INNER = 4
VMEM_LIMIT = 24 * 1024 * 1024


def tile_of(rows):
    return max(t for t in range(LANES, min(rows, 512) + 1, LANES) if rows % t == 0)


def whole(memory):
    return pl.BlockSpec(memory_space=memory)


def turn_by_i(rows):
    half = rows.shape[1] // 2
    swapped = pltpu.roll(rows, half, 1)
    column = lax.broadcasted_iota(jnp.int32, swapped.shape, 1)
    return jnp.where(column < half, -swapped, swapped)


def owner_of(distance, ways):
    return lax.rem(lax.axis_index("beamk") - distance + ways, ways)


def first_tile(m_value, owner, piece_rows, tile):
    return jnp.minimum(jnp.maximum(m_value - owner * piece_rows, 0) // tile, piece_rows // tile)


def first_kernel(
    ways, tile, m_list, sky, wigner, beam, part, factors, info, m_ref, sky_in, wigner_in, beam_in, own, m_sem, sky_sem, wigner_sem, distant_sem, beam_sem
):
    slots, piece_rows, columns = sky.shape
    k_local, cycles = wigner.shape[1], wigner.shape[2]
    rows = k_local * cycles
    tiles = piece_rows // tile
    all_tiles = ways * tiles
    first_k = lax.axis_index("beamk") * k_local - KB // 2
    last = tiles - 1

    def m_copy():
        return pltpu.make_async_copy(m_list, m_ref, m_sem)

    def beam_copy(distance, half):
        span = pl.ds(pl.multiple_of(owner_of(distance, ways) * piece_rows, tile), piece_rows)
        return pltpu.make_async_copy(beam.at[:, half, span], beam_in.at[half, :, span], beam_sem.at[distance, half])

    def sky_copy(slot, step):
        span = pl.ds(pl.multiple_of(step * tile, tile), tile)
        return pltpu.make_async_copy(sky.at[slot, span], sky_in.at[slot, span], sky_sem.at[slot, step])

    def wigner_copy(slot, step):
        start = pl.multiple_of(owner_of(0, ways) * piece_rows + step * tile, tile)
        span = pl.ds(start, tile)
        return pltpu.make_async_copy(wigner.at[slot, :, :, span], wigner_in.at[slot, :, :, span], wigner_sem.at[slot, step])

    def distant_copy(distance, slot):
        span = pl.ds(pl.multiple_of(owner_of(distance, ways) * piece_rows, tile), piece_rows)
        return pltpu.make_async_copy(wigner.at[slot, :, :, span], wigner_in.at[slot, :, :, span], distant_sem.at[distance - 1, slot])

    def begin(distance, slot):
        return first_tile(m_ref[slot], owner_of(distance, ways), piece_rows, tile)

    def fill(target, distance, slot, step):
        index = owner_of(distance, ways) * tiles + step
        rows_of = pl.ds(pl.multiple_of(index * tile, tile), tile)
        index = jnp.where(index == m_ref[slot] // tile, all_tiles + slot, index)
        span = pl.ds(pl.multiple_of(index * tile, tile), tile)
        for k in range(k_local):
            values = wigner_in[slot, k, :, rows_of]
            for half in range(2):
                factor = jnp.broadcast_to(beam_in[half, k : k + 1, span], (cycles, tile)).astype(jnp.bfloat16)
                target[half * rows + k * cycles : half * rows + (k + 1) * cycles, :] = values * factor

    def cut(slot):
        index = m_ref[slot] // tile
        degrees = index * tile + lax.broadcasted_iota(jnp.int32, (k_local, tile), 1)
        k_values = first_k + lax.broadcasted_iota(jnp.int32, (k_local, tile), 0)
        inside = degrees >= jnp.maximum(m_ref[slot], jnp.abs(k_values))
        span = pl.ds(pl.multiple_of(index * tile, tile), tile)
        for half in range(2):
            beam_in[half, :, (all_tiles + slot) * tile : (all_tiles + slot + 1) * tile] = jnp.where(inside, beam_in[half, :, span], 0.0)

    def cut_in(distance, slot):
        return m_ref[slot] // piece_rows == owner_of(distance, ways)

    def upper(distance):
        return 2 * (owner_of(distance, ways) + 1) > ways

    def where_needed(distance, slot, do):
        if slot % 2 == 0:
            do()
        else:
            pl.when(upper(distance))(do)

    m_copy().start()
    for slot in range(slots):

        def fetch(slot=slot):
            for step in reversed(range(tiles)):
                wigner_copy(slot, step).start()
                if slot == 0 and step == last:
                    for half in range(2):
                        beam_copy(0, half).start()
                sky_copy(slot, step).start()

        where_needed(0, slot, fetch)
    for distance in range(1, ways):
        for half in range(2):
            beam_copy(distance, half).start()
        for slot in range(slots):
            where_needed(distance, slot, lambda distance=distance, slot=slot: distant_copy(distance, slot).start())
    m_copy().wait()
    for slot in range(slots):
        info[slot : slot + 1, :] = jnp.full((1, LANES), m_ref[slot].astype(jnp.float32))
    def beam_arrives(distance):
        for half in range(2):
            beam_copy(distance, half).wait()
        for slot in range(slots):
            pl.when(cut_in(distance, slot))(functools.partial(cut, slot))

    beam_arrives(0)

    @pl.loop(0, slots)
    def _(slot):
        begins = begin(0, slot)

        @pl.loop(begins, tiles)
        def _(later):
            step = tiles - 1 - later + begins
            wigner_copy(slot, step).wait()
            span = pl.ds(pl.multiple_of(step * tile, tile), tile)
            fill(own.at[:, span], 0, slot, step)
            sky_copy(slot, step).wait()

        for skipped in range(tiles):

            @pl.when(begins == skipped)
            def _():
                span = slice(skipped * tile, piece_rows)
                part[slot] = jnp.dot(own[:, span], sky_in[slot, span], preferred_element_type=jnp.float32)

        @pl.when(begins == tiles)
        def _():
            part[slot] = jnp.zeros(part.shape[1:], part.dtype)

    for distance in range(1, ways):
        beam_arrives(distance)
        for slot in range(slots):
            where_needed(distance, slot, lambda distance=distance, slot=slot: distant_copy(distance, slot).wait())

        @pl.loop(0, slots)
        def _(slot):
            @pl.loop(begin(distance, slot), tiles)
            def _(step):
                span = pl.ds(pl.multiple_of(step * tile, tile), tile)
                fill(factors.at[distance - 1, slot, :, span], distance, slot, step)

    for slot in range(slots):

        def drop(slot=slot):
            @pl.loop(0, begin(0, slot))
            def _(step):
                wigner_copy(slot, step).wait()
                sky_copy(slot, step).wait()

        where_needed(0, slot, drop)


def second_kernel(ways, outer, tile, info, _, factors, *refs):
    pieces, refs = refs[: ways - 1], refs[ways - 1 :]
    outs, (acc, turned) = refs[:outer], refs[outer:]
    slots, rows, columns = acc.shape
    rows = rows // 2
    piece_rows = pieces[0].shape[1]
    tiles = piece_rows // tile
    width = outs[0].shape[1]
    cycles = outer * INNER
    k_local = width // slots
    pitch = turned.shape[1] // cycles

    @pl.loop(0, slots)
    def _(slot):
        m_value = jnp.max(info[pl.ds(slot, 1), :]).astype(jnp.int32)
        for distance in range(1, ways):
            missing = first_tile(m_value, owner_of(distance, ways), piece_rows, tile)
            for skipped in range(tiles):

                @pl.when(missing == skipped)
                def _():
                    span = slice(skipped * tile, piece_rows)
                    acc[slot] += jnp.dot(
                        factors[distance - 1, slot, :, span],
                        pieces[distance - 1][slot, span],
                        preferred_element_type=jnp.float32,
                    )

        for k in range(k_local):
            span = slice(k * cycles, (k + 1) * cycles)
            total = acc[slot, span] + turn_by_i(acc[slot, rows + k * cycles : rows + (k + 1) * cycles])
            for lane in range(columns // LANES):
                turned[lane, pl.ds(slot * k_local + k, cycles, stride=pitch), :] = total[:, lane * LANES : (lane + 1) * LANES]

    me = lax.axis_index("blk")
    for distance in range(cycles):
        start = (me ^ distance) * pitch
        for lane in range(columns // LANES):
            block = turned[lane, pl.ds(start, width), :].astype(jnp.bfloat16)
            outs[distance // INNER][distance % INNER, :, lane * LANES : (lane + 1) * LANES] = block


def regroup_kernel(*refs):
    count = len(refs) - INNER + 1
    for inner in range(1, INNER):
        for index in range(count):
            refs[count + inner - 1][index] = refs[index][inner]


def place_kernel(half, count, *refs):
    direct, moved, refs = refs[:count], refs[count : count + INNER - 1], refs[count + INNER - 1 :]
    out, turned, staged, sem = refs[-4:]
    k_local, slot_count, columns = staged.shape
    width = direct[0].shape[1]
    slots = width // k_local
    pitch = turned.shape[1] // k_local
    me = lax.axis_index("blk")
    for lane in range(columns // LANES):
        span = slice(lane * LANES, (lane + 1) * LANES)
        for index in range(count):
            for inner in range(INNER):
                block = direct[index][0, :, span] if inner == 0 else moved[inner - 1][index, :, span]
                block = block.astype(jnp.float32)
                source = (me ^ (index * INNER + inner)) % (count * INNER)
                for slot in range(slots):
                    turned[lane, pl.ds(slots * source + slot, k_local, stride=pitch), :] = block[slot * k_local : (slot + 1) * k_local]
        for k in range(k_local):
            staged[k, :, span] = turned[lane, k * pitch : k * pitch + slot_count].astype(staged.dtype)
    here = me // (count * INNER)
    start = pl.multiple_of((here if half == 0 else 1 - here) * slot_count, slot_count)
    copy = pltpu.make_async_copy(staged, out.at[:, pl.ds(start, slot_count), :], sem)
    copy.start()
    copy.wait()


def local(sky, beam, wigner, m_list, *, ways, peers):
    slots, piece_rows, columns = sky.shape
    _, k_local, cycles, degrees = wigner.shape
    rows = k_local * cycles
    tile = tile_of(piece_rows)
    tiles = piece_rows // tile
    lane_tiles = columns // LANES
    width = slots * k_local
    params = pltpu.CompilerParams(vmem_limit_bytes=VMEM_LIMIT)

    pieces = []
    for shift in range(1, ways):
        perm = [(c, (c + shift) % ways) for c in range(ways)]
        pieces.append(pltpu.with_memory_space_constraint(lax.ppermute(sky, "beamk", perm), pltpu.VMEM))
    sky, beam, wigner, m_list = (pltpu.with_memory_space_constraint(x, pltpu.HBM) for x in (sky, beam, wigner, m_list))

    part, factors, info = pl.pallas_call(
        functools.partial(first_kernel, ways, tile),
        out_shape=(
            pltpu.VMEM((slots, 2 * rows, columns), jnp.float32),
            pltpu.VMEM((ways - 1, slots, 2 * rows, piece_rows), jnp.bfloat16),
            pltpu.VMEM((8, LANES), jnp.float32),
        ),
        in_specs=[whole(pltpu.HBM)] * 4,
        out_specs=(whole(pltpu.VMEM),) * 3,
        scratch_shapes=[
            pltpu.SMEM(m_list.shape, jnp.int32),
            pltpu.VMEM((slots, piece_rows, columns), jnp.bfloat16),
            pltpu.VMEM(wigner.shape, jnp.bfloat16),
            pltpu.VMEM((2, k_local, degrees + slots * tile), jnp.float32),
            pltpu.VMEM((2 * rows, piece_rows), jnp.bfloat16),
            pltpu.SemaphoreType.DMA,
            pltpu.SemaphoreType.DMA((slots, tiles)),
            pltpu.SemaphoreType.DMA((slots, tiles)),
            pltpu.SemaphoreType.DMA((ways - 1, slots)),
            pltpu.SemaphoreType.DMA((ways, 2)),
        ],
        compiler_params=params,
        cost_estimate=pl.CostEstimate(
            flops=4 * slots * rows * piece_rows * columns, bytes_accessed=8 * 1024 * 1024, transcendentals=0
        ),
        name="own_half",
    )(m_list, sky, wigner, beam)

    outer = peers // INNER
    block = (width, columns)
    *sends, _ = pl.pallas_call(
        functools.partial(second_kernel, ways, outer, tile),
        out_shape=[pltpu.VMEM((INNER, *block), jnp.bfloat16)] * outer + [pltpu.VMEM(part.shape, part.dtype)],
        in_specs=[whole(pltpu.VMEM)] * (ways + 2),
        out_specs=[whole(pltpu.VMEM)] * (outer + 1),
        input_output_aliases={1: outer},
        scratch_shapes=[
            pltpu.VMEM((lane_tiles, cycles * (width + 1 - width % 2), LANES), jnp.float32),
        ],
        compiler_params=params,
        cost_estimate=pl.CostEstimate(
            flops=4 * slots * rows * piece_rows * columns, bytes_accessed=8 * 1024 * 1024, transcendentals=0
        ),
        name="other_half",
    )(info, part, factors, *pieces)

    def send(array, distance):
        perm = [(b, b ^ distance) for b in range(peers)]
        return pltpu.with_memory_space_constraint(lax.ppermute(array, "blk", perm), pltpu.VMEM)

    count = outer // 2
    arrived = [sends[0]] + [None] * (outer - 1)
    for distance in [*range(count, outer), *range(1, count)]:
        arrived[distance] = send(sends[distance], distance * INNER)
    out = None
    for half in range(2):
        direct = arrived[half * count : (half + 1) * count]
        grouped = pl.pallas_call(
            regroup_kernel,
            out_shape=[pltpu.VMEM((count, *block), jnp.bfloat16)] * (INNER - 1),
            in_specs=[whole(pltpu.VMEM)] * count,
            out_specs=[whole(pltpu.VMEM)] * (INNER - 1),
            compiler_params=params,
            name="regroup",
        )(*direct)
        moved = [None] * (INNER - 1)
        for inner in reversed(range(1, INNER)):
            moved[inner - 1] = send(grouped[inner - 1], inner)
        slot_count = slots * count * INNER
        operands = [*direct, *moved]
        in_specs = [whole(pltpu.VMEM)] * len(operands)
        if half:
            operands.append(out)
            in_specs.append(whole(pltpu.HBM))
        out = pl.pallas_call(
            functools.partial(place_kernel, half, count),
            out_shape=pltpu.HBM((k_local, slots * peers, columns), jnp.bfloat16),
            in_specs=in_specs,
            out_specs=whole(pltpu.HBM),
            input_output_aliases={len(operands) - 1: 0} if half else {},
            scratch_shapes=[
                pltpu.VMEM((lane_tiles, k_local * (slot_count + 1), LANES), jnp.float32),
                pltpu.VMEM((k_local, slot_count, columns), jnp.bfloat16),
                pltpu.SemaphoreType.DMA,
            ],
            compiler_params=params,
            name="place",
        )(*operands)
    return out.transpose(1, 0, 2)[None]


def solution(mesh):
    in_specs = (
        P("blk", "beamk", None),
        P("beamk", None, None),
        P("blk", "beamk", None, None),
        P("blk"),
    )
    out_specs = P("blk", None, "beamk", None)
    body = functools.partial(local, ways=mesh.shape["beamk"], peers=mesh.shape["blk"])
    return jax.shard_map(body, mesh=mesh, in_specs=in_specs, out_specs=out_specs, check_vma=False)
```

```python
import functools

import jax
import jax.numpy as jnp
from jax import lax
from jax.experimental import pallas as pl
from jax.experimental.pallas import tpu as pltpu
from jax.sharding import PartitionSpec as P

KB = 40
LANES = 128
INNER = 4
UNIT = 8
VMEM_LIMIT = 24 * 1024 * 1024


def tile_of(rows):
    return max(t for t in range(LANES, min(rows, 512) + 1, LANES) if rows % t == 0)


def whole(memory):
    return pl.BlockSpec(memory_space=memory)


def turn_by_i(rows):
    half = rows.shape[1] // 2
    swapped = pltpu.roll(rows, half, 1)
    column = lax.broadcasted_iota(jnp.int32, swapped.shape, 1)
    return jnp.where(column < half, -swapped, swapped)


def owner_of(distance, ways):
    return lax.rem(lax.axis_index("beamk") - distance + ways, ways)


def first_tile(m_value, owner, piece_rows, tile):
    return jnp.minimum(jnp.maximum(m_value - owner * piece_rows, 0) // tile, piece_rows // tile)


def first_kernel(
    ways, tile, m_list, sky, wigner, beam, part, factors, info, m_ref, sky_in, wigner_in, beam_in, own, m_sem, sky_sem, wigner_sem, distant_sem, beam_sem
):
    slots, piece_rows, columns = sky.shape
    k_local, cycles = wigner.shape[1], wigner.shape[2]
    rows = k_local * cycles
    tiles = piece_rows // tile
    all_tiles = ways * tiles
    first_k = lax.axis_index("beamk") * k_local - KB // 2
    last = tiles - 1

    def m_copy():
        return pltpu.make_async_copy(m_list, m_ref, m_sem)

    def beam_copy(distance, half):
        span = pl.ds(pl.multiple_of(owner_of(distance, ways) * piece_rows, tile), piece_rows)
        return pltpu.make_async_copy(beam.at[:, half, span], beam_in.at[half, :, span], beam_sem.at[distance, half])

    def sky_copy(slot, step):
        span = pl.ds(pl.multiple_of(step * tile, tile), tile)
        return pltpu.make_async_copy(sky.at[slot, span], sky_in.at[slot, span], sky_sem.at[slot, step])

    def wigner_copy(slot, step):
        start = pl.multiple_of(owner_of(0, ways) * piece_rows + step * tile, tile)
        span = pl.ds(start, tile)
        return pltpu.make_async_copy(wigner.at[slot, :, :, span], wigner_in.at[slot, :, :, span], wigner_sem.at[slot, step])

    def distant_copy(distance, slot):
        span = pl.ds(pl.multiple_of(owner_of(distance, ways) * piece_rows, tile), piece_rows)
        return pltpu.make_async_copy(wigner.at[slot, :, :, span], wigner_in.at[slot, :, :, span], distant_sem.at[distance - 1, slot])

    def begin(distance, slot):
        return first_tile(m_ref[slot], owner_of(distance, ways), piece_rows, tile)

    def fill(target, distance, slot, step):
        index = owner_of(distance, ways) * tiles + step
        rows_of = pl.ds(pl.multiple_of(index * tile, tile), tile)
        index = jnp.where(index == m_ref[slot] // tile, all_tiles + slot, index)
        span = pl.ds(pl.multiple_of(index * tile, tile), tile)
        for k in range(k_local):
            values = wigner_in[slot, k, :, rows_of]
            for half in range(2):
                factor = jnp.broadcast_to(beam_in[half, k : k + 1, span], (cycles, tile)).astype(jnp.bfloat16)
                target[half * rows + k * cycles : half * rows + (k + 1) * cycles, :] = values * factor

    def cut(slot):
        index = m_ref[slot] // tile
        degrees = index * tile + lax.broadcasted_iota(jnp.int32, (k_local, tile), 1)
        k_values = first_k + lax.broadcasted_iota(jnp.int32, (k_local, tile), 0)
        inside = degrees >= jnp.maximum(m_ref[slot], jnp.abs(k_values))
        span = pl.ds(pl.multiple_of(index * tile, tile), tile)
        for half in range(2):
            beam_in[half, :, (all_tiles + slot) * tile : (all_tiles + slot + 1) * tile] = jnp.where(inside, beam_in[half, :, span], 0.0)

    def cut_in(distance, slot):
        return m_ref[slot] // piece_rows == owner_of(distance, ways)

    def upper(distance):
        return 2 * (owner_of(distance, ways) + 1) > ways

    def where_needed(distance, slot, do):
        if slot % 2 == 0:
            do()
        else:
            pl.when(upper(distance))(do)

    m_copy().start()
    for slot in range(slots):

        def fetch(slot=slot):
            for step in reversed(range(tiles)):
                wigner_copy(slot, step).start()
                if slot == 0 and step == last:
                    for half in range(2):
                        beam_copy(0, half).start()
                sky_copy(slot, step).start()

        where_needed(0, slot, fetch)
    for distance in range(1, ways):
        for half in range(2):
            beam_copy(distance, half).start()
        for slot in range(slots):
            where_needed(distance, slot, lambda distance=distance, slot=slot: distant_copy(distance, slot).start())
    m_copy().wait()
    for slot in range(slots):
        info[slot : slot + 1, :] = jnp.full((1, LANES), m_ref[slot].astype(jnp.float32))
    def beam_arrives(distance):
        for half in range(2):
            beam_copy(distance, half).wait()
        for slot in range(slots):
            pl.when(cut_in(distance, slot))(functools.partial(cut, slot))

    beam_arrives(0)

    @pl.loop(0, slots)
    def _(slot):
        begins = begin(0, slot)

        @pl.loop(begins, tiles)
        def _(later):
            step = tiles - 1 - later + begins
            wigner_copy(slot, step).wait()
            span = pl.ds(pl.multiple_of(step * tile, tile), tile)
            fill(own.at[:, span], 0, slot, step)
            sky_copy(slot, step).wait()

        for skipped in range(tiles):

            @pl.when(begins == skipped)
            def _():
                span = slice(skipped * tile, piece_rows)
                part[slot] = jnp.dot(own[:, span], sky_in[slot, span], preferred_element_type=jnp.float32)

        @pl.when(begins == tiles)
        def _():
            part[slot] = jnp.zeros(part.shape[1:], part.dtype)

    for distance in range(1, ways):
        beam_arrives(distance)
        for slot in range(slots):
            where_needed(distance, slot, lambda distance=distance, slot=slot: distant_copy(distance, slot).wait())

        @pl.loop(0, slots)
        def _(slot):
            @pl.loop(begin(distance, slot), tiles)
            def _(step):
                span = pl.ds(pl.multiple_of(step * tile, tile), tile)
                fill(factors.at[distance - 1, slot, :, span], distance, slot, step)

    for slot in range(slots):

        def drop(slot=slot):
            @pl.loop(0, begin(0, slot))
            def _(step):
                wigner_copy(slot, step).wait()
                sky_copy(slot, step).wait()

        where_needed(0, slot, drop)


class Plan:
    def __init__(self, peers, width):
        self.outer = peers // INNER
        self.half = self.outer // 2
        self.units = -(-width // UNIT)
        self.early = (3 * self.units + 2) // 5
        self.late = self.units - self.early
        self.mixed = self.half * (self.units + self.late)

    def in_mixed(self, outer, unit):
        if outer < self.half:
            return outer * self.units + unit
        return self.half * self.units + (outer - self.half) * self.late + unit - self.early


def second_kernel(ways, plan, width, tile, info, _, factors, *refs):
    pieces, refs = refs[: ways - 1], refs[ways - 1 :]
    straight, mixed, (acc, turned) = refs[: plan.half], refs[plan.half : plan.half + INNER], refs[plan.half + INNER :]
    slots, rows, columns = acc.shape
    rows = rows // 2
    piece_rows = pieces[0].shape[1]
    tiles = piece_rows // tile
    cycles = plan.outer * INNER
    k_local = width // slots
    pitch = turned.shape[1] // cycles

    @pl.loop(0, slots)
    def _(slot):
        m_value = jnp.max(info[pl.ds(slot, 1), :]).astype(jnp.int32)
        for distance in range(1, ways):
            missing = first_tile(m_value, owner_of(distance, ways), piece_rows, tile)
            for skipped in range(tiles):

                @pl.when(missing == skipped)
                def _():
                    span = slice(skipped * tile, piece_rows)
                    acc[slot] += jnp.dot(
                        factors[distance - 1, slot, :, span],
                        pieces[distance - 1][slot, span],
                        preferred_element_type=jnp.float32,
                    )

        for k in range(k_local):
            span = slice(k * cycles, (k + 1) * cycles)
            total = acc[slot, span] + turn_by_i(acc[slot, rows + k * cycles : rows + (k + 1) * cycles])
            for lane in range(columns // LANES):
                turned[lane, pl.ds(slot * k_local + k, cycles, stride=pitch), :] = total[:, lane * LANES : (lane + 1) * LANES]

    me = lax.axis_index("blk")
    for distance in range(cycles):
        start = (me ^ distance) * pitch
        outer, inner = divmod(distance, INNER)
        for lane in range(columns // LANES):
            span = slice(lane * LANES, (lane + 1) * LANES)
            block = turned[lane, pl.ds(start, plan.units * UNIT), :]
            for unit in range(plan.units):
                values = block[unit * UNIT : (unit + 1) * UNIT].astype(jnp.bfloat16)
                if outer >= plan.half and unit < plan.early:
                    straight[outer - plan.half][inner * plan.early + unit, :, span] = values
                else:
                    mixed[inner][plan.in_mixed(outer, unit), :, span] = values


def regroup_kernel(plan, *refs):
    mixed, straight, refs = refs[:INNER], refs[INNER : plan.half + INNER], refs[plan.half + INNER :]
    spread, onward = refs[: INNER - 1], refs[INNER - 1 :]
    for outer in range(plan.half):
        for inner in range(1, INNER):
            spread[inner - 1][outer * plan.early : (outer + 1) * plan.early] = straight[outer][
                inner * plan.early : (inner + 1) * plan.early
            ]
    for outer in range(1, plan.outer):
        first = 0 if outer < plan.half else plan.early
        count = plan.units - first
        for inner in range(INNER):
            place = plan.in_mixed(outer, first)
            onward[outer - 1][inner * count : (inner + 1) * count] = mixed[inner][place : place + count]


def place_kernel(half, table, slots, *refs):
    out, turned, staged, sem = refs[-4:]
    k_local, slot_count, columns = staged.shape
    pitch = turned.shape[1] // k_local
    me = lax.axis_index("blk")
    for lane in range(columns // LANES):
        span = slice(lane * LANES, (lane + 1) * LANES)
        for distance, units in enumerate(table):
            source = (me ^ distance) % len(table)
            for unit, (array, place) in enumerate(units):
                values = refs[array][place, :, span].astype(jnp.float32)
                for slot in range(slots):
                    first = max(slot * k_local, unit * UNIT)
                    end = min((slot + 1) * k_local, (unit + 1) * UNIT)
                    if first < end:
                        row = (first - slot * k_local) * pitch + slots * source + slot
                        turned[lane, pl.ds(row, end - first, stride=pitch), :] = values[first - unit * UNIT : end - unit * UNIT]
        for k in range(k_local):
            staged[k, :, span] = turned[lane, k * pitch : k * pitch + slot_count].astype(staged.dtype)
    here = me // len(table)
    start = pl.multiple_of((here if half == 0 else 1 - here) * slot_count, slot_count)
    copy = pltpu.make_async_copy(staged, out.at[:, pl.ds(start, slot_count), :], sem)
    copy.start()
    copy.wait()


def local(sky, beam, wigner, m_list, *, ways, peers):
    slots, piece_rows, columns = sky.shape
    _, k_local, cycles, degrees = wigner.shape
    rows = k_local * cycles
    tile = tile_of(piece_rows)
    tiles = piece_rows // tile
    lane_tiles = columns // LANES
    width = slots * k_local
    params = pltpu.CompilerParams(vmem_limit_bytes=VMEM_LIMIT)

    pieces = []
    for shift in range(1, ways):
        perm = [(c, (c + shift) % ways) for c in range(ways)]
        pieces.append(pltpu.with_memory_space_constraint(lax.ppermute(sky, "beamk", perm), pltpu.VMEM))
    sky, beam, wigner, m_list = (pltpu.with_memory_space_constraint(x, pltpu.HBM) for x in (sky, beam, wigner, m_list))

    part, factors, info = pl.pallas_call(
        functools.partial(first_kernel, ways, tile),
        out_shape=(
            pltpu.VMEM((slots, 2 * rows, columns), jnp.float32),
            pltpu.VMEM((ways - 1, slots, 2 * rows, piece_rows), jnp.bfloat16),
            pltpu.VMEM((8, LANES), jnp.float32),
        ),
        in_specs=[whole(pltpu.HBM)] * 4,
        out_specs=(whole(pltpu.VMEM),) * 3,
        scratch_shapes=[
            pltpu.SMEM(m_list.shape, jnp.int32),
            pltpu.VMEM((slots, piece_rows, columns), jnp.bfloat16),
            pltpu.VMEM(wigner.shape, jnp.bfloat16),
            pltpu.VMEM((2, k_local, degrees + slots * tile), jnp.float32),
            pltpu.VMEM((2 * rows, piece_rows), jnp.bfloat16),
            pltpu.SemaphoreType.DMA,
            pltpu.SemaphoreType.DMA((slots, tiles)),
            pltpu.SemaphoreType.DMA((slots, tiles)),
            pltpu.SemaphoreType.DMA((ways - 1, slots)),
            pltpu.SemaphoreType.DMA((ways, 2)),
        ],
        compiler_params=params,
        cost_estimate=pl.CostEstimate(
            flops=4 * slots * rows * piece_rows * columns, bytes_accessed=8 * 1024 * 1024, transcendentals=0
        ),
        name="own_half",
    )(m_list, sky, wigner, beam)

    plan = Plan(peers, width)

    def units(count):
        return pltpu.VMEM((count, UNIT, columns), jnp.bfloat16)

    *sends, _ = pl.pallas_call(
        functools.partial(second_kernel, ways, plan, width, tile),
        out_shape=[units(INNER * plan.early)] * plan.half + [units(plan.mixed)] * INNER + [pltpu.VMEM(part.shape, part.dtype)],
        in_specs=[whole(pltpu.VMEM)] * (ways + 2),
        out_specs=[whole(pltpu.VMEM)] * (plan.half + INNER + 1),
        input_output_aliases={1: plan.half + INNER},
        scratch_shapes=[
            pltpu.VMEM((lane_tiles, cycles * (plan.units * UNIT + 1), LANES), jnp.float32),
        ],
        compiler_params=params,
        cost_estimate=pl.CostEstimate(
            flops=4 * slots * rows * piece_rows * columns, bytes_accessed=8 * 1024 * 1024, transcendentals=0
        ),
        name="other_half",
    )(info, part, factors, *pieces)
    straight, mixed = sends[: plan.half], sends[plan.half :]

    def send(array, distance):
        perm = [(b, b ^ distance) for b in range(peers)]
        return pltpu.with_memory_space_constraint(lax.ppermute(array, "blk", perm), pltpu.VMEM)

    outer_far = range(plan.half, plan.outer)
    straight = [send(array, outer * INNER) for array, outer in zip(straight, outer_far)]
    for inner in reversed(range(1, INNER)):
        mixed[inner] = send(mixed[inner], inner)
    counts = [plan.half * plan.early] * (INNER - 1)
    counts += [INNER * (plan.units if outer < plan.half else plan.late) for outer in range(1, plan.outer)]
    regrouped = pl.pallas_call(
        functools.partial(regroup_kernel, plan),
        out_shape=[units(count) for count in counts],
        in_specs=[whole(pltpu.VMEM)] * (plan.half + INNER),
        out_specs=[whole(pltpu.VMEM)] * len(counts),
        compiler_params=params,
        name="regroup",
    )(*mixed, *straight)
    spread, onward = list(regrouped[: INNER - 1]), list(regrouped[INNER - 1 :])
    for outer in [*outer_far, *range(1, plan.half)]:
        onward[outer - 1] = send(onward[outer - 1], outer * INNER)
    for inner in reversed(range(1, INNER)):
        spread[inner - 1] = send(spread[inner - 1], inner)

    near, far = [], []
    for outer in range(plan.half):
        for inner in range(INNER):
            if outer == 0:
                near.append([(inner, unit) for unit in range(plan.units)])
            else:
                near.append([(INNER + outer - 1, inner * plan.units + unit) for unit in range(plan.units)])
            if inner == 0:
                first = [(outer, unit) for unit in range(plan.early)]
            else:
                first = [(plan.half + inner - 1, outer * plan.early + unit) for unit in range(plan.early)]
            far.append(first + [(plan.half + INNER - 1 + outer, inner * plan.late + unit) for unit in range(plan.late)])
    slot_count = slots * plan.half * INNER
    out = None
    for half, table, operands in (
        (0, near, [*mixed, *onward[: plan.half - 1]]),
        (1, far, [*straight, *spread, *onward[plan.half - 1 :]]),
    ):
        in_specs = [whole(pltpu.VMEM)] * len(operands)
        if half:
            operands.append(out)
            in_specs.append(whole(pltpu.HBM))
        out = pl.pallas_call(
            functools.partial(place_kernel, half, table, slots),
            out_shape=pltpu.HBM((k_local, slots * peers, columns), jnp.bfloat16),
            in_specs=in_specs,
            out_specs=whole(pltpu.HBM),
            input_output_aliases={len(operands) - 1: 0} if half else {},
            scratch_shapes=[
                pltpu.VMEM((lane_tiles, k_local * (slot_count + 1), LANES), jnp.float32),
                pltpu.VMEM((k_local, slot_count, columns), jnp.bfloat16),
                pltpu.SemaphoreType.DMA,
            ],
            compiler_params=params,
            name="place",
        )(*operands)
    return out.transpose(1, 0, 2)[None]


def solution(mesh):
    in_specs = (
        P("blk", "beamk", None),
        P("beamk", None, None),
        P("blk", "beamk", None, None),
        P("blk"),
    )
    out_specs = P("blk", None, "beamk", None)
    body = functools.partial(local, ways=mesh.shape["beamk"], peers=mesh.shape["blk"])
    return jax.shard_map(body, mesh=mesh, in_specs=in_specs, out_specs=out_specs, check_vma=False)
```

```python
import functools

import jax
import jax.numpy as jnp
from jax import lax
from jax.experimental import pallas as pl
from jax.experimental.pallas import tpu as pltpu
from jax.sharding import PartitionSpec as P

KB = 40
LANES = 128
INNER = 4
VMEM_LIMIT = 24 * 1024 * 1024


def tile_of(rows):
    return max(t for t in range(LANES, min(rows, 512) + 1, LANES) if rows % t == 0)


def whole(memory):
    return pl.BlockSpec(memory_space=memory)


def turn_by_i(rows):
    half = rows.shape[1] // 2
    swapped = pltpu.roll(rows, half, 1)
    column = lax.broadcasted_iota(jnp.int32, swapped.shape, 1)
    return jnp.where(column < half, -swapped, swapped)


def owner_of(distance, ways):
    return lax.rem(lax.axis_index("beamk") - distance + ways, ways)


def first_tile(m_value, owner, piece_rows, tile):
    return jnp.minimum(jnp.maximum(m_value - owner * piece_rows, 0) // tile, piece_rows // tile)


def first_kernel(
    ways, tile, m_list, sky, wigner, beam, part, factors, info, m_ref, sky_in, wigner_in, beam_in, own, m_sem, sky_sem, wigner_sem, distant_sem, beam_sem
):
    slots, piece_rows, columns = sky.shape
    k_local, cycles = wigner.shape[1], wigner.shape[2]
    rows = k_local * cycles
    tiles = piece_rows // tile
    all_tiles = ways * tiles
    first_k = lax.axis_index("beamk") * k_local - KB // 2
    last = tiles - 1

    def m_copy():
        return pltpu.make_async_copy(m_list, m_ref, m_sem)

    def beam_copy(distance, half):
        span = pl.ds(pl.multiple_of(owner_of(distance, ways) * piece_rows, tile), piece_rows)
        return pltpu.make_async_copy(beam.at[:, half, span], beam_in.at[half, :, span], beam_sem.at[distance, half])

    def sky_copy(slot, step):
        span = pl.ds(pl.multiple_of(step * tile, tile), tile)
        return pltpu.make_async_copy(sky.at[slot, span], sky_in.at[slot, span], sky_sem.at[slot, step])

    def wigner_copy(slot, step):
        start = pl.multiple_of(owner_of(0, ways) * piece_rows + step * tile, tile)
        span = pl.ds(start, tile)
        return pltpu.make_async_copy(wigner.at[slot, :, :, span], wigner_in.at[slot, :, :, span], wigner_sem.at[slot, step])

    def distant_copy(distance, slot):
        span = pl.ds(pl.multiple_of(owner_of(distance, ways) * piece_rows, tile), piece_rows)
        return pltpu.make_async_copy(wigner.at[slot, :, :, span], wigner_in.at[slot, :, :, span], distant_sem.at[distance - 1, slot])

    def begin(distance, slot):
        return first_tile(m_ref[slot], owner_of(distance, ways), piece_rows, tile)

    def fill(target, distance, slot, step):
        index = owner_of(distance, ways) * tiles + step
        rows_of = pl.ds(pl.multiple_of(index * tile, tile), tile)
        index = jnp.where(index == m_ref[slot] // tile, all_tiles + slot, index)
        span = pl.ds(pl.multiple_of(index * tile, tile), tile)
        for k in range(k_local):
            values = wigner_in[slot, k, :, rows_of]
            for half in range(2):
                factor = jnp.broadcast_to(beam_in[half, k : k + 1, span], (cycles, tile)).astype(jnp.bfloat16)
                target[half * rows + k * cycles : half * rows + (k + 1) * cycles, :] = values * factor

    def cut(slot):
        index = m_ref[slot] // tile
        degrees = index * tile + lax.broadcasted_iota(jnp.int32, (k_local, tile), 1)
        k_values = first_k + lax.broadcasted_iota(jnp.int32, (k_local, tile), 0)
        inside = degrees >= jnp.maximum(m_ref[slot], jnp.abs(k_values))
        span = pl.ds(pl.multiple_of(index * tile, tile), tile)
        for half in range(2):
            beam_in[half, :, (all_tiles + slot) * tile : (all_tiles + slot + 1) * tile] = jnp.where(inside, beam_in[half, :, span], 0.0)

    def cut_in(distance, slot):
        return m_ref[slot] // piece_rows == owner_of(distance, ways)

    def upper(distance):
        return 2 * (owner_of(distance, ways) + 1) > ways

    def where_needed(distance, slot, do):
        if slot % 2 == 0:
            do()
        else:
            pl.when(upper(distance))(do)

    m_copy().start()
    for slot in range(slots):

        def fetch(slot=slot):
            for step in reversed(range(tiles)):
                wigner_copy(slot, step).start()
                if slot == 0 and step == last:
                    for half in range(2):
                        beam_copy(0, half).start()
                sky_copy(slot, step).start()

        where_needed(0, slot, fetch)
    for distance in range(1, ways):
        for half in range(2):
            beam_copy(distance, half).start()
        for slot in range(slots):
            where_needed(distance, slot, lambda distance=distance, slot=slot: distant_copy(distance, slot).start())
    m_copy().wait()
    for slot in range(slots):
        info[slot : slot + 1, :] = jnp.full((1, LANES), m_ref[slot].astype(jnp.float32))
    def beam_arrives(distance):
        for half in range(2):
            beam_copy(distance, half).wait()
        for slot in range(slots):
            pl.when(cut_in(distance, slot))(functools.partial(cut, slot))

    beam_arrives(0)

    @pl.loop(0, slots)
    def _(slot):
        begins = begin(0, slot)

        @pl.loop(begins, tiles)
        def _(later):
            step = tiles - 1 - later + begins
            wigner_copy(slot, step).wait()
            span = pl.ds(pl.multiple_of(step * tile, tile), tile)
            fill(own.at[:, span], 0, slot, step)
            sky_copy(slot, step).wait()

        for skipped in range(tiles):

            @pl.when(begins == skipped)
            def _():
                span = slice(skipped * tile, piece_rows)
                part[slot] = jnp.dot(own[:, span], sky_in[slot, span], preferred_element_type=jnp.float32)

        @pl.when(begins == tiles)
        def _():
            part[slot] = jnp.zeros(part.shape[1:], part.dtype)

    for distance in range(1, ways):
        beam_arrives(distance)
        for slot in range(slots):
            where_needed(distance, slot, lambda distance=distance, slot=slot: distant_copy(distance, slot).wait())

        @pl.loop(0, slots)
        def _(slot):
            @pl.loop(begin(distance, slot), tiles)
            def _(step):
                span = pl.ds(pl.multiple_of(step * tile, tile), tile)
                fill(factors.at[distance - 1, slot, :, span], distance, slot, step)

    for slot in range(slots):

        def drop(slot=slot):
            @pl.loop(0, begin(0, slot))
            def _(step):
                wigner_copy(slot, step).wait()
                sky_copy(slot, step).wait()

        where_needed(0, slot, drop)


def second_kernel(ways, outer, tile, info, _, factors, *refs):
    pieces, refs = refs[: ways - 1], refs[ways - 1 :]
    count = outer // 2
    near, far, (acc, turned) = refs[:count], refs[count : count + INNER], refs[count + INNER :]
    slots, rows, columns = acc.shape
    rows = rows // 2
    piece_rows = pieces[0].shape[1]
    tiles = piece_rows // tile
    width = far[0].shape[1]
    cycles = outer * INNER
    k_local = width // slots
    pitch = turned.shape[1] // cycles

    @pl.loop(0, slots)
    def _(slot):
        m_value = jnp.max(info[pl.ds(slot, 1), :]).astype(jnp.int32)
        for distance in range(1, ways):
            missing = first_tile(m_value, owner_of(distance, ways), piece_rows, tile)
            for skipped in range(tiles):

                @pl.when(missing == skipped)
                def _():
                    span = slice(skipped * tile, piece_rows)
                    acc[slot] += jnp.dot(
                        factors[distance - 1, slot, :, span],
                        pieces[distance - 1][slot, span],
                        preferred_element_type=jnp.float32,
                    )

        for k in range(k_local):
            span = slice(k * cycles, (k + 1) * cycles)
            total = acc[slot, span] + turn_by_i(acc[slot, rows + k * cycles : rows + (k + 1) * cycles])
            for lane in range(columns // LANES):
                turned[lane, pl.ds(slot * k_local + k, cycles, stride=pitch), :] = total[:, lane * LANES : (lane + 1) * LANES]

    me = lax.axis_index("blk")
    for distance in range(cycles):
        start = (me ^ distance) * pitch
        for lane in range(columns // LANES):
            block = turned[lane, pl.ds(start, width), :].astype(jnp.bfloat16)
            away, inner = divmod(distance, INNER)
            span = slice(lane * LANES, (lane + 1) * LANES)
            if away < count:
                near[away][inner, :, span] = block
            else:
                far[inner][away - count, :, span] = block


def regroup_kernel(count, *refs):
    near, far, refs = refs[:count], refs[count : count + INNER], refs[count + INNER :]
    for index in range(count):
        for inner in range(INNER):
            refs[index][inner] = far[inner][index]
            if inner:
                refs[count + inner - 1][index] = near[index][inner]


def place_kernel(half, count, *refs):
    out, turned, staged, sem = refs[-4:]
    k_local, slot_count, columns = staged.shape
    width = refs[0].shape[1]
    slots = width // k_local
    pitch = turned.shape[1] // k_local
    me = lax.axis_index("blk")
    for lane in range(columns // LANES):
        span = slice(lane * LANES, (lane + 1) * LANES)
        for index in range(count):
            for inner in range(INNER):
                if half:
                    block = refs[index][inner, :, span]
                else:
                    block = refs[count + inner - 1][index, :, span] if inner else refs[index][0, :, span]
                block = block.astype(jnp.float32)
                source = (me ^ (index * INNER + inner)) % (count * INNER)
                for slot in range(slots):
                    turned[lane, pl.ds(slots * source + slot, k_local, stride=pitch), :] = block[slot * k_local : (slot + 1) * k_local]
        for k in range(k_local):
            staged[k, :, span] = turned[lane, k * pitch : k * pitch + slot_count].astype(staged.dtype)
    here = me // (count * INNER)
    start = pl.multiple_of((here if half == 0 else 1 - here) * slot_count, slot_count)
    copy = pltpu.make_async_copy(staged, out.at[:, pl.ds(start, slot_count), :], sem)
    copy.start()
    copy.wait()


def local(sky, beam, wigner, m_list, *, ways, peers):
    slots, piece_rows, columns = sky.shape
    _, k_local, cycles, degrees = wigner.shape
    rows = k_local * cycles
    tile = tile_of(piece_rows)
    tiles = piece_rows // tile
    lane_tiles = columns // LANES
    width = slots * k_local
    params = pltpu.CompilerParams(vmem_limit_bytes=VMEM_LIMIT)

    pieces = []
    for shift in range(1, ways):
        perm = [(c, (c + shift) % ways) for c in range(ways)]
        pieces.append(pltpu.with_memory_space_constraint(lax.ppermute(sky, "beamk", perm), pltpu.VMEM))
    sky, beam, wigner, m_list = (pltpu.with_memory_space_constraint(x, pltpu.HBM) for x in (sky, beam, wigner, m_list))

    part, factors, info = pl.pallas_call(
        functools.partial(first_kernel, ways, tile),
        out_shape=(
            pltpu.VMEM((slots, 2 * rows, columns), jnp.float32),
            pltpu.VMEM((ways - 1, slots, 2 * rows, piece_rows), jnp.bfloat16),
            pltpu.VMEM((8, LANES), jnp.float32),
        ),
        in_specs=[whole(pltpu.HBM)] * 4,
        out_specs=(whole(pltpu.VMEM),) * 3,
        scratch_shapes=[
            pltpu.SMEM(m_list.shape, jnp.int32),
            pltpu.VMEM((slots, piece_rows, columns), jnp.bfloat16),
            pltpu.VMEM(wigner.shape, jnp.bfloat16),
            pltpu.VMEM((2, k_local, degrees + slots * tile), jnp.float32),
            pltpu.VMEM((2 * rows, piece_rows), jnp.bfloat16),
            pltpu.SemaphoreType.DMA,
            pltpu.SemaphoreType.DMA((slots, tiles)),
            pltpu.SemaphoreType.DMA((slots, tiles)),
            pltpu.SemaphoreType.DMA((ways - 1, slots)),
            pltpu.SemaphoreType.DMA((ways, 2)),
        ],
        compiler_params=params,
        cost_estimate=pl.CostEstimate(
            flops=4 * slots * rows * piece_rows * columns, bytes_accessed=8 * 1024 * 1024, transcendentals=0
        ),
        name="own_half",
    )(m_list, sky, wigner, beam)

    outer = peers // INNER
    count = outer // 2

    def blocks(number):
        return pltpu.VMEM((number, width, columns), jnp.bfloat16)

    *sends, _ = pl.pallas_call(
        functools.partial(second_kernel, ways, outer, tile),
        out_shape=[blocks(INNER)] * count + [blocks(count)] * INNER + [pltpu.VMEM(part.shape, part.dtype)],
        in_specs=[whole(pltpu.VMEM)] * (ways + 2),
        out_specs=[whole(pltpu.VMEM)] * (count + INNER + 1),
        input_output_aliases={1: count + INNER},
        scratch_shapes=[
            pltpu.VMEM((lane_tiles, cycles * (width + 1 - width % 2), LANES), jnp.float32),
        ],
        compiler_params=params,
        cost_estimate=pl.CostEstimate(
            flops=4 * slots * rows * piece_rows * columns, bytes_accessed=8 * 1024 * 1024, transcendentals=0
        ),
        name="other_half",
    )(info, part, factors, *pieces)

    def send(array, distance):
        perm = [(b, b ^ distance) for b in range(peers)]
        return pltpu.with_memory_space_constraint(lax.ppermute(array, "blk", perm), pltpu.VMEM)

    near, far = list(sends[:count]), list(sends[count:])
    for inner in reversed(range(1, INNER)):
        far[inner] = send(far[inner], inner)
    for index in range(1, count):
        near[index] = send(near[index], index * INNER)
    shapes = [blocks(INNER)] * count + [blocks(count)] * (INNER - 1)
    regrouped = pl.pallas_call(
        functools.partial(regroup_kernel, count),
        out_shape=shapes,
        in_specs=[whole(pltpu.VMEM)] * (count + INNER),
        out_specs=[whole(pltpu.VMEM)] * len(shapes),
        compiler_params=params,
        name="regroup",
    )(*near, *far)
    far = [send(array, (count + index) * INNER) for index, array in enumerate(regrouped[:count])]
    moved = list(regrouped[count:])
    for inner in reversed(range(1, INNER)):
        moved[inner - 1] = send(moved[inner - 1], inner)
    near += moved
    out = None
    for half, operands in enumerate((near, far)):
        slot_count = slots * count * INNER
        in_specs = [whole(pltpu.VMEM)] * len(operands)
        if half:
            operands.append(out)
            in_specs.append(whole(pltpu.HBM))
        out = pl.pallas_call(
            functools.partial(place_kernel, half, count),
            out_shape=pltpu.HBM((k_local, slots * peers, columns), jnp.bfloat16),
            in_specs=in_specs,
            out_specs=whole(pltpu.HBM),
            input_output_aliases={len(operands) - 1: 0} if half else {},
            scratch_shapes=[
                pltpu.VMEM((lane_tiles, k_local * (slot_count + 1), LANES), jnp.float32),
                pltpu.VMEM((k_local, slot_count, columns), jnp.bfloat16),
                pltpu.SemaphoreType.DMA,
            ],
            compiler_params=params,
            name="place",
        )(*operands)
    return out.transpose(1, 0, 2)[None]


def solution(mesh):
    in_specs = (
        P("blk", "beamk", None),
        P("beamk", None, None),
        P("blk", "beamk", None, None),
        P("blk"),
    )
    out_specs = P("blk", None, "beamk", None)
    body = functools.partial(local, ways=mesh.shape["beamk"], peers=mesh.shape["blk"])
    return jax.shard_map(body, mesh=mesh, in_specs=in_specs, out_specs=out_specs, check_vma=False)
```

```python
import functools

import jax
import jax.numpy as jnp
from jax import lax
from jax.experimental import pallas as pl
from jax.experimental.pallas import tpu as pltpu
from jax.sharding import PartitionSpec as P

KB = 40
LANES = 128
INNER = 4
VMEM_LIMIT = 24 * 1024 * 1024


def tile_of(rows):
    return max(t for t in range(LANES, min(rows, 512) + 1, LANES) if rows % t == 0)


def whole(memory):
    return pl.BlockSpec(memory_space=memory)


def turn_by_i(rows):
    half = rows.shape[1] // 2
    swapped = pltpu.roll(rows, half, 1)
    column = lax.broadcasted_iota(jnp.int32, swapped.shape, 1)
    return jnp.where(column < half, -swapped, swapped)


def owner_of(distance, ways):
    return lax.rem(lax.axis_index("beamk") - distance + ways, ways)


def first_tile(m_value, owner, piece_rows, tile):
    return jnp.minimum(jnp.maximum(m_value - owner * piece_rows, 0) // tile, piece_rows // tile)


def first_kernel(
    ways, tile, m_list, sky, wigner, beam, part, factors, info, m_ref, sky_in, wigner_in, beam_in, own, m_sem, sky_sem, wigner_sem, distant_sem, beam_sem
):
    slots, piece_rows, columns = sky.shape
    k_local, cycles = wigner.shape[1], wigner.shape[2]
    rows = k_local * cycles
    tiles = piece_rows // tile
    all_tiles = ways * tiles
    first_k = lax.axis_index("beamk") * k_local - KB // 2
    last = tiles - 1

    def m_copy():
        return pltpu.make_async_copy(m_list, m_ref, m_sem)

    def beam_copy(distance, half):
        span = pl.ds(pl.multiple_of(owner_of(distance, ways) * piece_rows, tile), piece_rows)
        return pltpu.make_async_copy(beam.at[:, half, span], beam_in.at[half, :, span], beam_sem.at[distance, half])

    def sky_copy(slot, step):
        span = pl.ds(pl.multiple_of(step * tile, tile), tile)
        return pltpu.make_async_copy(sky.at[slot, span], sky_in.at[slot, span], sky_sem.at[slot, step])

    def wigner_copy(slot, step):
        start = pl.multiple_of(owner_of(0, ways) * piece_rows + step * tile, tile)
        span = pl.ds(start, tile)
        return pltpu.make_async_copy(wigner.at[slot, :, :, span], wigner_in.at[slot, :, :, span], wigner_sem.at[slot, step])

    def distant_copy(distance, slot):
        span = pl.ds(pl.multiple_of(owner_of(distance, ways) * piece_rows, tile), piece_rows)
        return pltpu.make_async_copy(wigner.at[slot, :, :, span], wigner_in.at[slot, :, :, span], distant_sem.at[distance - 1, slot])

    def begin(distance, slot):
        return first_tile(m_ref[slot], owner_of(distance, ways), piece_rows, tile)

    def fill(target, distance, slot, step):
        index = owner_of(distance, ways) * tiles + step
        rows_of = pl.ds(pl.multiple_of(index * tile, tile), tile)
        index = jnp.where(index == m_ref[slot] // tile, all_tiles + slot, index)
        span = pl.ds(pl.multiple_of(index * tile, tile), tile)
        for k in range(k_local):
            values = wigner_in[slot, k, :, rows_of]
            for half in range(2):
                factor = jnp.broadcast_to(beam_in[half, k : k + 1, span], (cycles, tile)).astype(jnp.bfloat16)
                target[half * rows + k * cycles : half * rows + (k + 1) * cycles, :] = values * factor

    def cut(slot):
        index = m_ref[slot] // tile
        degrees = index * tile + lax.broadcasted_iota(jnp.int32, (k_local, tile), 1)
        k_values = first_k + lax.broadcasted_iota(jnp.int32, (k_local, tile), 0)
        inside = degrees >= jnp.maximum(m_ref[slot], jnp.abs(k_values))
        span = pl.ds(pl.multiple_of(index * tile, tile), tile)
        for half in range(2):
            beam_in[half, :, (all_tiles + slot) * tile : (all_tiles + slot + 1) * tile] = jnp.where(inside, beam_in[half, :, span], 0.0)

    def cut_in(distance, slot):
        return m_ref[slot] // piece_rows == owner_of(distance, ways)

    def upper(distance):
        return 2 * (owner_of(distance, ways) + 1) > ways

    def where_needed(distance, slot, do):
        if slot % 2 == 0:
            do()
        else:
            pl.when(upper(distance))(do)

    m_copy().start()
    for slot in range(slots):

        def fetch(slot=slot):
            for step in reversed(range(tiles)):
                wigner_copy(slot, step).start()
                if slot == 0 and step == last:
                    for half in range(2):
                        beam_copy(0, half).start()
                sky_copy(slot, step).start()

        where_needed(0, slot, fetch)
    for distance in range(1, ways):
        for half in range(2):
            beam_copy(distance, half).start()
        for slot in range(slots):
            where_needed(distance, slot, lambda distance=distance, slot=slot: distant_copy(distance, slot).start())
    m_copy().wait()
    for slot in range(slots):
        info[slot : slot + 1, :] = jnp.full((1, LANES), m_ref[slot].astype(jnp.float32))
    def beam_arrives(distance):
        for half in range(2):
            beam_copy(distance, half).wait()
        for slot in range(slots):
            pl.when(cut_in(distance, slot))(functools.partial(cut, slot))

    beam_arrives(0)

    @pl.loop(0, slots)
    def _(slot):
        begins = begin(0, slot)

        @pl.loop(begins, tiles)
        def _(later):
            step = tiles - 1 - later + begins
            wigner_copy(slot, step).wait()
            span = pl.ds(pl.multiple_of(step * tile, tile), tile)
            fill(own.at[:, span], 0, slot, step)
            sky_copy(slot, step).wait()

        for skipped in range(tiles):

            @pl.when(begins == skipped)
            def _():
                span = slice(skipped * tile, piece_rows)
                part[slot] = jnp.dot(own[:, span], sky_in[slot, span], preferred_element_type=jnp.float32)

        @pl.when(begins == tiles)
        def _():
            part[slot] = jnp.zeros(part.shape[1:], part.dtype)

    for distance in range(1, ways):
        beam_arrives(distance)
        for slot in range(slots):
            where_needed(distance, slot, lambda distance=distance, slot=slot: distant_copy(distance, slot).wait())

        @pl.loop(0, slots)
        def _(slot):
            @pl.loop(begin(distance, slot), tiles)
            def _(step):
                span = pl.ds(pl.multiple_of(step * tile, tile), tile)
                fill(factors.at[distance - 1, slot, :, span], distance, slot, step)

    for slot in range(slots):

        def drop(slot=slot):
            @pl.loop(0, begin(0, slot))
            def _(step):
                wigner_copy(slot, step).wait()
                sky_copy(slot, step).wait()

        where_needed(0, slot, drop)


def crossed(core, outer):
    return (core % 2) * (outer == INNER)


def distance_of(first, second, outer):
    straight = second * INNER + first
    return jnp.where(crossed(lax.axis_index("beamk"), outer) == 1, first * INNER + second, straight)


def second_kernel(ways, outer, tile, info, _, factors, *refs):
    pieces, refs = refs[: ways - 1], refs[ways - 1 :]
    outs, (acc, turned) = refs[:INNER], refs[INNER:]
    slots, rows, columns = acc.shape
    rows = rows // 2
    piece_rows = pieces[0].shape[1]
    tiles = piece_rows // tile
    width = outs[0].shape[1]
    cycles = outer * INNER
    k_local = width // slots
    pitch = turned.shape[1] // cycles

    @pl.loop(0, slots)
    def _(slot):
        m_value = jnp.max(info[pl.ds(slot, 1), :]).astype(jnp.int32)
        for distance in range(1, ways):
            missing = first_tile(m_value, owner_of(distance, ways), piece_rows, tile)
            for skipped in range(tiles):

                @pl.when(missing == skipped)
                def _():
                    span = slice(skipped * tile, piece_rows)
                    acc[slot] += jnp.dot(
                        factors[distance - 1, slot, :, span],
                        pieces[distance - 1][slot, span],
                        preferred_element_type=jnp.float32,
                    )

        for k in range(k_local):
            span = slice(k * cycles, (k + 1) * cycles)
            total = acc[slot, span] + turn_by_i(acc[slot, rows + k * cycles : rows + (k + 1) * cycles])
            for lane in range(columns // LANES):
                turned[lane, pl.ds(slot * k_local + k, cycles, stride=pitch), :] = total[:, lane * LANES : (lane + 1) * LANES]

    me = lax.axis_index("blk")
    for first in range(INNER):
        for second in range(outer):
            start = (me ^ distance_of(first, second, outer)) * pitch
            for lane in range(columns // LANES):
                block = turned[lane, pl.ds(start, width), :].astype(jnp.bfloat16)
                outs[first][second, :, lane * LANES : (lane + 1) * LANES] = block


def regroup_kernel(outer, *refs):
    for second in range(outer):
        for first in range(INNER):
            refs[INNER + second][first] = refs[first][second]


def place_kernel(outer, *refs):
    out, turned, staged, sem = refs[outer:]
    k_local, slot_count, columns = staged.shape
    width = refs[0].shape[1]
    slots = width // k_local
    pitch = turned.shape[1] // k_local
    me = lax.axis_index("blk")
    for lane in range(columns // LANES):
        span = slice(lane * LANES, (lane + 1) * LANES)
        for second in range(outer):
            for first in range(INNER):
                block = refs[second][first, :, span].astype(jnp.float32)
                source = me ^ distance_of(first, second, outer)
                for slot in range(slots):
                    turned[lane, pl.ds(slots * source + slot, k_local, stride=pitch), :] = block[slot * k_local : (slot + 1) * k_local]
    copies = []
    step = -(-k_local // 4)
    for number, start in enumerate(range(0, k_local, step)):
        end = min(start + step, k_local)
        for k in range(start, end):
            for lane in range(columns // LANES):
                values = turned[lane, k * pitch : k * pitch + slot_count]
                staged[k, :, lane * LANES : (lane + 1) * LANES] = values.astype(staged.dtype)
        copies.append(pltpu.make_async_copy(staged.at[start:end], out.at[start:end], sem.at[number]))
        copies[-1].start()
    for copy in copies:
        copy.wait()


def local(sky, beam, wigner, m_list, *, ways, peers):
    slots, piece_rows, columns = sky.shape
    _, k_local, cycles, degrees = wigner.shape
    rows = k_local * cycles
    tile = tile_of(piece_rows)
    tiles = piece_rows // tile
    lane_tiles = columns // LANES
    width = slots * k_local
    params = pltpu.CompilerParams(vmem_limit_bytes=VMEM_LIMIT)

    pieces = []
    for shift in range(1, ways):
        perm = [(c, (c + shift) % ways) for c in range(ways)]
        pieces.append(pltpu.with_memory_space_constraint(lax.ppermute(sky, "beamk", perm), pltpu.VMEM))
    sky, beam, wigner, m_list = (pltpu.with_memory_space_constraint(x, pltpu.HBM) for x in (sky, beam, wigner, m_list))

    part, factors, info = pl.pallas_call(
        functools.partial(first_kernel, ways, tile),
        out_shape=(
            pltpu.VMEM((slots, 2 * rows, columns), jnp.float32),
            pltpu.VMEM((ways - 1, slots, 2 * rows, piece_rows), jnp.bfloat16),
            pltpu.VMEM((8, LANES), jnp.float32),
        ),
        in_specs=[whole(pltpu.HBM)] * 4,
        out_specs=(whole(pltpu.VMEM),) * 3,
        scratch_shapes=[
            pltpu.SMEM(m_list.shape, jnp.int32),
            pltpu.VMEM((slots, piece_rows, columns), jnp.bfloat16),
            pltpu.VMEM(wigner.shape, jnp.bfloat16),
            pltpu.VMEM((2, k_local, degrees + slots * tile), jnp.float32),
            pltpu.VMEM((2 * rows, piece_rows), jnp.bfloat16),
            pltpu.SemaphoreType.DMA,
            pltpu.SemaphoreType.DMA((slots, tiles)),
            pltpu.SemaphoreType.DMA((slots, tiles)),
            pltpu.SemaphoreType.DMA((ways - 1, slots)),
            pltpu.SemaphoreType.DMA((ways, 2)),
        ],
        compiler_params=params,
        cost_estimate=pl.CostEstimate(
            flops=4 * slots * rows * piece_rows * columns, bytes_accessed=8 * 1024 * 1024, transcendentals=0
        ),
        name="own_half",
    )(m_list, sky, wigner, beam)

    outer = peers // INNER

    def blocks(number):
        return pltpu.VMEM((number, width, columns), jnp.bfloat16)

    *sends, _ = pl.pallas_call(
        functools.partial(second_kernel, ways, outer, tile),
        out_shape=[blocks(outer)] * INNER + [pltpu.VMEM(part.shape, part.dtype)],
        in_specs=[whole(pltpu.VMEM)] * (ways + 2),
        out_specs=[whole(pltpu.VMEM)] * (INNER + 1),
        input_output_aliases={1: INNER},
        scratch_shapes=[
            pltpu.VMEM((lane_tiles, cycles * (width + 1 - width % 2), LANES), jnp.float32),
        ],
        compiler_params=params,
        cost_estimate=pl.CostEstimate(
            flops=4 * slots * rows * piece_rows * columns, bytes_accessed=8 * 1024 * 1024, transcendentals=0
        ),
        name="other_half",
    )(info, part, factors, *pieces)

    def send(array, number, step):
        perm = []
        for b in range(peers):
            for core in range(ways):
                over_outer = (step == 0) == bool(crossed(core, outer))
                perm.append((b * ways + core, (b ^ (number * INNER if over_outer else number)) * ways + core))
        return pltpu.with_memory_space_constraint(lax.ppermute(array, ("blk", "beamk"), perm), pltpu.VMEM)

    first = list(sends)
    for number in reversed(range(1, INNER)):
        first[number] = send(first[number], number, 0)
    second = list(
        pl.pallas_call(
            functools.partial(regroup_kernel, outer),
            out_shape=[blocks(INNER)] * outer,
            in_specs=[whole(pltpu.VMEM)] * INNER,
            out_specs=[whole(pltpu.VMEM)] * outer,
            compiler_params=params,
            name="regroup",
        )(*first)
    )
    for number in reversed(range(1, outer)):
        second[number] = send(second[number], number, 1)
    slot_count = slots * peers
    out = pl.pallas_call(
        functools.partial(place_kernel, outer),
        out_shape=pltpu.HBM((k_local, slot_count, columns), jnp.bfloat16),
        in_specs=[whole(pltpu.VMEM)] * outer,
        out_specs=whole(pltpu.HBM),
        scratch_shapes=[
            pltpu.VMEM((lane_tiles, k_local * (slot_count + 1), LANES), jnp.float32),
            pltpu.VMEM((k_local, slot_count, columns), jnp.bfloat16),
            pltpu.SemaphoreType.DMA((4,)),
        ],
        compiler_params=params,
        name="place",
    )(*second)
    return out.transpose(1, 0, 2)[None]


def solution(mesh):
    in_specs = (
        P("blk", "beamk", None),
        P("beamk", None, None),
        P("blk", "beamk", None, None),
        P("blk"),
    )
    out_specs = P("blk", None, "beamk", None)
    body = functools.partial(local, ways=mesh.shape["beamk"], peers=mesh.shape["blk"])
    return jax.shard_map(body, mesh=mesh, in_specs=in_specs, out_specs=out_specs, check_vma=False)
```

```python
import functools

import jax
import jax.numpy as jnp
from jax import lax
from jax.experimental import pallas as pl
from jax.experimental.pallas import tpu as pltpu
from jax.sharding import PartitionSpec as P

KB = 40
LANES = 128
INNER = 4
VMEM_LIMIT = 24 * 1024 * 1024


def tile_of(rows):
    return max(t for t in range(LANES, min(rows, 512) + 1, LANES) if rows % t == 0)


def whole(memory):
    return pl.BlockSpec(memory_space=memory)


def turn_by_i(rows):
    half = rows.shape[1] // 2
    swapped = pltpu.roll(rows, half, 1)
    column = lax.broadcasted_iota(jnp.int32, swapped.shape, 1)
    return jnp.where(column < half, -swapped, swapped)


def owner_of(distance, ways):
    return lax.rem(lax.axis_index("beamk") - distance + ways, ways)


def first_tile(m_value, owner, piece_rows, tile):
    return jnp.minimum(jnp.maximum(m_value - owner * piece_rows, 0) // tile, piece_rows // tile)


def first_kernel(
    ways, tile, m_list, sky, wigner, beam, part, factors, info, m_ref, sky_in, wigner_in, beam_in, own, m_sem, sky_sem, wigner_sem, distant_sem, beam_sem
):
    slots, piece_rows, columns = sky.shape
    k_local, cycles = wigner.shape[1], wigner.shape[2]
    rows = k_local * cycles
    tiles = piece_rows // tile
    all_tiles = ways * tiles
    first_k = lax.axis_index("beamk") * k_local - KB // 2
    last = tiles - 1

    def m_copy():
        return pltpu.make_async_copy(m_list, m_ref, m_sem)

    def beam_copy(distance, half):
        span = pl.ds(pl.multiple_of(owner_of(distance, ways) * piece_rows, tile), piece_rows)
        return pltpu.make_async_copy(beam.at[:, half, span], beam_in.at[half, :, span], beam_sem.at[distance, half])

    def sky_copy(slot, step):
        span = pl.ds(pl.multiple_of(step * tile, tile), tile)
        return pltpu.make_async_copy(sky.at[slot, span], sky_in.at[slot, span], sky_sem.at[slot, step])

    def wigner_copy(slot, step):
        start = pl.multiple_of(owner_of(0, ways) * piece_rows + step * tile, tile)
        span = pl.ds(start, tile)
        return pltpu.make_async_copy(wigner.at[slot, :, :, span], wigner_in.at[slot, :, :, span], wigner_sem.at[slot, step])

    def distant_copy(distance, slot):
        span = pl.ds(pl.multiple_of(owner_of(distance, ways) * piece_rows, tile), piece_rows)
        return pltpu.make_async_copy(wigner.at[slot, :, :, span], wigner_in.at[slot, :, :, span], distant_sem.at[distance - 1, slot])

    def begin(distance, slot):
        return first_tile(m_ref[slot], owner_of(distance, ways), piece_rows, tile)

    def fill(target, distance, slot, step):
        index = owner_of(distance, ways) * tiles + step
        rows_of = pl.ds(pl.multiple_of(index * tile, tile), tile)
        index = jnp.where(index == m_ref[slot] // tile, all_tiles + slot, index)
        span = pl.ds(pl.multiple_of(index * tile, tile), tile)
        for k in range(k_local):
            values = wigner_in[slot, k, :, rows_of]
            for half in range(2):
                factor = jnp.broadcast_to(beam_in[half, k : k + 1, span], (cycles, tile)).astype(jnp.bfloat16)
                target[half * rows + k * cycles : half * rows + (k + 1) * cycles, :] = values * factor

    def cut(slot):
        index = m_ref[slot] // tile
        degrees = index * tile + lax.broadcasted_iota(jnp.int32, (k_local, tile), 1)
        k_values = first_k + lax.broadcasted_iota(jnp.int32, (k_local, tile), 0)
        inside = degrees >= jnp.maximum(m_ref[slot], jnp.abs(k_values))
        span = pl.ds(pl.multiple_of(index * tile, tile), tile)
        for half in range(2):
            beam_in[half, :, (all_tiles + slot) * tile : (all_tiles + slot + 1) * tile] = jnp.where(inside, beam_in[half, :, span], 0.0)

    def cut_in(distance, slot):
        return m_ref[slot] // piece_rows == owner_of(distance, ways)

    def upper(distance):
        return 2 * (owner_of(distance, ways) + 1) > ways

    def where_needed(distance, slot, do):
        if slot % 2 == 0:
            do()
        else:
            pl.when(upper(distance))(do)

    m_copy().start()
    for slot in range(slots):

        def fetch(slot=slot):
            for step in reversed(range(tiles)):
                wigner_copy(slot, step).start()
                if slot == 0 and step == last:
                    for half in range(2):
                        beam_copy(0, half).start()
                sky_copy(slot, step).start()

        where_needed(0, slot, fetch)
    for distance in range(1, ways):
        for half in range(2):
            beam_copy(distance, half).start()
        for slot in range(slots):
            where_needed(distance, slot, lambda distance=distance, slot=slot: distant_copy(distance, slot).start())
    m_copy().wait()
    for slot in range(slots):
        info[slot : slot + 1, :] = jnp.full((1, LANES), m_ref[slot].astype(jnp.float32))
    def beam_arrives(distance):
        for half in range(2):
            beam_copy(distance, half).wait()
        for slot in range(slots):
            pl.when(cut_in(distance, slot))(functools.partial(cut, slot))

    beam_arrives(0)

    @pl.loop(0, slots)
    def _(slot):
        begins = begin(0, slot)

        @pl.loop(begins, tiles)
        def _(later):
            step = tiles - 1 - later + begins
            wigner_copy(slot, step).wait()
            span = pl.ds(pl.multiple_of(step * tile, tile), tile)
            fill(own.at[:, span], 0, slot, step)
            sky_copy(slot, step).wait()

        for skipped in range(tiles):

            @pl.when(begins == skipped)
            def _():
                span = slice(skipped * tile, piece_rows)
                part[slot] = jnp.dot(own[:, span], sky_in[slot, span], preferred_element_type=jnp.float32)

        @pl.when(begins == tiles)
        def _():
            part[slot] = jnp.zeros(part.shape[1:], part.dtype)

    for distance in range(1, ways):
        beam_arrives(distance)
        for slot in range(slots):
            where_needed(distance, slot, lambda distance=distance, slot=slot: distant_copy(distance, slot).wait())

        @pl.loop(0, slots)
        def _(slot):
            @pl.loop(begin(distance, slot), tiles)
            def _(step):
                span = pl.ds(pl.multiple_of(step * tile, tile), tile)
                fill(factors.at[distance - 1, slot, :, span], distance, slot, step)

    for slot in range(slots):

        def drop(slot=slot):
            @pl.loop(0, begin(0, slot))
            def _(step):
                wigner_copy(slot, step).wait()
                sky_copy(slot, step).wait()

        where_needed(0, slot, drop)


def crossed(core, outer):
    return (core % 2) * (outer == INNER)


def distance_of(first, second, outer):
    straight = second * INNER + first
    return jnp.where(crossed(lax.axis_index("beamk"), outer) == 1, first * INNER + second, straight)


def second_kernel(ways, outer, tile, info, _, factors, *refs):
    pieces, refs = refs[: ways - 1], refs[ways - 1 :]
    outs, (acc, turned) = refs[:INNER], refs[INNER:]
    slots, rows, columns = acc.shape
    rows = rows // 2
    piece_rows = pieces[0].shape[1]
    tiles = piece_rows // tile
    width = outs[0].shape[1]
    cycles = outer * INNER
    k_local = width // slots
    pitch = turned.shape[1] // cycles

    @pl.loop(0, slots)
    def _(slot):
        m_value = jnp.max(info[pl.ds(slot, 1), :]).astype(jnp.int32)
        for distance in range(1, ways):
            missing = first_tile(m_value, owner_of(distance, ways), piece_rows, tile)
            for skipped in range(tiles):

                @pl.when(missing == skipped)
                def _():
                    span = slice(skipped * tile, piece_rows)
                    acc[slot] += jnp.dot(
                        factors[distance - 1, slot, :, span],
                        pieces[distance - 1][slot, span],
                        preferred_element_type=jnp.float32,
                    )

        for k in range(k_local):
            span = slice(k * cycles, (k + 1) * cycles)
            total = acc[slot, span] + turn_by_i(acc[slot, rows + k * cycles : rows + (k + 1) * cycles])
            for lane in range(columns // LANES):
                turned[lane, pl.ds(slot * k_local + k, cycles, stride=pitch), :] = total[:, lane * LANES : (lane + 1) * LANES]

    me = lax.axis_index("blk")
    for first in range(INNER):
        for second in range(outer):
            start = (me ^ distance_of(first, second, outer)) * pitch
            for lane in range(columns // LANES):
                block = turned[lane, pl.ds(start, width), :].astype(jnp.bfloat16)
                outs[first][second, :, lane * LANES : (lane + 1) * LANES] = block


def far_first(arrays):
    return [arrays[0], *reversed(arrays[1:])]


def regroup_kernel(outer, *refs):
    arrived, onward = far_first(refs[:INNER]), refs[INNER:]
    for second in range(outer):
        for first in range(INNER):
            onward[second][first] = arrived[first][second]


def place_kernel(outer, *refs):
    arrived, (out, turned, staged, sem) = far_first(refs[:outer]), refs[outer:]
    k_local, slot_count, columns = staged.shape
    width = arrived[0].shape[1]
    slots = width // k_local
    pitch = turned.shape[1] // k_local
    me = lax.axis_index("blk")
    for lane in range(columns // LANES):
        span = slice(lane * LANES, (lane + 1) * LANES)
        for second in range(outer):
            for first in range(INNER):
                block = arrived[second][first, :, span].astype(jnp.float32)
                source = me ^ distance_of(first, second, outer)
                for slot in range(slots):
                    turned[lane, pl.ds(slots * source + slot, k_local, stride=pitch), :] = block[slot * k_local : (slot + 1) * k_local]
    copies = []
    step = -(-k_local // 4)
    for number, start in enumerate(range(0, k_local, step)):
        end = min(start + step, k_local)
        for k in range(start, end):
            for lane in range(columns // LANES):
                values = turned[lane, k * pitch : k * pitch + slot_count]
                staged[k, :, lane * LANES : (lane + 1) * LANES] = values.astype(staged.dtype)
        copies.append(pltpu.make_async_copy(staged.at[start:end], out.at[start:end], sem.at[number]))
        copies[-1].start()
    for copy in copies:
        copy.wait()


def local(sky, beam, wigner, m_list, *, ways, peers):
    slots, piece_rows, columns = sky.shape
    _, k_local, cycles, degrees = wigner.shape
    rows = k_local * cycles
    tile = tile_of(piece_rows)
    tiles = piece_rows // tile
    lane_tiles = columns // LANES
    width = slots * k_local
    params = pltpu.CompilerParams(vmem_limit_bytes=VMEM_LIMIT)

    pieces = []
    for shift in range(1, ways):
        perm = [(c, (c + shift) % ways) for c in range(ways)]
        pieces.append(pltpu.with_memory_space_constraint(lax.ppermute(sky, "beamk", perm), pltpu.VMEM))
    sky, beam, wigner, m_list = (pltpu.with_memory_space_constraint(x, pltpu.HBM) for x in (sky, beam, wigner, m_list))

    part, factors, info = pl.pallas_call(
        functools.partial(first_kernel, ways, tile),
        out_shape=(
            pltpu.VMEM((slots, 2 * rows, columns), jnp.float32),
            pltpu.VMEM((ways - 1, slots, 2 * rows, piece_rows), jnp.bfloat16),
            pltpu.VMEM((8, LANES), jnp.float32),
        ),
        in_specs=[whole(pltpu.HBM)] * 4,
        out_specs=(whole(pltpu.VMEM),) * 3,
        scratch_shapes=[
            pltpu.SMEM(m_list.shape, jnp.int32),
            pltpu.VMEM((slots, piece_rows, columns), jnp.bfloat16),
            pltpu.VMEM(wigner.shape, jnp.bfloat16),
            pltpu.VMEM((2, k_local, degrees + slots * tile), jnp.float32),
            pltpu.VMEM((2 * rows, piece_rows), jnp.bfloat16),
            pltpu.SemaphoreType.DMA,
            pltpu.SemaphoreType.DMA((slots, tiles)),
            pltpu.SemaphoreType.DMA((slots, tiles)),
            pltpu.SemaphoreType.DMA((ways - 1, slots)),
            pltpu.SemaphoreType.DMA((ways, 2)),
        ],
        compiler_params=params,
        cost_estimate=pl.CostEstimate(
            flops=4 * slots * rows * piece_rows * columns, bytes_accessed=8 * 1024 * 1024, transcendentals=0
        ),
        name="own_half",
    )(m_list, sky, wigner, beam)

    outer = peers // INNER

    def blocks(number):
        return pltpu.VMEM((number, width, columns), jnp.bfloat16)

    *sends, _ = pl.pallas_call(
        functools.partial(second_kernel, ways, outer, tile),
        out_shape=[blocks(outer)] * INNER + [pltpu.VMEM(part.shape, part.dtype)],
        in_specs=[whole(pltpu.VMEM)] * (ways + 2),
        out_specs=[whole(pltpu.VMEM)] * (INNER + 1),
        input_output_aliases={1: INNER},
        scratch_shapes=[
            pltpu.VMEM((lane_tiles, cycles * (width + 1 - width % 2), LANES), jnp.float32),
        ],
        compiler_params=params,
        cost_estimate=pl.CostEstimate(
            flops=4 * slots * rows * piece_rows * columns, bytes_accessed=8 * 1024 * 1024, transcendentals=0
        ),
        name="other_half",
    )(info, part, factors, *pieces)

    def send(array, number, step):
        perm = []
        for b in range(peers):
            for core in range(ways):
                over_outer = (step == 0) == bool(crossed(core, outer))
                perm.append((b * ways + core, (b ^ (number * INNER if over_outer else number)) * ways + core))
        return pltpu.with_memory_space_constraint(lax.ppermute(array, ("blk", "beamk"), perm), pltpu.VMEM)

    first = list(sends)
    for number in range(1, INNER):
        first[number] = send(first[number], number, 0)
    second = list(
        pl.pallas_call(
            functools.partial(regroup_kernel, outer),
            out_shape=[blocks(INNER)] * outer,
            in_specs=[whole(pltpu.VMEM)] * INNER,
            out_specs=[whole(pltpu.VMEM)] * outer,
            compiler_params=params,
            name="regroup",
        )(*far_first(first))
    )
    for number in range(1, outer):
        second[number] = send(second[number], number, 1)
    slot_count = slots * peers
    out = pl.pallas_call(
        functools.partial(place_kernel, outer),
        out_shape=pltpu.HBM((k_local, slot_count, columns), jnp.bfloat16),
        in_specs=[whole(pltpu.VMEM)] * outer,
        out_specs=whole(pltpu.HBM),
        scratch_shapes=[
            pltpu.VMEM((lane_tiles, k_local * (slot_count + 1), LANES), jnp.float32),
            pltpu.VMEM((k_local, slot_count, columns), jnp.bfloat16),
            pltpu.SemaphoreType.DMA((4,)),
        ],
        compiler_params=params,
        name="place",
    )(*far_first(second))
    return out.transpose(1, 0, 2)[None]


def solution(mesh):
    in_specs = (
        P("blk", "beamk", None),
        P("beamk", None, None),
        P("blk", "beamk", None, None),
        P("blk"),
    )
    out_specs = P("blk", None, "beamk", None)
    body = functools.partial(local, ways=mesh.shape["beamk"], peers=mesh.shape["blk"])
    return jax.shard_map(body, mesh=mesh, in_specs=in_specs, out_specs=out_specs, check_vma=False)
```

```python
import functools

import jax
import jax.numpy as jnp
from jax import lax
from jax.experimental import pallas as pl
from jax.experimental.pallas import tpu as pltpu
from jax.sharding import PartitionSpec as P

KB = 40
LANES = 128
INNER = 4
VMEM_LIMIT = 24 * 1024 * 1024


def tile_of(rows):
    return max(t for t in range(LANES, min(rows, 512) + 1, LANES) if rows % t == 0)


def whole(memory):
    return pl.BlockSpec(memory_space=memory)


def turn_by_i(rows):
    half = rows.shape[1] // 2
    swapped = pltpu.roll(rows, half, 1)
    column = lax.broadcasted_iota(jnp.int32, swapped.shape, 1)
    return jnp.where(column < half, -swapped, swapped)


def owner_of(distance, ways):
    return lax.rem(lax.axis_index("beamk") - distance + ways, ways)


def first_tile(m_value, owner, piece_rows, tile):
    return jnp.minimum(jnp.maximum(m_value - owner * piece_rows, 0) // tile, piece_rows // tile)


def first_kernel(
    ways, tile, m_list, sky, wigner, beam, part, factors, info, m_ref, sky_in, wigner_in, beam_in, own, m_sem, sky_sem, wigner_sem, distant_sem, beam_sem
):
    slots, piece_rows, columns = sky.shape
    k_local, cycles = wigner.shape[1], wigner.shape[2]
    rows = k_local * cycles
    tiles = piece_rows // tile
    all_tiles = ways * tiles
    first_k = lax.axis_index("beamk") * k_local - KB // 2
    last = tiles - 1

    def m_copy():
        return pltpu.make_async_copy(m_list, m_ref, m_sem)

    def beam_copy(distance, half):
        span = pl.ds(pl.multiple_of(owner_of(distance, ways) * piece_rows, tile), piece_rows)
        return pltpu.make_async_copy(beam.at[:, half, span], beam_in.at[half, :, span], beam_sem.at[distance, half])

    def sky_copy(slot, step):
        span = pl.ds(pl.multiple_of(step * tile, tile), tile)
        return pltpu.make_async_copy(sky.at[slot, span], sky_in.at[slot, span], sky_sem.at[slot, step])

    def wigner_copy(slot, step):
        start = pl.multiple_of(owner_of(0, ways) * piece_rows + step * tile, tile)
        span = pl.ds(start, tile)
        return pltpu.make_async_copy(wigner.at[slot, :, :, span], wigner_in.at[slot, :, :, span], wigner_sem.at[slot, step])

    def distant_copy(distance, slot):
        span = pl.ds(pl.multiple_of(owner_of(distance, ways) * piece_rows, tile), piece_rows)
        return pltpu.make_async_copy(wigner.at[slot, :, :, span], wigner_in.at[slot, :, :, span], distant_sem.at[distance - 1, slot])

    def begin(distance, slot):
        return first_tile(m_ref[slot], owner_of(distance, ways), piece_rows, tile)

    def fill(target, distance, slot, step):
        index = owner_of(distance, ways) * tiles + step
        rows_of = pl.ds(pl.multiple_of(index * tile, tile), tile)
        index = jnp.where(index == m_ref[slot] // tile, all_tiles + slot, index)
        span = pl.ds(pl.multiple_of(index * tile, tile), tile)
        for k in range(k_local):
            values = wigner_in[slot, k, :, rows_of]
            for half in range(2):
                factor = jnp.broadcast_to(beam_in[half, k : k + 1, span], (cycles, tile)).astype(jnp.bfloat16)
                target[half * rows + k * cycles : half * rows + (k + 1) * cycles, :] = values * factor

    def cut(slot):
        index = m_ref[slot] // tile
        degrees = index * tile + lax.broadcasted_iota(jnp.int32, (k_local, tile), 1)
        k_values = first_k + lax.broadcasted_iota(jnp.int32, (k_local, tile), 0)
        inside = degrees >= jnp.maximum(m_ref[slot], jnp.abs(k_values))
        span = pl.ds(pl.multiple_of(index * tile, tile), tile)
        for half in range(2):
            beam_in[half, :, (all_tiles + slot) * tile : (all_tiles + slot + 1) * tile] = jnp.where(inside, beam_in[half, :, span], 0.0)

    def cut_in(distance, slot):
        return m_ref[slot] // piece_rows == owner_of(distance, ways)

    def upper(distance):
        return 2 * (owner_of(distance, ways) + 1) > ways

    def where_needed(distance, slot, do):
        if slot % 2 == 0:
            do()
        else:
            pl.when(upper(distance))(do)

    m_copy().start()
    for slot in range(slots):

        def fetch(slot=slot):
            for step in reversed(range(tiles)):
                wigner_copy(slot, step).start()
                if slot == 0 and step == last:
                    for half in range(2):
                        beam_copy(0, half).start()
                sky_copy(slot, step).start()

        where_needed(0, slot, fetch)
    for distance in range(1, ways):
        for half in range(2):
            beam_copy(distance, half).start()
        for slot in range(slots):
            where_needed(distance, slot, lambda distance=distance, slot=slot: distant_copy(distance, slot).start())
    m_copy().wait()
    for slot in range(slots):
        info[slot : slot + 1, :] = jnp.full((1, LANES), m_ref[slot].astype(jnp.float32))
    def beam_arrives(distance):
        for half in range(2):
            beam_copy(distance, half).wait()
        for slot in range(slots):
            pl.when(cut_in(distance, slot))(functools.partial(cut, slot))

    beam_arrives(0)

    @pl.loop(0, slots)
    def _(slot):
        begins = begin(0, slot)

        @pl.loop(begins, tiles)
        def _(later):
            step = tiles - 1 - later + begins
            wigner_copy(slot, step).wait()
            span = pl.ds(pl.multiple_of(step * tile, tile), tile)
            fill(own.at[:, span], 0, slot, step)
            sky_copy(slot, step).wait()

        for skipped in range(tiles):

            @pl.when(begins == skipped)
            def _():
                span = slice(skipped * tile, piece_rows)
                part[slot] = jnp.dot(own[:, span], sky_in[slot, span], preferred_element_type=jnp.float32)

        @pl.when(begins == tiles)
        def _():
            part[slot] = jnp.zeros(part.shape[1:], part.dtype)

    for distance in range(1, ways):
        beam_arrives(distance)
        for slot in range(slots):
            where_needed(distance, slot, lambda distance=distance, slot=slot: distant_copy(distance, slot).wait())

        @pl.loop(0, slots)
        def _(slot):
            @pl.loop(begin(distance, slot), tiles)
            def _(step):
                span = pl.ds(pl.multiple_of(step * tile, tile), tile)
                fill(factors.at[distance - 1, slot, :, span], distance, slot, step)

    for slot in range(slots):

        def drop(slot=slot):
            @pl.loop(0, begin(0, slot))
            def _(step):
                wigner_copy(slot, step).wait()
                sky_copy(slot, step).wait()

        where_needed(0, slot, drop)


def crossed(core, outer):
    return (1 - core % 2) * (outer == INNER)


def distance_of(first, second, outer):
    straight = second * INNER + first
    return jnp.where(crossed(lax.axis_index("beamk"), outer) == 1, first * INNER + second, straight)


def second_kernel(ways, outer, tile, info, _, factors, *refs):
    pieces, refs = refs[: ways - 1], refs[ways - 1 :]
    outs, (acc, turned) = refs[:INNER], refs[INNER:]
    slots, rows, columns = acc.shape
    rows = rows // 2
    piece_rows = pieces[0].shape[1]
    tiles = piece_rows // tile
    width = outs[0].shape[1]
    cycles = outer * INNER
    k_local = width // slots
    pitch = turned.shape[1] // cycles

    @pl.loop(0, slots)
    def _(slot):
        m_value = jnp.max(info[pl.ds(slot, 1), :]).astype(jnp.int32)
        for distance in range(1, ways):
            missing = first_tile(m_value, owner_of(distance, ways), piece_rows, tile)
            for skipped in range(tiles):

                @pl.when(missing == skipped)
                def _():
                    span = slice(skipped * tile, piece_rows)
                    acc[slot] += jnp.dot(
                        factors[distance - 1, slot, :, span],
                        pieces[distance - 1][slot, span],
                        preferred_element_type=jnp.float32,
                    )

        for k in range(k_local):
            span = slice(k * cycles, (k + 1) * cycles)
            total = acc[slot, span] + turn_by_i(acc[slot, rows + k * cycles : rows + (k + 1) * cycles])
            for lane in range(columns // LANES):
                turned[lane, pl.ds(slot * k_local + k, cycles, stride=pitch), :] = total[:, lane * LANES : (lane + 1) * LANES]

    me = lax.axis_index("blk")
    for first in range(INNER):
        for second in range(outer):
            start = (me ^ distance_of(first, second, outer)) * pitch
            for lane in range(columns // LANES):
                block = turned[lane, pl.ds(start, width), :].astype(jnp.bfloat16)
                outs[first][second, :, lane * LANES : (lane + 1) * LANES] = block


def far_first(arrays):
    return [arrays[0], *reversed(arrays[1:])]


def regroup_kernel(outer, *refs):
    arrived, onward = far_first(refs[:INNER]), refs[INNER:]
    for second in range(outer):
        for first in range(INNER):
            onward[second][first] = arrived[first][second]


def place_kernel(outer, *refs):
    arrived, (out, turned, staged, sem) = far_first(refs[:outer]), refs[outer:]
    k_local, slot_count, columns = staged.shape
    width = arrived[0].shape[1]
    slots = width // k_local
    pitch = turned.shape[1] // k_local
    me = lax.axis_index("blk")
    for lane in range(columns // LANES):
        span = slice(lane * LANES, (lane + 1) * LANES)
        for second in range(outer):
            for first in range(INNER):
                block = arrived[second][first, :, span].astype(jnp.float32)
                source = me ^ distance_of(first, second, outer)
                for slot in range(slots):
                    turned[lane, pl.ds(slots * source + slot, k_local, stride=pitch), :] = block[slot * k_local : (slot + 1) * k_local]
    copies = []
    step = -(-k_local // 4)
    for number, start in enumerate(range(0, k_local, step)):
        end = min(start + step, k_local)
        for k in range(start, end):
            for lane in range(columns // LANES):
                values = turned[lane, k * pitch : k * pitch + slot_count]
                staged[k, :, lane * LANES : (lane + 1) * LANES] = values.astype(staged.dtype)
        copies.append(pltpu.make_async_copy(staged.at[start:end], out.at[start:end], sem.at[number]))
        copies[-1].start()
    for copy in copies:
        copy.wait()


def local(sky, beam, wigner, m_list, *, ways, peers):
    slots, piece_rows, columns = sky.shape
    _, k_local, cycles, degrees = wigner.shape
    rows = k_local * cycles
    tile = tile_of(piece_rows)
    tiles = piece_rows // tile
    lane_tiles = columns // LANES
    width = slots * k_local
    params = pltpu.CompilerParams(vmem_limit_bytes=VMEM_LIMIT)

    pieces = []
    for shift in range(1, ways):
        perm = [(c, (c + shift) % ways) for c in range(ways)]
        pieces.append(pltpu.with_memory_space_constraint(lax.ppermute(sky, "beamk", perm), pltpu.VMEM))
    sky, beam, wigner, m_list = (pltpu.with_memory_space_constraint(x, pltpu.HBM) for x in (sky, beam, wigner, m_list))

    part, factors, info = pl.pallas_call(
        functools.partial(first_kernel, ways, tile),
        out_shape=(
            pltpu.VMEM((slots, 2 * rows, columns), jnp.float32),
            pltpu.VMEM((ways - 1, slots, 2 * rows, piece_rows), jnp.bfloat16),
            pltpu.VMEM((8, LANES), jnp.float32),
        ),
        in_specs=[whole(pltpu.HBM)] * 4,
        out_specs=(whole(pltpu.VMEM),) * 3,
        scratch_shapes=[
            pltpu.SMEM(m_list.shape, jnp.int32),
            pltpu.VMEM((slots, piece_rows, columns), jnp.bfloat16),
            pltpu.VMEM(wigner.shape, jnp.bfloat16),
            pltpu.VMEM((2, k_local, degrees + slots * tile), jnp.float32),
            pltpu.VMEM((2 * rows, piece_rows), jnp.bfloat16),
            pltpu.SemaphoreType.DMA,
            pltpu.SemaphoreType.DMA((slots, tiles)),
            pltpu.SemaphoreType.DMA((slots, tiles)),
            pltpu.SemaphoreType.DMA((ways - 1, slots)),
            pltpu.SemaphoreType.DMA((ways, 2)),
        ],
        compiler_params=params,
        cost_estimate=pl.CostEstimate(
            flops=4 * slots * rows * piece_rows * columns, bytes_accessed=8 * 1024 * 1024, transcendentals=0
        ),
        name="own_half",
    )(m_list, sky, wigner, beam)

    outer = peers // INNER

    def blocks(number):
        return pltpu.VMEM((number, width, columns), jnp.bfloat16)

    *sends, _ = pl.pallas_call(
        functools.partial(second_kernel, ways, outer, tile),
        out_shape=[blocks(outer)] * INNER + [pltpu.VMEM(part.shape, part.dtype)],
        in_specs=[whole(pltpu.VMEM)] * (ways + 2),
        out_specs=[whole(pltpu.VMEM)] * (INNER + 1),
        input_output_aliases={1: INNER},
        scratch_shapes=[
            pltpu.VMEM((lane_tiles, cycles * (width + 1 - width % 2), LANES), jnp.float32),
        ],
        compiler_params=params,
        cost_estimate=pl.CostEstimate(
            flops=4 * slots * rows * piece_rows * columns, bytes_accessed=8 * 1024 * 1024, transcendentals=0
        ),
        name="other_half",
    )(info, part, factors, *pieces)

    def send(array, number, step):
        perm = []
        for b in range(peers):
            for core in range(ways):
                over_outer = (step == 0) == bool(crossed(core, outer))
                perm.append((b * ways + core, (b ^ (number * INNER if over_outer else number)) * ways + core))
        return pltpu.with_memory_space_constraint(lax.ppermute(array, ("blk", "beamk"), perm), pltpu.VMEM)

    first = list(sends)
    for number in range(1, INNER):
        first[number] = send(first[number], number, 0)
    second = list(
        pl.pallas_call(
            functools.partial(regroup_kernel, outer),
            out_shape=[blocks(INNER)] * outer,
            in_specs=[whole(pltpu.VMEM)] * INNER,
            out_specs=[whole(pltpu.VMEM)] * outer,
            compiler_params=params,
            name="regroup",
        )(*far_first(first))
    )
    for number in range(1, outer):
        second[number] = send(second[number], number, 1)
    slot_count = slots * peers
    out = pl.pallas_call(
        functools.partial(place_kernel, outer),
        out_shape=pltpu.HBM((k_local, slot_count, columns), jnp.bfloat16),
        in_specs=[whole(pltpu.VMEM)] * outer,
        out_specs=whole(pltpu.HBM),
        scratch_shapes=[
            pltpu.VMEM((lane_tiles, k_local * (slot_count + 1), LANES), jnp.float32),
            pltpu.VMEM((k_local, slot_count, columns), jnp.bfloat16),
            pltpu.SemaphoreType.DMA((4,)),
        ],
        compiler_params=params,
        name="place",
    )(*far_first(second))
    return out.transpose(1, 0, 2)[None]


def solution(mesh):
    in_specs = (
        P("blk", "beamk", None),
        P("beamk", None, None),
        P("blk", "beamk", None, None),
        P("blk"),
    )
    out_specs = P("blk", None, "beamk", None)
    body = functools.partial(local, ways=mesh.shape["beamk"], peers=mesh.shape["blk"])
    return jax.shard_map(body, mesh=mesh, in_specs=in_specs, out_specs=out_specs, check_vma=False)
```

```python
import functools

import jax
import jax.numpy as jnp
from jax import lax
from jax.experimental import pallas as pl
from jax.experimental.pallas import tpu as pltpu
from jax.sharding import PartitionSpec as P

KB = 40
SLOTS = 2
LANES = 128
INNER = 4
VMEM_LIMIT = 24 * 1024 * 1024


def tile_of(rows):
    return max(t for t in range(LANES, min(rows, 512) + 1, LANES) if rows % t == 0)


def whole(memory):
    return pl.BlockSpec(memory_space=memory)


def turn_by_i(rows):
    half = rows.shape[1] // 2
    swapped = pltpu.roll(rows, half, 1)
    column = lax.broadcasted_iota(jnp.int32, swapped.shape, 1)
    return jnp.where(column < half, -swapped, swapped)


def owner_of(distance, ways):
    return lax.rem(lax.axis_index("beamk") - distance + ways, ways)


def first_tile(m_value, owner, piece_rows, tile):
    return jnp.minimum(jnp.maximum(m_value - owner * piece_rows, 0) // tile, piece_rows // tile)


def first_kernel(
    ways, tile, m_list, sky, wigner, beam, part, factors, info, m_ref, sky_in, wigner_in, beam_in, own, m_sem, sky_sem, wigner_sem, distant_sem, beam_sem
):
    slots, piece_rows, columns = sky.shape
    k_local, cycles = wigner.shape[1], wigner.shape[2]
    rows = k_local * cycles
    tiles = piece_rows // tile
    all_tiles = ways * tiles
    first_k = lax.axis_index("beamk") * k_local - KB // 2
    last = tiles - 1

    def m_copy():
        return pltpu.make_async_copy(m_list, m_ref, m_sem)

    def beam_copy(distance, half):
        span = pl.ds(pl.multiple_of(owner_of(distance, ways) * piece_rows, tile), piece_rows)
        return pltpu.make_async_copy(beam.at[:, half, span], beam_in.at[half, :, span], beam_sem.at[distance, half])

    def sky_copy(slot, step):
        span = pl.ds(pl.multiple_of(step * tile, tile), tile)
        return pltpu.make_async_copy(sky.at[slot, span], sky_in.at[slot, span], sky_sem.at[slot, step])

    def wigner_copy(slot, step):
        start = pl.multiple_of(owner_of(0, ways) * piece_rows + step * tile, tile)
        span = pl.ds(start, tile)
        return pltpu.make_async_copy(wigner.at[slot, :, :, span], wigner_in.at[slot, :, :, span], wigner_sem.at[slot, step])

    def distant_copy(distance, slot):
        span = pl.ds(pl.multiple_of(owner_of(distance, ways) * piece_rows, tile), piece_rows)
        return pltpu.make_async_copy(wigner.at[slot, :, :, span], wigner_in.at[slot, :, :, span], distant_sem.at[distance - 1, slot])

    def begin(distance, slot):
        return first_tile(m_ref[slot], owner_of(distance, ways), piece_rows, tile)

    def fill(target, distance, slot, step):
        index = owner_of(distance, ways) * tiles + step
        rows_of = pl.ds(pl.multiple_of(index * tile, tile), tile)
        index = jnp.where(index == m_ref[slot] // tile, all_tiles + slot, index)
        span = pl.ds(pl.multiple_of(index * tile, tile), tile)
        for k in range(k_local):
            values = wigner_in[slot, k, :, rows_of]
            for half in range(2):
                factor = jnp.broadcast_to(beam_in[half, k : k + 1, span], (cycles, tile)).astype(jnp.bfloat16)
                target[half * rows + k * cycles : half * rows + (k + 1) * cycles, :] = values * factor

    def cut(slot):
        index = m_ref[slot] // tile
        degrees = index * tile + lax.broadcasted_iota(jnp.int32, (k_local, tile), 1)
        k_values = first_k + lax.broadcasted_iota(jnp.int32, (k_local, tile), 0)
        inside = degrees >= jnp.maximum(m_ref[slot], jnp.abs(k_values))
        span = pl.ds(pl.multiple_of(index * tile, tile), tile)
        for half in range(2):
            beam_in[half, :, (all_tiles + slot) * tile : (all_tiles + slot + 1) * tile] = jnp.where(inside, beam_in[half, :, span], 0.0)

    def cut_in(distance, slot):
        return m_ref[slot] // piece_rows == owner_of(distance, ways)

    def upper(distance):
        return 2 * (owner_of(distance, ways) + 1) > ways

    def where_needed(distance, slot, do):
        if slot % 2 == 0:
            do()
        else:
            pl.when(upper(distance))(do)

    m_copy().start()
    for slot in range(slots):

        def fetch(slot=slot):
            for step in reversed(range(tiles)):
                wigner_copy(slot, step).start()
                if slot == 0 and step == last:
                    for half in range(2):
                        beam_copy(0, half).start()
                sky_copy(slot, step).start()

        where_needed(0, slot, fetch)
    for distance in range(1, ways):
        for half in range(2):
            beam_copy(distance, half).start()
        for slot in range(slots):
            where_needed(distance, slot, lambda distance=distance, slot=slot: distant_copy(distance, slot).start())
    m_copy().wait()
    for slot in range(slots):
        info[slot : slot + 1, :] = jnp.full((1, LANES), m_ref[slot].astype(jnp.float32))
    def beam_arrives(distance):
        for half in range(2):
            beam_copy(distance, half).wait()
        for slot in range(slots):
            pl.when(cut_in(distance, slot))(functools.partial(cut, slot))

    beam_arrives(0)

    @pl.loop(0, slots)
    def _(slot):
        begins = begin(0, slot)

        @pl.loop(begins, tiles)
        def _(later):
            step = tiles - 1 - later + begins
            wigner_copy(slot, step).wait()
            span = pl.ds(pl.multiple_of(step * tile, tile), tile)
            fill(own.at[:, span], 0, slot, step)
            sky_copy(slot, step).wait()

        for skipped in range(tiles):

            @pl.when(begins == skipped)
            def _():
                span = slice(skipped * tile, piece_rows)
                part[slot] = jnp.dot(own[:, span], sky_in[slot, span], preferred_element_type=jnp.float32)

        @pl.when(begins == tiles)
        def _():
            part[slot] = jnp.zeros(part.shape[1:], part.dtype)

    for distance in range(1, ways):
        beam_arrives(distance)
        for slot in range(slots):
            where_needed(distance, slot, lambda distance=distance, slot=slot: distant_copy(distance, slot).wait())

        @pl.loop(0, slots)
        def _(slot):
            @pl.loop(begin(distance, slot), tiles)
            def _(step):
                span = pl.ds(pl.multiple_of(step * tile, tile), tile)
                fill(factors.at[distance - 1, slot, :, span], distance, slot, step)

    for slot in range(slots):

        def drop(slot=slot):
            @pl.loop(0, begin(0, slot))
            def _(step):
                wigner_copy(slot, step).wait()
                sky_copy(slot, step).wait()

        where_needed(0, slot, drop)


def crossed(core, outer):
    return (core % 2) * (outer == INNER)


def outer_distance(number, outer):
    half = outer // 2
    return [0, *range(half, outer), *range(1, half)][number]


def inner_distance(number):
    return [0, *reversed(range(1, INNER))][number]


def distance_of(first, second, outer):
    straight = outer_distance(second, outer) * INNER + inner_distance(first)
    if outer != INNER:
        return straight
    other = outer_distance(first, outer) * INNER + inner_distance(second)
    return jnp.where(crossed(lax.axis_index("beamk"), outer) == 1, other, straight)


def second_kernel(ways, outer, tile, info, _, factors, *refs):
    pieces, refs = refs[: ways - 1], refs[ways - 1 :]
    outs, (acc, turned) = refs[:INNER], refs[INNER:]
    slots, rows, columns = acc.shape
    rows = rows // 2
    piece_rows = pieces[0].shape[1]
    tiles = piece_rows // tile
    width = outs[0].shape[1]
    cycles = outer * INNER
    k_local = width // slots
    pitch = turned.shape[1] // cycles

    @pl.loop(0, slots)
    def _(slot):
        m_value = jnp.max(info[pl.ds(slot, 1), :]).astype(jnp.int32)
        for distance in range(1, ways):
            missing = first_tile(m_value, owner_of(distance, ways), piece_rows, tile)
            for skipped in range(tiles):

                @pl.when(missing == skipped)
                def _():
                    span = slice(skipped * tile, piece_rows)
                    acc[slot] += jnp.dot(
                        factors[distance - 1, slot, :, span],
                        pieces[distance - 1][slot, span],
                        preferred_element_type=jnp.float32,
                    )

        for k in range(k_local):
            span = slice(k * cycles, (k + 1) * cycles)
            total = acc[slot, span] + turn_by_i(acc[slot, rows + k * cycles : rows + (k + 1) * cycles])
            for lane in range(columns // LANES):
                turned[lane, pl.ds(slot * k_local + k, cycles, stride=pitch), :] = total[:, lane * LANES : (lane + 1) * LANES]

    me = lax.axis_index("blk")
    for first in range(INNER):
        for second in range(outer):
            start = (me ^ distance_of(first, second, outer)) * pitch
            for lane in range(columns // LANES):
                block = turned[lane, pl.ds(start, width), :].astype(jnp.bfloat16)
                outs[first][second, :, lane * LANES : (lane + 1) * LANES] = block


def regroup_kernel(outer, *refs):
    arrived, onward = refs[:INNER], refs[INNER:]
    for second in range(outer):
        for first in range(INNER):
            onward[second][first] = arrived[first][second]


def place_kernel(outer, numbers, *refs):
    arrived, refs = refs[: len(numbers)], refs[len(numbers) :]
    width = arrived[0].shape[1]
    final = numbers[-1] == outer - 1
    if final:
        _, out, turned, staged, sem = refs
        k_local, slot_count, columns = staged.shape
    else:
        (turned,) = refs
        slot_count = SLOTS * outer * INNER
        k_local, columns = width // SLOTS, turned.shape[0] * LANES
    pitch = turned.shape[1] // k_local
    me = lax.axis_index("blk")
    for lane in range(columns // LANES):
        span = slice(lane * LANES, (lane + 1) * LANES)
        for array, second in zip(arrived, numbers):
            for first in range(INNER):
                block = array[first, :, span].astype(jnp.float32)
                source = me ^ distance_of(first, second, outer)
                for slot in range(SLOTS):
                    turned[lane, pl.ds(SLOTS * source + slot, k_local, stride=pitch), :] = block[slot * k_local : (slot + 1) * k_local]
    if not final:
        return
    copies = []
    step = -(-k_local // 4)
    for number, start in enumerate(range(0, k_local, step)):
        end = min(start + step, k_local)
        for k in range(start, end):
            for lane in range(columns // LANES):
                values = turned[lane, k * pitch : k * pitch + slot_count]
                staged[k, :, lane * LANES : (lane + 1) * LANES] = values.astype(staged.dtype)
        copies.append(pltpu.make_async_copy(staged.at[start:end], out.at[start:end], sem.at[number]))
        copies[-1].start()
    for copy in copies:
        copy.wait()


def local(sky, beam, wigner, m_list, *, ways, peers):
    slots, piece_rows, columns = sky.shape
    _, k_local, cycles, degrees = wigner.shape
    rows = k_local * cycles
    tile = tile_of(piece_rows)
    tiles = piece_rows // tile
    lane_tiles = columns // LANES
    width = slots * k_local
    params = pltpu.CompilerParams(vmem_limit_bytes=VMEM_LIMIT)

    pieces = []
    for shift in range(1, ways):
        perm = [(c, (c + shift) % ways) for c in range(ways)]
        pieces.append(pltpu.with_memory_space_constraint(lax.ppermute(sky, "beamk", perm), pltpu.VMEM))
    sky, beam, wigner, m_list = (pltpu.with_memory_space_constraint(x, pltpu.HBM) for x in (sky, beam, wigner, m_list))

    part, factors, info = pl.pallas_call(
        functools.partial(first_kernel, ways, tile),
        out_shape=(
            pltpu.VMEM((slots, 2 * rows, columns), jnp.float32),
            pltpu.VMEM((ways - 1, slots, 2 * rows, piece_rows), jnp.bfloat16),
            pltpu.VMEM((8, LANES), jnp.float32),
        ),
        in_specs=[whole(pltpu.HBM)] * 4,
        out_specs=(whole(pltpu.VMEM),) * 3,
        scratch_shapes=[
            pltpu.SMEM(m_list.shape, jnp.int32),
            pltpu.VMEM((slots, piece_rows, columns), jnp.bfloat16),
            pltpu.VMEM(wigner.shape, jnp.bfloat16),
            pltpu.VMEM((2, k_local, degrees + slots * tile), jnp.float32),
            pltpu.VMEM((2 * rows, piece_rows), jnp.bfloat16),
            pltpu.SemaphoreType.DMA,
            pltpu.SemaphoreType.DMA((slots, tiles)),
            pltpu.SemaphoreType.DMA((slots, tiles)),
            pltpu.SemaphoreType.DMA((ways - 1, slots)),
            pltpu.SemaphoreType.DMA((ways, 2)),
        ],
        compiler_params=params,
        cost_estimate=pl.CostEstimate(
            flops=4 * slots * rows * piece_rows * columns, bytes_accessed=8 * 1024 * 1024, transcendentals=0
        ),
        name="own_half",
    )(m_list, sky, wigner, beam)

    outer = peers // INNER

    def blocks(number):
        return pltpu.VMEM((number, width, columns), jnp.bfloat16)

    *sends, _ = pl.pallas_call(
        functools.partial(second_kernel, ways, outer, tile),
        out_shape=[blocks(outer)] * INNER + [pltpu.VMEM(part.shape, part.dtype)],
        in_specs=[whole(pltpu.VMEM)] * (ways + 2),
        out_specs=[whole(pltpu.VMEM)] * (INNER + 1),
        input_output_aliases={1: INNER},
        scratch_shapes=[
            pltpu.VMEM((lane_tiles, cycles * (width + 1 - width % 2), LANES), jnp.float32),
        ],
        compiler_params=params,
        cost_estimate=pl.CostEstimate(
            flops=4 * slots * rows * piece_rows * columns, bytes_accessed=8 * 1024 * 1024, transcendentals=0
        ),
        name="other_half",
    )(info, part, factors, *pieces)

    def send(array, number, step):
        perm = []
        for b in range(peers):
            for core in range(ways):
                over_outer = (step == 0) == bool(crossed(core, outer))
                distance = outer_distance(number, outer) * INNER if over_outer else inner_distance(number)
                perm.append((b * ways + core, (b ^ distance) * ways + core))
        return pltpu.with_memory_space_constraint(lax.ppermute(array, ("blk", "beamk"), perm), pltpu.VMEM)

    first = list(sends)
    for number in range(1, INNER):
        first[number] = send(first[number], number, 0)
    second = list(
        pl.pallas_call(
            functools.partial(regroup_kernel, outer),
            out_shape=[blocks(INNER)] * outer,
            in_specs=[whole(pltpu.VMEM)] * INNER,
            out_specs=[whole(pltpu.VMEM)] * outer,
            compiler_params=params,
            name="regroup",
        )(*first)
    )
    for number in range(1, outer):
        second[number] = send(second[number], number, 1)
    slot_count = slots * peers
    placed = pltpu.VMEM((lane_tiles, k_local * (slot_count + 1), LANES), jnp.float32)
    result = pltpu.HBM((k_local, slot_count, columns), jnp.bfloat16)
    early = outer // 2
    turned = pl.pallas_call(
        functools.partial(place_kernel, outer, range(early)),
        out_shape=placed,
        in_specs=[whole(pltpu.VMEM)] * early,
        out_specs=whole(pltpu.VMEM),
        compiler_params=params,
        name="place_early",
    )(*second[:early])
    out, _ = pl.pallas_call(
        functools.partial(place_kernel, outer, range(early, outer)),
        out_shape=(result, placed),
        in_specs=[whole(pltpu.VMEM)] * (outer - early + 1),
        out_specs=(whole(pltpu.HBM), whole(pltpu.VMEM)),
        input_output_aliases={outer - early: 1},
        scratch_shapes=[
            pltpu.VMEM((k_local, slot_count, columns), jnp.bfloat16),
            pltpu.SemaphoreType.DMA((4,)),
        ],
        compiler_params=params,
        name="place_late",
    )(*second[early:], turned)
    return out.transpose(1, 0, 2)[None]


def solution(mesh):
    in_specs = (
        P("blk", "beamk", None),
        P("beamk", None, None),
        P("blk", "beamk", None, None),
        P("blk"),
    )
    out_specs = P("blk", None, "beamk", None)
    body = functools.partial(local, ways=mesh.shape["beamk"], peers=mesh.shape["blk"])
    return jax.shard_map(body, mesh=mesh, in_specs=in_specs, out_specs=out_specs, check_vma=False)
```

```python
import functools

import jax
import jax.numpy as jnp
from jax import lax
from jax.experimental import pallas as pl
from jax.experimental.pallas import tpu as pltpu
from jax.sharding import PartitionSpec as P

KB = 40
SLOTS = 2
LANES = 128
INNER = 4
VMEM_LIMIT = 24 * 1024 * 1024


def tile_of(rows):
    return max(t for t in range(LANES, min(rows, 512) + 1, LANES) if rows % t == 0)


def whole(memory):
    return pl.BlockSpec(memory_space=memory)


def turn_by_i(rows):
    half = rows.shape[1] // 2
    swapped = pltpu.roll(rows, half, 1)
    column = lax.broadcasted_iota(jnp.int32, swapped.shape, 1)
    return jnp.where(column < half, -swapped, swapped)


def owner_of(distance, ways):
    return lax.rem(lax.axis_index("beamk") - distance + ways, ways)


def first_tile(m_value, owner, piece_rows, tile):
    return jnp.minimum(jnp.maximum(m_value - owner * piece_rows, 0) // tile, piece_rows // tile)


def first_kernel(
    ways, tile, m_list, sky, wigner, beam, part, factors, info, m_ref, sky_in, wigner_in, beam_in, own, m_sem, sky_sem, wigner_sem, distant_sem, beam_sem
):
    slots, piece_rows, columns = sky.shape
    k_local, cycles = wigner.shape[1], wigner.shape[2]
    rows = k_local * cycles
    tiles = piece_rows // tile
    all_tiles = ways * tiles
    first_k = lax.axis_index("beamk") * k_local - KB // 2
    last = tiles - 1

    def m_copy():
        return pltpu.make_async_copy(m_list, m_ref, m_sem)

    def beam_copy(distance, half):
        span = pl.ds(pl.multiple_of(owner_of(distance, ways) * piece_rows, tile), piece_rows)
        return pltpu.make_async_copy(beam.at[:, half, span], beam_in.at[half, :, span], beam_sem.at[distance, half])

    def sky_copy(slot, step):
        span = pl.ds(pl.multiple_of(step * tile, tile), tile)
        return pltpu.make_async_copy(sky.at[slot, span], sky_in.at[slot, span], sky_sem.at[slot, step])

    def wigner_copy(slot, step):
        start = pl.multiple_of(owner_of(0, ways) * piece_rows + step * tile, tile)
        span = pl.ds(start, tile)
        return pltpu.make_async_copy(wigner.at[slot, :, :, span], wigner_in.at[slot, :, :, span], wigner_sem.at[slot, step])

    def distant_copy(distance, slot):
        span = pl.ds(pl.multiple_of(owner_of(distance, ways) * piece_rows, tile), piece_rows)
        return pltpu.make_async_copy(wigner.at[slot, :, :, span], wigner_in.at[slot, :, :, span], distant_sem.at[distance - 1, slot])

    def begin(distance, slot):
        return first_tile(m_ref[slot], owner_of(distance, ways), piece_rows, tile)

    def fill(target, distance, slot, step):
        index = owner_of(distance, ways) * tiles + step
        rows_of = pl.ds(pl.multiple_of(index * tile, tile), tile)
        index = jnp.where(index == m_ref[slot] // tile, all_tiles + slot, index)
        span = pl.ds(pl.multiple_of(index * tile, tile), tile)
        for k in range(k_local):
            values = wigner_in[slot, k, :, rows_of]
            for half in range(2):
                factor = jnp.broadcast_to(beam_in[half, k : k + 1, span], (cycles, tile)).astype(jnp.bfloat16)
                target[half * rows + k * cycles : half * rows + (k + 1) * cycles, :] = values * factor

    def cut(slot):
        index = m_ref[slot] // tile
        degrees = index * tile + lax.broadcasted_iota(jnp.int32, (k_local, tile), 1)
        k_values = first_k + lax.broadcasted_iota(jnp.int32, (k_local, tile), 0)
        inside = degrees >= jnp.maximum(m_ref[slot], jnp.abs(k_values))
        span = pl.ds(pl.multiple_of(index * tile, tile), tile)
        for half in range(2):
            beam_in[half, :, (all_tiles + slot) * tile : (all_tiles + slot + 1) * tile] = jnp.where(inside, beam_in[half, :, span], 0.0)

    def cut_in(distance, slot):
        return m_ref[slot] // piece_rows == owner_of(distance, ways)

    def upper(distance):
        return 2 * (owner_of(distance, ways) + 1) > ways

    def where_needed(distance, slot, do):
        if slot % 2 == 0:
            do()
        else:
            pl.when(upper(distance))(do)

    m_copy().start()
    for slot in range(slots):

        def fetch(slot=slot):
            for step in reversed(range(tiles)):
                wigner_copy(slot, step).start()
                if slot == 0 and step == last:
                    for half in range(2):
                        beam_copy(0, half).start()
                sky_copy(slot, step).start()

        where_needed(0, slot, fetch)
    for distance in range(1, ways):
        for half in range(2):
            beam_copy(distance, half).start()
        for slot in range(slots):
            where_needed(distance, slot, lambda distance=distance, slot=slot: distant_copy(distance, slot).start())
    m_copy().wait()
    for slot in range(slots):
        info[slot : slot + 1, :] = jnp.full((1, LANES), m_ref[slot].astype(jnp.float32))
    def beam_arrives(distance):
        for half in range(2):
            beam_copy(distance, half).wait()
        for slot in range(slots):
            pl.when(cut_in(distance, slot))(functools.partial(cut, slot))

    beam_arrives(0)

    @pl.loop(0, slots)
    def _(slot):
        begins = begin(0, slot)

        @pl.loop(begins, tiles)
        def _(later):
            step = tiles - 1 - later + begins
            wigner_copy(slot, step).wait()
            span = pl.ds(pl.multiple_of(step * tile, tile), tile)
            fill(own.at[:, span], 0, slot, step)
            sky_copy(slot, step).wait()

        for skipped in range(tiles):

            @pl.when(begins == skipped)
            def _():
                span = slice(skipped * tile, piece_rows)
                part[slot] = jnp.dot(own[:, span], sky_in[slot, span], preferred_element_type=jnp.float32)

        @pl.when(begins == tiles)
        def _():
            part[slot] = jnp.zeros(part.shape[1:], part.dtype)

    for distance in range(1, ways):
        beam_arrives(distance)
        for slot in range(slots):
            where_needed(distance, slot, lambda distance=distance, slot=slot: distant_copy(distance, slot).wait())

        @pl.loop(0, slots)
        def _(slot):
            @pl.loop(begin(distance, slot), tiles)
            def _(step):
                span = pl.ds(pl.multiple_of(step * tile, tile), tile)
                fill(factors.at[distance - 1, slot, :, span], distance, slot, step)

    for slot in range(slots):

        def drop(slot=slot):
            @pl.loop(0, begin(0, slot))
            def _(step):
                wigner_copy(slot, step).wait()
                sky_copy(slot, step).wait()

        where_needed(0, slot, drop)


def crossed(core, outer):
    return (core % 2) * (outer == INNER)


def outer_distance(number, outer):
    half = outer // 2
    return [0, *range(half, outer), *range(1, half)][number]


def inner_distance(number):
    return [0, *reversed(range(1, INNER))][number]


def distance_of(first, second, outer):
    straight = outer_distance(second, outer) * INNER + inner_distance(first)
    if outer != INNER:
        return straight
    other = outer_distance(first, outer) * INNER + inner_distance(second)
    return jnp.where(crossed(lax.axis_index("beamk"), outer) == 1, other, straight)


def second_kernel(ways, outer, tile, info, _, factors, *refs):
    pieces, refs = refs[: ways - 1], refs[ways - 1 :]
    outs, direct, (acc, turned) = refs[: INNER - 1], refs[INNER - 1 : outer + INNER - 1], refs[outer + INNER - 1 :]
    slots, rows, columns = acc.shape
    rows = rows // 2
    piece_rows = pieces[0].shape[1]
    tiles = piece_rows // tile
    width = outs[0].shape[1]
    cycles = outer * INNER
    k_local = width // slots
    pitch = turned.shape[1] // cycles

    @pl.loop(0, slots)
    def _(slot):
        m_value = jnp.max(info[pl.ds(slot, 1), :]).astype(jnp.int32)
        for distance in range(1, ways):
            missing = first_tile(m_value, owner_of(distance, ways), piece_rows, tile)
            for skipped in range(tiles):

                @pl.when(missing == skipped)
                def _():
                    span = slice(skipped * tile, piece_rows)
                    acc[slot] += jnp.dot(
                        factors[distance - 1, slot, :, span],
                        pieces[distance - 1][slot, span],
                        preferred_element_type=jnp.float32,
                    )

        for k in range(k_local):
            span = slice(k * cycles, (k + 1) * cycles)
            total = acc[slot, span] + turn_by_i(acc[slot, rows + k * cycles : rows + (k + 1) * cycles])
            for lane in range(columns // LANES):
                turned[lane, pl.ds(slot * k_local + k, cycles, stride=pitch), :] = total[:, lane * LANES : (lane + 1) * LANES]

    me = lax.axis_index("blk")
    for first in range(INNER):
        for second in range(outer):
            start = (me ^ distance_of(first, second, outer)) * pitch
            for lane in range(columns // LANES):
                block = turned[lane, pl.ds(start, width), :].astype(jnp.bfloat16)
                span = slice(lane * LANES, (lane + 1) * LANES)
                if first:
                    outs[first - 1][second, :, span] = block
                else:
                    direct[second][0, :, span] = block


def regroup_kernel(outer, *refs):
    arrived, direct, refs = refs[: INNER - 1], refs[INNER - 1 : INNER - 1 + outer], refs[INNER - 1 + outer :]
    here, onward = refs[0], refs[1:]
    for second in range(outer):
        here[second] = direct[second][0]
        for first in range(1, INNER):
            onward[second][first - 1] = arrived[first - 1][second]


def place_kernel(outer, numbers, *refs):
    here, arrived, refs = refs[0], refs[1 : len(numbers) + 1], refs[len(numbers) + 1 :]
    width = here.shape[1]
    final = numbers[-1] == outer - 1
    if final:
        _, out, turned, staged, sem = refs
        k_local, slot_count, columns = staged.shape
    else:
        (turned,) = refs
        slot_count = SLOTS * outer * INNER
        k_local, columns = width // SLOTS, turned.shape[0] * LANES
    pitch = turned.shape[1] // k_local
    me = lax.axis_index("blk")
    for lane in range(columns // LANES):
        span = slice(lane * LANES, (lane + 1) * LANES)
        for array, second in zip(arrived, numbers):
            for first in range(INNER):
                block = array[first - 1, :, span] if first else here[second, :, span]
                block = block.astype(jnp.float32)
                source = me ^ distance_of(first, second, outer)
                for slot in range(SLOTS):
                    turned[lane, pl.ds(SLOTS * source + slot, k_local, stride=pitch), :] = block[slot * k_local : (slot + 1) * k_local]
    if not final:
        return
    copies = []
    step = -(-k_local // 4)
    for number, start in enumerate(range(0, k_local, step)):
        end = min(start + step, k_local)
        for k in range(start, end):
            for lane in range(columns // LANES):
                values = turned[lane, k * pitch : k * pitch + slot_count]
                staged[k, :, lane * LANES : (lane + 1) * LANES] = values.astype(staged.dtype)
        copies.append(pltpu.make_async_copy(staged.at[start:end], out.at[start:end], sem.at[number]))
        copies[-1].start()
    for copy in copies:
        copy.wait()


def local(sky, beam, wigner, m_list, *, ways, peers):
    slots, piece_rows, columns = sky.shape
    _, k_local, cycles, degrees = wigner.shape
    rows = k_local * cycles
    tile = tile_of(piece_rows)
    tiles = piece_rows // tile
    lane_tiles = columns // LANES
    width = slots * k_local
    params = pltpu.CompilerParams(vmem_limit_bytes=VMEM_LIMIT)

    pieces = []
    for shift in range(1, ways):
        perm = [(c, (c + shift) % ways) for c in range(ways)]
        pieces.append(pltpu.with_memory_space_constraint(lax.ppermute(sky, "beamk", perm), pltpu.VMEM))
    sky, beam, wigner, m_list = (pltpu.with_memory_space_constraint(x, pltpu.HBM) for x in (sky, beam, wigner, m_list))

    part, factors, info = pl.pallas_call(
        functools.partial(first_kernel, ways, tile),
        out_shape=(
            pltpu.VMEM((slots, 2 * rows, columns), jnp.float32),
            pltpu.VMEM((ways - 1, slots, 2 * rows, piece_rows), jnp.bfloat16),
            pltpu.VMEM((8, LANES), jnp.float32),
        ),
        in_specs=[whole(pltpu.HBM)] * 4,
        out_specs=(whole(pltpu.VMEM),) * 3,
        scratch_shapes=[
            pltpu.SMEM(m_list.shape, jnp.int32),
            pltpu.VMEM((slots, piece_rows, columns), jnp.bfloat16),
            pltpu.VMEM(wigner.shape, jnp.bfloat16),
            pltpu.VMEM((2, k_local, degrees + slots * tile), jnp.float32),
            pltpu.VMEM((2 * rows, piece_rows), jnp.bfloat16),
            pltpu.SemaphoreType.DMA,
            pltpu.SemaphoreType.DMA((slots, tiles)),
            pltpu.SemaphoreType.DMA((slots, tiles)),
            pltpu.SemaphoreType.DMA((ways - 1, slots)),
            pltpu.SemaphoreType.DMA((ways, 2)),
        ],
        compiler_params=params,
        cost_estimate=pl.CostEstimate(
            flops=4 * slots * rows * piece_rows * columns, bytes_accessed=8 * 1024 * 1024, transcendentals=0
        ),
        name="own_half",
    )(m_list, sky, wigner, beam)

    outer = peers // INNER

    def blocks(number):
        return pltpu.VMEM((number, width, columns), jnp.bfloat16)

    *sends, _ = pl.pallas_call(
        functools.partial(second_kernel, ways, outer, tile),
        out_shape=[blocks(outer)] * (INNER - 1) + [blocks(1)] * outer + [pltpu.VMEM(part.shape, part.dtype)],
        in_specs=[whole(pltpu.VMEM)] * (ways + 2),
        out_specs=[whole(pltpu.VMEM)] * (outer + INNER),
        input_output_aliases={1: outer + INNER - 1},
        scratch_shapes=[
            pltpu.VMEM((lane_tiles, cycles * (width + 1 - width % 2), LANES), jnp.float32),
        ],
        compiler_params=params,
        cost_estimate=pl.CostEstimate(
            flops=4 * slots * rows * piece_rows * columns, bytes_accessed=8 * 1024 * 1024, transcendentals=0
        ),
        name="other_half",
    )(info, part, factors, *pieces)

    def send(array, number, step):
        perm = []
        for b in range(peers):
            for core in range(ways):
                over_outer = (step == 0) == bool(crossed(core, outer))
                distance = outer_distance(number, outer) * INNER if over_outer else inner_distance(number)
                perm.append((b * ways + core, (b ^ distance) * ways + core))
        return pltpu.with_memory_space_constraint(lax.ppermute(array, ("blk", "beamk"), perm), pltpu.VMEM)

    first, direct = list(sends[: INNER - 1]), list(sends[INNER - 1 :])
    for number in range(1, INNER):
        first[number - 1] = send(first[number - 1], number, 0)
    for number in range(1, outer):
        direct[number] = send(direct[number], number, 1)
    here, *second = pl.pallas_call(
        functools.partial(regroup_kernel, outer),
        out_shape=[blocks(outer)] + [blocks(INNER - 1)] * outer,
        in_specs=[whole(pltpu.VMEM)] * (INNER - 1 + outer),
        out_specs=[whole(pltpu.VMEM)] * (outer + 1),
        compiler_params=params,
        name="regroup",
    )(*first, *direct)
    for number in range(1, outer):
        second[number] = send(second[number], number, 1)
    slot_count = slots * peers
    placed = pltpu.VMEM((lane_tiles, k_local * (slot_count + 1), LANES), jnp.float32)
    result = pltpu.HBM((k_local, slot_count, columns), jnp.bfloat16)
    early = outer // 2
    turned = pl.pallas_call(
        functools.partial(place_kernel, outer, range(early)),
        out_shape=placed,
        in_specs=[whole(pltpu.VMEM)] * (early + 1),
        out_specs=whole(pltpu.VMEM),
        compiler_params=params,
        name="place_early",
    )(here, *second[:early])
    out, _ = pl.pallas_call(
        functools.partial(place_kernel, outer, range(early, outer)),
        out_shape=(result, placed),
        in_specs=[whole(pltpu.VMEM)] * (outer - early + 2),
        out_specs=(whole(pltpu.HBM), whole(pltpu.VMEM)),
        input_output_aliases={outer - early + 1: 1},
        scratch_shapes=[
            pltpu.VMEM((k_local, slot_count, columns), jnp.bfloat16),
            pltpu.SemaphoreType.DMA((4,)),
        ],
        compiler_params=params,
        name="place_late",
    )(here, *second[early:], turned)
    return out.transpose(1, 0, 2)[None]


def solution(mesh):
    in_specs = (
        P("blk", "beamk", None),
        P("beamk", None, None),
        P("blk", "beamk", None, None),
        P("blk"),
    )
    out_specs = P("blk", None, "beamk", None)
    body = functools.partial(local, ways=mesh.shape["beamk"], peers=mesh.shape["blk"])
    return jax.shard_map(body, mesh=mesh, in_specs=in_specs, out_specs=out_specs, check_vma=False)
```

```python
import functools

import jax
import jax.numpy as jnp
from jax import lax
from jax.experimental import pallas as pl
from jax.experimental.pallas import tpu as pltpu
from jax.sharding import PartitionSpec as P

KB = 40
SLOTS = 2
LANES = 128
INNER = 4
VMEM_LIMIT = 24 * 1024 * 1024


def tile_of(rows):
    return max(t for t in range(LANES, min(rows, 512) + 1, LANES) if rows % t == 0)


def whole(memory):
    return pl.BlockSpec(memory_space=memory)


def turn_by_i(rows):
    half = rows.shape[1] // 2
    swapped = pltpu.roll(rows, half, 1)
    column = lax.broadcasted_iota(jnp.int32, swapped.shape, 1)
    return jnp.where(column < half, -swapped, swapped)


def owner_of(distance, ways):
    return lax.rem(lax.axis_index("beamk") - distance + ways, ways)


def first_tile(m_value, owner, piece_rows, tile):
    return jnp.minimum(jnp.maximum(m_value - owner * piece_rows, 0) // tile, piece_rows // tile)


def first_kernel(
    ways, tile, m_list, sky, wigner, beam, part, factors, info, m_ref, sky_in, wigner_in, beam_in, own, m_sem, sky_sem, wigner_sem, distant_sem, beam_sem
):
    slots, piece_rows, columns = sky.shape
    k_local, cycles = wigner.shape[1], wigner.shape[2]
    rows = k_local * cycles
    tiles = piece_rows // tile
    all_tiles = ways * tiles
    first_k = lax.axis_index("beamk") * k_local - KB // 2
    last = tiles - 1

    def m_copy():
        return pltpu.make_async_copy(m_list, m_ref, m_sem)

    def beam_copy(distance, half):
        span = pl.ds(pl.multiple_of(owner_of(distance, ways) * piece_rows, tile), piece_rows)
        return pltpu.make_async_copy(beam.at[:, half, span], beam_in.at[half, :, span], beam_sem.at[distance, half])

    def sky_copy(slot, step):
        span = pl.ds(pl.multiple_of(step * tile, tile), tile)
        return pltpu.make_async_copy(sky.at[slot, span], sky_in.at[slot, span], sky_sem.at[slot, step])

    def wigner_copy(slot, step):
        start = pl.multiple_of(owner_of(0, ways) * piece_rows + step * tile, tile)
        span = pl.ds(start, tile)
        return pltpu.make_async_copy(wigner.at[slot, :, :, span], wigner_in.at[slot, :, :, span], wigner_sem.at[slot, step])

    def distant_copy(distance, slot):
        span = pl.ds(pl.multiple_of(owner_of(distance, ways) * piece_rows, tile), piece_rows)
        return pltpu.make_async_copy(wigner.at[slot, :, :, span], wigner_in.at[slot, :, :, span], distant_sem.at[distance - 1, slot])

    def begin(distance, slot):
        return first_tile(m_ref[slot], owner_of(distance, ways), piece_rows, tile)

    def fill(target, distance, slot, step):
        index = owner_of(distance, ways) * tiles + step
        rows_of = pl.ds(pl.multiple_of(index * tile, tile), tile)
        index = jnp.where(index == m_ref[slot] // tile, all_tiles + slot, index)
        span = pl.ds(pl.multiple_of(index * tile, tile), tile)
        for k in range(k_local):
            values = wigner_in[slot, k, :, rows_of]
            for half in range(2):
                factor = jnp.broadcast_to(beam_in[half, k : k + 1, span], (cycles, tile)).astype(jnp.bfloat16)
                target[half * rows + k * cycles : half * rows + (k + 1) * cycles, :] = values * factor

    def cut(slot):
        index = m_ref[slot] // tile
        degrees = index * tile + lax.broadcasted_iota(jnp.int32, (k_local, tile), 1)
        k_values = first_k + lax.broadcasted_iota(jnp.int32, (k_local, tile), 0)
        inside = degrees >= jnp.maximum(m_ref[slot], jnp.abs(k_values))
        span = pl.ds(pl.multiple_of(index * tile, tile), tile)
        for half in range(2):
            beam_in[half, :, (all_tiles + slot) * tile : (all_tiles + slot + 1) * tile] = jnp.where(inside, beam_in[half, :, span], 0.0)

    def cut_in(distance, slot):
        return m_ref[slot] // piece_rows == owner_of(distance, ways)

    def upper(distance):
        return 2 * (owner_of(distance, ways) + 1) > ways

    def where_needed(distance, slot, do):
        if slot % 2 == 0:
            do()
        else:
            pl.when(upper(distance))(do)

    m_copy().start()
    for slot in range(slots):

        def fetch(slot=slot):
            for step in reversed(range(tiles)):
                wigner_copy(slot, step).start()
                if slot == 0 and step == last:
                    for half in range(2):
                        beam_copy(0, half).start()
                sky_copy(slot, step).start()

        where_needed(0, slot, fetch)
    for distance in range(1, ways):
        for half in range(2):
            beam_copy(distance, half).start()
        for slot in range(slots):
            where_needed(distance, slot, lambda distance=distance, slot=slot: distant_copy(distance, slot).start())
    m_copy().wait()
    for slot in range(slots):
        info[slot : slot + 1, :] = jnp.full((1, LANES), m_ref[slot].astype(jnp.float32))
    def beam_arrives(distance):
        for half in range(2):
            beam_copy(distance, half).wait()
        for slot in range(slots):
            pl.when(cut_in(distance, slot))(functools.partial(cut, slot))

    beam_arrives(0)

    @pl.loop(0, slots)
    def _(slot):
        begins = begin(0, slot)

        @pl.loop(begins, tiles)
        def _(later):
            step = tiles - 1 - later + begins
            wigner_copy(slot, step).wait()
            span = pl.ds(pl.multiple_of(step * tile, tile), tile)
            fill(own.at[:, span], 0, slot, step)
            sky_copy(slot, step).wait()

        for skipped in range(tiles):

            @pl.when(begins == skipped)
            def _():
                span = slice(skipped * tile, piece_rows)
                part[slot] = jnp.dot(own[:, span], sky_in[slot, span], preferred_element_type=jnp.float32)

        @pl.when(begins == tiles)
        def _():
            part[slot] = jnp.zeros(part.shape[1:], part.dtype)

    for distance in range(1, ways):
        beam_arrives(distance)
        for slot in range(slots):
            where_needed(distance, slot, lambda distance=distance, slot=slot: distant_copy(distance, slot).wait())

        @pl.loop(0, slots)
        def _(slot):
            @pl.loop(begin(distance, slot), tiles)
            def _(step):
                span = pl.ds(pl.multiple_of(step * tile, tile), tile)
                fill(factors.at[distance - 1, slot, :, span], distance, slot, step)

    for slot in range(slots):

        def drop(slot=slot):
            @pl.loop(0, begin(0, slot))
            def _(step):
                wigner_copy(slot, step).wait()
                sky_copy(slot, step).wait()

        where_needed(0, slot, drop)


def crossed(core, outer):
    return (core % 2) * (outer == INNER)


def device_of(first, second, outer):
    straight = second * INNER + first
    if outer != INNER:
        return straight
    return jnp.where(crossed(lax.axis_index("beamk"), outer) == 1, first * INNER + second, straight)


def second_kernel(ways, outer, tile, info, _, factors, *refs):
    pieces, refs = refs[: ways - 1], refs[ways - 1 :]
    out, acc, turned = refs
    slots, rows, columns = acc.shape
    rows = rows // 2
    piece_rows = pieces[0].shape[1]
    tiles = piece_rows // tile
    width = out.shape[2]
    cycles = outer * INNER
    k_local = width // slots
    pitch = turned.shape[1] // cycles

    @pl.loop(0, slots)
    def _(slot):
        m_value = jnp.max(info[pl.ds(slot, 1), :]).astype(jnp.int32)
        for distance in range(1, ways):
            missing = first_tile(m_value, owner_of(distance, ways), piece_rows, tile)
            for skipped in range(tiles):

                @pl.when(missing == skipped)
                def _():
                    span = slice(skipped * tile, piece_rows)
                    acc[slot] += jnp.dot(
                        factors[distance - 1, slot, :, span],
                        pieces[distance - 1][slot, span],
                        preferred_element_type=jnp.float32,
                    )

        for k in range(k_local):
            span = slice(k * cycles, (k + 1) * cycles)
            total = acc[slot, span] + turn_by_i(acc[slot, rows + k * cycles : rows + (k + 1) * cycles])
            for lane in range(columns // LANES):
                turned[lane, pl.ds(slot * k_local + k, cycles, stride=pitch), :] = total[:, lane * LANES : (lane + 1) * LANES]

    for first in range(INNER):
        for second in range(outer):
            start = device_of(first, second, outer) * pitch
            for lane in range(columns // LANES):
                block = turned[lane, pl.ds(start, width), :].astype(jnp.bfloat16)
                out[first, second, :, lane * LANES : (lane + 1) * LANES] = block


def regroup_kernel(arrived, onward):
    for first in range(arrived.shape[0]):
        for second in range(arrived.shape[1]):
            onward[second, first] = arrived[first, second]


def place_kernel(arrived, out, turned, staged, sem):
    outer, _, width, columns = arrived.shape
    k_local, slot_count, _ = staged.shape
    pitch = turned.shape[1] // k_local
    for lane in range(columns // LANES):
        span = slice(lane * LANES, (lane + 1) * LANES)
        for second in range(outer):
            for first in range(INNER):
                block = arrived[second, first, :, span].astype(jnp.float32)
                source = device_of(first, second, outer)
                for slot in range(SLOTS):
                    turned[lane, pl.ds(SLOTS * source + slot, k_local, stride=pitch), :] = block[slot * k_local : (slot + 1) * k_local]
    copies = []
    step = -(-k_local // 4)
    for number, start in enumerate(range(0, k_local, step)):
        end = min(start + step, k_local)
        for k in range(start, end):
            for lane in range(columns // LANES):
                values = turned[lane, k * pitch : k * pitch + slot_count]
                staged[k, :, lane * LANES : (lane + 1) * LANES] = values.astype(staged.dtype)
        copies.append(pltpu.make_async_copy(staged.at[start:end], out.at[start:end], sem.at[number]))
        copies[-1].start()
    for copy in copies:
        copy.wait()


def local(sky, beam, wigner, m_list, *, ways, peers):
    slots, piece_rows, columns = sky.shape
    _, k_local, cycles, degrees = wigner.shape
    rows = k_local * cycles
    tile = tile_of(piece_rows)
    tiles = piece_rows // tile
    lane_tiles = columns // LANES
    width = slots * k_local
    params = pltpu.CompilerParams(vmem_limit_bytes=VMEM_LIMIT)

    pieces = []
    for shift in range(1, ways):
        perm = [(c, (c + shift) % ways) for c in range(ways)]
        pieces.append(pltpu.with_memory_space_constraint(lax.ppermute(sky, "beamk", perm), pltpu.VMEM))
    sky, beam, wigner, m_list = (pltpu.with_memory_space_constraint(x, pltpu.HBM) for x in (sky, beam, wigner, m_list))

    part, factors, info = pl.pallas_call(
        functools.partial(first_kernel, ways, tile),
        out_shape=(
            pltpu.VMEM((slots, 2 * rows, columns), jnp.float32),
            pltpu.VMEM((ways - 1, slots, 2 * rows, piece_rows), jnp.bfloat16),
            pltpu.VMEM((8, LANES), jnp.float32),
        ),
        in_specs=[whole(pltpu.HBM)] * 4,
        out_specs=(whole(pltpu.VMEM),) * 3,
        scratch_shapes=[
            pltpu.SMEM(m_list.shape, jnp.int32),
            pltpu.VMEM((slots, piece_rows, columns), jnp.bfloat16),
            pltpu.VMEM(wigner.shape, jnp.bfloat16),
            pltpu.VMEM((2, k_local, degrees + slots * tile), jnp.float32),
            pltpu.VMEM((2 * rows, piece_rows), jnp.bfloat16),
            pltpu.SemaphoreType.DMA,
            pltpu.SemaphoreType.DMA((slots, tiles)),
            pltpu.SemaphoreType.DMA((slots, tiles)),
            pltpu.SemaphoreType.DMA((ways - 1, slots)),
            pltpu.SemaphoreType.DMA((ways, 2)),
        ],
        compiler_params=params,
        cost_estimate=pl.CostEstimate(
            flops=4 * slots * rows * piece_rows * columns, bytes_accessed=8 * 1024 * 1024, transcendentals=0
        ),
        name="own_half",
    )(m_list, sky, wigner, beam)

    outer = peers // INNER

    def blocks(*numbers):
        return pltpu.VMEM((*numbers, width, columns), jnp.bfloat16)

    blocks_out, _ = pl.pallas_call(
        functools.partial(second_kernel, ways, outer, tile),
        out_shape=(blocks(INNER, outer), pltpu.VMEM(part.shape, part.dtype)),
        in_specs=[whole(pltpu.VMEM)] * (ways + 2),
        out_specs=(whole(pltpu.VMEM),) * 2,
        input_output_aliases={1: 1},
        scratch_shapes=[
            pltpu.VMEM((lane_tiles, cycles * (width + 1 - width % 2), LANES), jnp.float32),
        ],
        compiler_params=params,
        cost_estimate=pl.CostEstimate(
            flops=4 * slots * rows * piece_rows * columns, bytes_accessed=8 * 1024 * 1024, transcendentals=0
        ),
        name="other_half",
    )(info, part, factors, *pieces)

    def exchange(array, step):
        groups = []
        for core in range(ways):
            if (step == 0) == bool(crossed(core, outer)):
                places = [[o * INNER + i for o in range(outer)] for i in range(INNER)]
            else:
                places = [[o * INNER + i for i in range(INNER)] for o in range(outer)]
            groups += [[b * ways + core for b in group] for group in places]
        array = lax.all_to_all(array, ("blk", "beamk"), 0, 0, axis_index_groups=groups, tiled=True)
        return pltpu.with_memory_space_constraint(array, pltpu.VMEM)

    first = exchange(blocks_out, 0)
    second = pl.pallas_call(
        regroup_kernel,
        out_shape=blocks(outer, INNER),
        in_specs=[whole(pltpu.VMEM)],
        out_specs=whole(pltpu.VMEM),
        compiler_params=params,
        name="regroup",
    )(first)
    second = exchange(second, 1)
    slot_count = slots * peers
    out = pl.pallas_call(
        place_kernel,
        out_shape=pltpu.HBM((k_local, slot_count, columns), jnp.bfloat16),
        in_specs=[whole(pltpu.VMEM)],
        out_specs=whole(pltpu.HBM),
        scratch_shapes=[
            pltpu.VMEM((lane_tiles, k_local * (slot_count + 1), LANES), jnp.float32),
            pltpu.VMEM((k_local, slot_count, columns), jnp.bfloat16),
            pltpu.SemaphoreType.DMA((4,)),
        ],
        compiler_params=params,
        name="place",
    )(second)
    return out.transpose(1, 0, 2)[None]


def solution(mesh):
    in_specs = (
        P("blk", "beamk", None),
        P("beamk", None, None),
        P("blk", "beamk", None, None),
        P("blk"),
    )
    out_specs = P("blk", None, "beamk", None)
    body = functools.partial(local, ways=mesh.shape["beamk"], peers=mesh.shape["blk"])
    return jax.shard_map(body, mesh=mesh, in_specs=in_specs, out_specs=out_specs, check_vma=False)
```

```python
import functools

import jax
import jax.numpy as jnp
from jax import lax
from jax.experimental import pallas as pl
from jax.experimental.pallas import tpu as pltpu
from jax.sharding import PartitionSpec as P

KB = 40
LANES = 128
INNER = 4
VMEM_LIMIT = 24 * 1024 * 1024


def tile_of(rows):
    return max(t for t in range(LANES, min(rows, 512) + 1, LANES) if rows % t == 0)


def whole(memory):
    return pl.BlockSpec(memory_space=memory)


def turn_by_i(rows):
    half = rows.shape[1] // 2
    swapped = pltpu.roll(rows, half, 1)
    column = lax.broadcasted_iota(jnp.int32, swapped.shape, 1)
    return jnp.where(column < half, -swapped, swapped)


def owner_of(distance, ways):
    return lax.rem(lax.axis_index("beamk") - distance + ways, ways)


def first_tile(m_value, owner, piece_rows, tile):
    return jnp.minimum(jnp.maximum(m_value - owner * piece_rows, 0) // tile, piece_rows // tile)


def first_kernel(
    ways, tile, m_list, sky, wigner, beam, part, factors, info, m_ref, sky_in, wigner_in, beam_in, own, m_sem, sky_sem, wigner_sem, distant_sem, beam_sem
):
    slots, piece_rows, columns = sky.shape
    k_local, cycles = wigner.shape[1], wigner.shape[2]
    rows = k_local * cycles
    tiles = piece_rows // tile
    all_tiles = ways * tiles
    first_k = lax.axis_index("beamk") * k_local - KB // 2
    last = tiles - 1

    def m_copy():
        return pltpu.make_async_copy(m_list, m_ref, m_sem)

    def beam_copy(distance, half):
        span = pl.ds(pl.multiple_of(owner_of(distance, ways) * piece_rows, tile), piece_rows)
        return pltpu.make_async_copy(beam.at[:, half, span], beam_in.at[half, :, span], beam_sem.at[distance, half])

    def sky_copy(slot, step):
        span = pl.ds(pl.multiple_of(step * tile, tile), tile)
        return pltpu.make_async_copy(sky.at[slot, span], sky_in.at[slot, span], sky_sem.at[slot, step])

    def wigner_copy(slot, step):
        start = pl.multiple_of(owner_of(0, ways) * piece_rows + step * tile, tile)
        span = pl.ds(start, tile)
        return pltpu.make_async_copy(wigner.at[slot, :, :, span], wigner_in.at[slot, :, :, span], wigner_sem.at[slot, step])

    def distant_copy(distance, slot):
        span = pl.ds(pl.multiple_of(owner_of(distance, ways) * piece_rows, tile), piece_rows)
        return pltpu.make_async_copy(wigner.at[slot, :, :, span], wigner_in.at[slot, :, :, span], distant_sem.at[distance - 1, slot])

    def begin(distance, slot):
        return first_tile(m_ref[slot], owner_of(distance, ways), piece_rows, tile)

    def fill(target, distance, slot, step):
        index = owner_of(distance, ways) * tiles + step
        rows_of = pl.ds(pl.multiple_of(index * tile, tile), tile)
        index = jnp.where(index == m_ref[slot] // tile, all_tiles + slot, index)
        span = pl.ds(pl.multiple_of(index * tile, tile), tile)
        for k in range(k_local):
            values = wigner_in[slot, k, :, rows_of]
            for half in range(2):
                factor = jnp.broadcast_to(beam_in[half, k : k + 1, span], (cycles, tile)).astype(jnp.bfloat16)
                target[half * rows + k * cycles : half * rows + (k + 1) * cycles, :] = values * factor

    def cut(slot):
        index = m_ref[slot] // tile
        degrees = index * tile + lax.broadcasted_iota(jnp.int32, (k_local, tile), 1)
        k_values = first_k + lax.broadcasted_iota(jnp.int32, (k_local, tile), 0)
        inside = degrees >= jnp.maximum(m_ref[slot], jnp.abs(k_values))
        span = pl.ds(pl.multiple_of(index * tile, tile), tile)
        for half in range(2):
            beam_in[half, :, (all_tiles + slot) * tile : (all_tiles + slot + 1) * tile] = jnp.where(inside, beam_in[half, :, span], 0.0)

    def cut_in(distance, slot):
        return m_ref[slot] // piece_rows == owner_of(distance, ways)

    def upper(distance):
        return 2 * (owner_of(distance, ways) + 1) > ways

    def where_needed(distance, slot, do):
        if slot % 2 == 0:
            do()
        else:
            pl.when(upper(distance))(do)

    m_copy().start()
    for slot in range(slots):

        def fetch(slot=slot):
            for step in reversed(range(tiles)):
                wigner_copy(slot, step).start()
                if slot == 0 and step == last:
                    for half in range(2):
                        beam_copy(0, half).start()
                sky_copy(slot, step).start()

        where_needed(0, slot, fetch)
    for distance in range(1, ways):
        for half in range(2):
            beam_copy(distance, half).start()
        for slot in range(slots):
            where_needed(distance, slot, lambda distance=distance, slot=slot: distant_copy(distance, slot).start())
    m_copy().wait()
    for slot in range(slots):
        info[slot : slot + 1, :] = jnp.full((1, LANES), m_ref[slot].astype(jnp.float32))
    def beam_arrives(distance):
        for half in range(2):
            beam_copy(distance, half).wait()
        for slot in range(slots):
            pl.when(cut_in(distance, slot))(functools.partial(cut, slot))

    beam_arrives(0)

    @pl.loop(0, slots)
    def _(slot):
        begins = begin(0, slot)

        @pl.loop(begins, tiles)
        def _(later):
            step = tiles - 1 - later + begins
            wigner_copy(slot, step).wait()
            span = pl.ds(pl.multiple_of(step * tile, tile), tile)
            fill(own.at[:, span], 0, slot, step)
            sky_copy(slot, step).wait()

        for skipped in range(tiles):

            @pl.when(begins == skipped)
            def _():
                span = slice(skipped * tile, piece_rows)
                part[slot] = jnp.dot(own[:, span], sky_in[slot, span], preferred_element_type=jnp.float32)

        @pl.when(begins == tiles)
        def _():
            part[slot] = jnp.zeros(part.shape[1:], part.dtype)

    for distance in range(1, ways):
        beam_arrives(distance)
        for slot in range(slots):
            where_needed(distance, slot, lambda distance=distance, slot=slot: distant_copy(distance, slot).wait())

        @pl.loop(0, slots)
        def _(slot):
            @pl.loop(begin(distance, slot), tiles)
            def _(step):
                span = pl.ds(pl.multiple_of(step * tile, tile), tile)
                fill(factors.at[distance - 1, slot, :, span], distance, slot, step)

    for slot in range(slots):

        def drop(slot=slot):
            @pl.loop(0, begin(0, slot))
            def _(step):
                wigner_copy(slot, step).wait()
                sky_copy(slot, step).wait()

        where_needed(0, slot, drop)


def crossed(core, outer):
    return (core % 2) * (outer == INNER)


def distance_of(first, second, outer):
    straight = second * INNER + first
    return jnp.where(crossed(lax.axis_index("beamk"), outer) == 1, first * INNER + second, straight)


def second_kernel(ways, outer, tile, info, _, factors, *refs):
    pieces, refs = refs[: ways - 1], refs[ways - 1 :]
    outs, (acc, turned) = refs[:INNER], refs[INNER:]
    slots, rows, columns = acc.shape
    rows = rows // 2
    piece_rows = pieces[0].shape[1]
    tiles = piece_rows // tile
    width = outs[0].shape[1]
    cycles = outer * INNER
    k_local = width // slots
    pitch = turned.shape[1] // cycles

    m_values = [jnp.max(info[slot : slot + 1, :]).astype(jnp.int32) for slot in range(slots)]

    def finish(slot):
        for k in range(k_local):
            span = slice(k * cycles, (k + 1) * cycles)
            total = acc[slot, span] + turn_by_i(acc[slot, rows + k * cycles : rows + (k + 1) * cycles])
            for lane in range(columns // LANES):
                turned[lane, pl.ds(slot * k_local + k, cycles, stride=pitch), :] = total[:, lane * LANES : (lane + 1) * LANES]

    for slot in range(slots):
        for distance in range(1, ways):
            beside = slot > 0 and distance == ways - 1
            missing = first_tile(m_values[slot], owner_of(distance, ways), piece_rows, tile)
            for skipped in range(tiles + (1 if beside else 0)):

                @pl.when(missing == skipped)
                def _():
                    span = slice(skipped * tile, piece_rows)
                    if skipped < tiles:
                        acc[slot] += jnp.dot(
                            factors[distance - 1, slot, :, span],
                            pieces[distance - 1][slot, span],
                            preferred_element_type=jnp.float32,
                        )
                    if beside:
                        finish(slot - 1)

    finish(slots - 1)
    me = lax.axis_index("blk")
    for first in range(INNER):
        for second in range(outer):
            start = (me ^ distance_of(first, second, outer)) * pitch
            for lane in range(columns // LANES):
                block = turned[lane, pl.ds(start, width), :].astype(jnp.bfloat16)
                outs[first][second, :, lane * LANES : (lane + 1) * LANES] = block


def far_first(arrays):
    return [arrays[0], *reversed(arrays[1:])]


def regroup_kernel(outer, *refs):
    arrived, onward = far_first(refs[:INNER]), refs[INNER:]
    for second in range(outer):
        for first in range(INNER):
            onward[second][first] = arrived[first][second]


def place_kernel(outer, *refs):
    arrived, (out, turned, staged, sem) = far_first(refs[:outer]), refs[outer:]
    k_local, slot_count, columns = staged.shape
    width = arrived[0].shape[1]
    slots = width // k_local
    pitch = turned.shape[1] // k_local
    me = lax.axis_index("blk")
    for lane in range(columns // LANES):
        span = slice(lane * LANES, (lane + 1) * LANES)
        for second in range(outer):
            for first in range(INNER):
                block = arrived[second][first, :, span].astype(jnp.float32)
                source = me ^ distance_of(first, second, outer)
                for slot in range(slots):
                    turned[lane, pl.ds(slots * source + slot, k_local, stride=pitch), :] = block[slot * k_local : (slot + 1) * k_local]
    copies = []
    step = -(-k_local // 4)
    for number, start in enumerate(range(0, k_local, step)):
        end = min(start + step, k_local)
        for k in range(start, end):
            for lane in range(columns // LANES):
                values = turned[lane, k * pitch : k * pitch + slot_count]
                staged[k, :, lane * LANES : (lane + 1) * LANES] = values.astype(staged.dtype)
        copies.append(pltpu.make_async_copy(staged.at[start:end], out.at[start:end], sem.at[number]))
        copies[-1].start()
    for copy in copies:
        copy.wait()


def local(sky, beam, wigner, m_list, *, ways, peers):
    slots, piece_rows, columns = sky.shape
    _, k_local, cycles, degrees = wigner.shape
    rows = k_local * cycles
    tile = tile_of(piece_rows)
    tiles = piece_rows // tile
    lane_tiles = columns // LANES
    width = slots * k_local
    params = pltpu.CompilerParams(vmem_limit_bytes=VMEM_LIMIT)

    pieces = []
    for shift in range(1, ways):
        perm = [(c, (c + shift) % ways) for c in range(ways)]
        pieces.append(pltpu.with_memory_space_constraint(lax.ppermute(sky, "beamk", perm), pltpu.VMEM))
    sky, beam, wigner, m_list = (pltpu.with_memory_space_constraint(x, pltpu.HBM) for x in (sky, beam, wigner, m_list))

    part, factors, info = pl.pallas_call(
        functools.partial(first_kernel, ways, tile),
        out_shape=(
            pltpu.VMEM((slots, 2 * rows, columns), jnp.float32),
            pltpu.VMEM((ways - 1, slots, 2 * rows, piece_rows), jnp.bfloat16),
            pltpu.VMEM((8, LANES), jnp.float32),
        ),
        in_specs=[whole(pltpu.HBM)] * 4,
        out_specs=(whole(pltpu.VMEM),) * 3,
        scratch_shapes=[
            pltpu.SMEM(m_list.shape, jnp.int32),
            pltpu.VMEM((slots, piece_rows, columns), jnp.bfloat16),
            pltpu.VMEM(wigner.shape, jnp.bfloat16),
            pltpu.VMEM((2, k_local, degrees + slots * tile), jnp.float32),
            pltpu.VMEM((2 * rows, piece_rows), jnp.bfloat16),
            pltpu.SemaphoreType.DMA,
            pltpu.SemaphoreType.DMA((slots, tiles)),
            pltpu.SemaphoreType.DMA((slots, tiles)),
            pltpu.SemaphoreType.DMA((ways - 1, slots)),
            pltpu.SemaphoreType.DMA((ways, 2)),
        ],
        compiler_params=params,
        cost_estimate=pl.CostEstimate(
            flops=4 * slots * rows * piece_rows * columns, bytes_accessed=8 * 1024 * 1024, transcendentals=0
        ),
        name="own_half",
    )(m_list, sky, wigner, beam)

    outer = peers // INNER

    def blocks(number):
        return pltpu.VMEM((number, width, columns), jnp.bfloat16)

    *sends, _ = pl.pallas_call(
        functools.partial(second_kernel, ways, outer, tile),
        out_shape=[blocks(outer)] * INNER + [pltpu.VMEM(part.shape, part.dtype)],
        in_specs=[whole(pltpu.VMEM)] * (ways + 2),
        out_specs=[whole(pltpu.VMEM)] * (INNER + 1),
        input_output_aliases={1: INNER},
        scratch_shapes=[
            pltpu.VMEM((lane_tiles, cycles * (width + 1 - width % 2), LANES), jnp.float32),
        ],
        compiler_params=params,
        cost_estimate=pl.CostEstimate(
            flops=4 * slots * rows * piece_rows * columns, bytes_accessed=8 * 1024 * 1024, transcendentals=0
        ),
        name="other_half",
    )(info, part, factors, *pieces)

    def send(array, number, step):
        perm = []
        for b in range(peers):
            for core in range(ways):
                over_outer = (step == 0) == bool(crossed(core, outer))
                perm.append((b * ways + core, (b ^ (number * INNER if over_outer else number)) * ways + core))
        return pltpu.with_memory_space_constraint(lax.ppermute(array, ("blk", "beamk"), perm), pltpu.VMEM)

    first = list(sends)
    for number in range(1, INNER):
        first[number] = send(first[number], number, 0)
    second = list(
        pl.pallas_call(
            functools.partial(regroup_kernel, outer),
            out_shape=[blocks(INNER)] * outer,
            in_specs=[whole(pltpu.VMEM)] * INNER,
            out_specs=[whole(pltpu.VMEM)] * outer,
            compiler_params=params,
            name="regroup",
        )(*far_first(first))
    )
    for number in range(1, outer):
        second[number] = send(second[number], number, 1)
    slot_count = slots * peers
    out = pl.pallas_call(
        functools.partial(place_kernel, outer),
        out_shape=pltpu.HBM((k_local, slot_count, columns), jnp.bfloat16),
        in_specs=[whole(pltpu.VMEM)] * outer,
        out_specs=whole(pltpu.HBM),
        scratch_shapes=[
            pltpu.VMEM((lane_tiles, k_local * (slot_count + 1), LANES), jnp.float32),
            pltpu.VMEM((k_local, slot_count, columns), jnp.bfloat16),
            pltpu.SemaphoreType.DMA((4,)),
        ],
        compiler_params=params,
        name="place",
    )(*far_first(second))
    return out.transpose(1, 0, 2)[None]


def solution(mesh):
    in_specs = (
        P("blk", "beamk", None),
        P("beamk", None, None),
        P("blk", "beamk", None, None),
        P("blk"),
    )
    out_specs = P("blk", None, "beamk", None)
    body = functools.partial(local, ways=mesh.shape["beamk"], peers=mesh.shape["blk"])
    return jax.shard_map(body, mesh=mesh, in_specs=in_specs, out_specs=out_specs, check_vma=False)
```

```python
import functools

import jax
import jax.numpy as jnp
from jax import lax
from jax.experimental import pallas as pl
from jax.experimental.pallas import tpu as pltpu
from jax.sharding import PartitionSpec as P

KB = 40
LANES = 128
INNER = 4
VMEM_LIMIT = 24 * 1024 * 1024


def tile_of(rows):
    return max(t for t in range(LANES, min(rows, 512) + 1, LANES) if rows % t == 0)


def whole(memory):
    return pl.BlockSpec(memory_space=memory)


def turn_by_i(rows):
    half = rows.shape[1] // 2
    swapped = pltpu.roll(rows, half, 1)
    column = lax.broadcasted_iota(jnp.int32, swapped.shape, 1)
    return jnp.where(column < half, -swapped, swapped)


def owner_of(distance, ways):
    return lax.rem(lax.axis_index("beamk") - distance + ways, ways)


def first_tile(m_value, owner, piece_rows, tile):
    return jnp.minimum(jnp.maximum(m_value - owner * piece_rows, 0) // tile, piece_rows // tile)


def first_kernel(
    ways, tile, m_list, sky, wigner, beam, part, factors, info, m_ref, sky_in, wigner_in, beam_in, own, m_sem, sky_sem, wigner_sem, distant_sem, beam_sem
):
    slots, piece_rows, columns = sky.shape
    k_local, cycles = wigner.shape[1], wigner.shape[2]
    rows = k_local * cycles
    tiles = piece_rows // tile
    all_tiles = ways * tiles
    first_k = lax.axis_index("beamk") * k_local - KB // 2
    last = tiles - 1

    def m_copy():
        return pltpu.make_async_copy(m_list, m_ref, m_sem)

    def beam_copy(distance, half):
        span = pl.ds(pl.multiple_of(owner_of(distance, ways) * piece_rows, tile), piece_rows)
        return pltpu.make_async_copy(beam.at[:, half, span], beam_in.at[half, :, span], beam_sem.at[distance, half])

    def sky_copy(slot, step):
        span = pl.ds(pl.multiple_of(step * tile, tile), tile)
        return pltpu.make_async_copy(sky.at[slot, span], sky_in.at[slot, span], sky_sem.at[slot, step])

    def wigner_copy(slot, step):
        start = pl.multiple_of(owner_of(0, ways) * piece_rows + step * tile, tile)
        span = pl.ds(start, tile)
        return pltpu.make_async_copy(wigner.at[slot, :, :, span], wigner_in.at[slot, :, :, span], wigner_sem.at[slot, step])

    def distant_copy(distance, slot):
        span = pl.ds(pl.multiple_of(owner_of(distance, ways) * piece_rows, tile), piece_rows)
        return pltpu.make_async_copy(wigner.at[slot, :, :, span], wigner_in.at[slot, :, :, span], distant_sem.at[distance - 1, slot])

    def begin(distance, slot):
        return first_tile(m_ref[slot], owner_of(distance, ways), piece_rows, tile)

    def fill(target, distance, slot, step):
        index = owner_of(distance, ways) * tiles + step
        rows_of = pl.ds(pl.multiple_of(index * tile, tile), tile)
        index = jnp.where(index == m_ref[slot] // tile, all_tiles + slot, index)
        span = pl.ds(pl.multiple_of(index * tile, tile), tile)
        for k in range(k_local):
            values = wigner_in[slot, k, :, rows_of]
            for half in range(2):
                factor = jnp.broadcast_to(beam_in[half, k : k + 1, span], (cycles, tile)).astype(jnp.bfloat16)
                target[half * rows + k * cycles : half * rows + (k + 1) * cycles, :] = values * factor

    def cut(slot):
        index = m_ref[slot] // tile
        degrees = index * tile + lax.broadcasted_iota(jnp.int32, (k_local, tile), 1)
        k_values = first_k + lax.broadcasted_iota(jnp.int32, (k_local, tile), 0)
        inside = degrees >= jnp.maximum(m_ref[slot], jnp.abs(k_values))
        span = pl.ds(pl.multiple_of(index * tile, tile), tile)
        for half in range(2):
            beam_in[half, :, (all_tiles + slot) * tile : (all_tiles + slot + 1) * tile] = jnp.where(inside, beam_in[half, :, span], 0.0)

    def cut_in(distance, slot):
        return m_ref[slot] // piece_rows == owner_of(distance, ways)

    def upper(distance):
        return 2 * (owner_of(distance, ways) + 1) > ways

    def where_needed(distance, slot, do):
        if slot % 2 == 0:
            do()
        else:
            pl.when(upper(distance))(do)

    m_copy().start()
    for slot in range(slots):

        def fetch(slot=slot):
            for step in reversed(range(tiles)):
                wigner_copy(slot, step).start()
                if slot == 0 and step == last:
                    for half in range(2):
                        beam_copy(0, half).start()
                sky_copy(slot, step).start()

        where_needed(0, slot, fetch)
    for distance in range(1, ways):
        for half in range(2):
            beam_copy(distance, half).start()
        for slot in range(slots):
            where_needed(distance, slot, lambda distance=distance, slot=slot: distant_copy(distance, slot).start())
    m_copy().wait()
    for slot in range(slots):
        info[slot : slot + 1, :] = jnp.full((1, LANES), m_ref[slot].astype(jnp.float32))
    def beam_arrives(distance):
        for half in range(2):
            beam_copy(distance, half).wait()
        for slot in range(slots):
            pl.when(cut_in(distance, slot))(functools.partial(cut, slot))

    beam_arrives(0)

    @pl.loop(0, slots)
    def _(slot):
        begins = begin(0, slot)

        @pl.loop(begins, tiles)
        def _(later):
            step = tiles - 1 - later + begins
            wigner_copy(slot, step).wait()
            span = pl.ds(pl.multiple_of(step * tile, tile), tile)
            fill(own.at[:, span], 0, slot, step)
            sky_copy(slot, step).wait()

        for skipped in range(tiles):

            @pl.when(begins == skipped)
            def _():
                span = slice(skipped * tile, piece_rows)
                part[slot] = jnp.dot(own[:, span], sky_in[slot, span], preferred_element_type=jnp.float32)

        @pl.when(begins == tiles)
        def _():
            part[slot] = jnp.zeros(part.shape[1:], part.dtype)

    for distance in range(1, ways):
        beam_arrives(distance)
        for slot in range(slots):
            where_needed(distance, slot, lambda distance=distance, slot=slot: distant_copy(distance, slot).wait())

        @pl.loop(0, slots)
        def _(slot):
            @pl.loop(begin(distance, slot), tiles)
            def _(step):
                span = pl.ds(pl.multiple_of(step * tile, tile), tile)
                fill(factors.at[distance - 1, slot, :, span], distance, slot, step)

    for slot in range(slots):

        def drop(slot=slot):
            @pl.loop(0, begin(0, slot))
            def _(step):
                wigner_copy(slot, step).wait()
                sky_copy(slot, step).wait()

        where_needed(0, slot, drop)


def crossed(core, outer):
    return (core % 2) * (outer == INNER)


def outer_distance(number, outer):
    return (outer - number) % outer


def inner_distance(number):
    return (0, 1, 3, 2)[number]


def distance_of(first, second, outer):
    straight = outer_distance(second, outer) * INNER + inner_distance(first)
    if outer != INNER:
        return straight
    other = outer_distance(first, outer) * INNER + inner_distance(second)
    return jnp.where(crossed(lax.axis_index("beamk"), outer) == 1, other, straight)


def second_kernel(ways, outer, tile, info, _, factors, *refs):
    pieces, refs = refs[: ways - 1], refs[ways - 1 :]
    outs, (acc, turned) = refs[:INNER], refs[INNER:]
    slots, rows, columns = acc.shape
    rows = rows // 2
    piece_rows = pieces[0].shape[1]
    tiles = piece_rows // tile
    width = outs[0].shape[1]
    cycles = outer * INNER
    k_local = width // slots
    pitch = turned.shape[1] // cycles

    m_values = [jnp.max(info[slot : slot + 1, :]).astype(jnp.int32) for slot in range(slots)]

    def finish(slot):
        for k in range(k_local):
            span = slice(k * cycles, (k + 1) * cycles)
            total = acc[slot, span] + turn_by_i(acc[slot, rows + k * cycles : rows + (k + 1) * cycles])
            for lane in range(columns // LANES):
                turned[lane, pl.ds(slot * k_local + k, cycles, stride=pitch), :] = total[:, lane * LANES : (lane + 1) * LANES]

    for slot in range(slots):
        for distance in range(1, ways):
            beside = slot > 0 and distance == ways - 1
            missing = first_tile(m_values[slot], owner_of(distance, ways), piece_rows, tile)
            for skipped in range(tiles + (1 if beside else 0)):

                @pl.when(missing == skipped)
                def _():
                    span = slice(skipped * tile, piece_rows)
                    if skipped < tiles:
                        acc[slot] += jnp.dot(
                            factors[distance - 1, slot, :, span],
                            pieces[distance - 1][slot, span],
                            preferred_element_type=jnp.float32,
                        )
                    if beside:
                        finish(slot - 1)

    finish(slots - 1)
    me = lax.axis_index("blk")
    for first in range(INNER):
        for second in range(outer):
            start = (me ^ distance_of(first, second, outer)) * pitch
            for lane in range(columns // LANES):
                block = turned[lane, pl.ds(start, width), :].astype(jnp.bfloat16)
                outs[first][second, :, lane * LANES : (lane + 1) * LANES] = block


def regroup_kernel(outer, *refs):
    arrived, onward = refs[:INNER], refs[INNER:]
    for second in range(outer):
        for first in range(INNER):
            onward[second][first] = arrived[first][second]


def place_kernel(outer, *refs):
    arrived, (out, turned, staged, sem) = refs[:outer], refs[outer:]
    lane_tiles, k_local, slot_count, _ = staged.shape
    columns = lane_tiles * LANES
    width = arrived[0].shape[1]
    slots = width // k_local
    pitch = turned.shape[1] // k_local
    me = lax.axis_index("blk")
    copies = []
    for lane in range(columns // LANES):
        span = slice(lane * LANES, (lane + 1) * LANES)
        for second in range(outer):
            for first in range(INNER):
                block = arrived[second][first, :, span].astype(jnp.float32)
                source = me ^ distance_of(first, second, outer)
                for slot in range(slots):
                    turned[lane, pl.ds(slots * source + slot, k_local, stride=pitch), :] = block[slot * k_local : (slot + 1) * k_local]
        for k in range(k_local):
            staged[lane, k] = turned[lane, k * pitch : k * pitch + slot_count].astype(staged.dtype)
        copies.append(pltpu.make_async_copy(staged.at[lane], out.at[:, :, span], sem.at[lane]))
        copies[-1].start()
    for copy in copies:
        copy.wait()


def local(sky, beam, wigner, m_list, *, ways, peers):
    slots, piece_rows, columns = sky.shape
    _, k_local, cycles, degrees = wigner.shape
    rows = k_local * cycles
    tile = tile_of(piece_rows)
    tiles = piece_rows // tile
    lane_tiles = columns // LANES
    width = slots * k_local
    params = pltpu.CompilerParams(vmem_limit_bytes=VMEM_LIMIT)

    pieces = []
    for shift in range(1, ways):
        perm = [(c, (c + shift) % ways) for c in range(ways)]
        pieces.append(pltpu.with_memory_space_constraint(lax.ppermute(sky, "beamk", perm), pltpu.VMEM))
    sky, beam, wigner, m_list = (pltpu.with_memory_space_constraint(x, pltpu.HBM) for x in (sky, beam, wigner, m_list))

    part, factors, info = pl.pallas_call(
        functools.partial(first_kernel, ways, tile),
        out_shape=(
            pltpu.VMEM((slots, 2 * rows, columns), jnp.float32),
            pltpu.VMEM((ways - 1, slots, 2 * rows, piece_rows), jnp.bfloat16),
            pltpu.VMEM((8, LANES), jnp.float32),
        ),
        in_specs=[whole(pltpu.HBM)] * 4,
        out_specs=(whole(pltpu.VMEM),) * 3,
        scratch_shapes=[
            pltpu.SMEM(m_list.shape, jnp.int32),
            pltpu.VMEM((slots, piece_rows, columns), jnp.bfloat16),
            pltpu.VMEM(wigner.shape, jnp.bfloat16),
            pltpu.VMEM((2, k_local, degrees + slots * tile), jnp.float32),
            pltpu.VMEM((2 * rows, piece_rows), jnp.bfloat16),
            pltpu.SemaphoreType.DMA,
            pltpu.SemaphoreType.DMA((slots, tiles)),
            pltpu.SemaphoreType.DMA((slots, tiles)),
            pltpu.SemaphoreType.DMA((ways - 1, slots)),
            pltpu.SemaphoreType.DMA((ways, 2)),
        ],
        compiler_params=params,
        cost_estimate=pl.CostEstimate(
            flops=4 * slots * rows * piece_rows * columns, bytes_accessed=8 * 1024 * 1024, transcendentals=0
        ),
        name="own_half",
    )(m_list, sky, wigner, beam)

    outer = peers // INNER

    def blocks(number):
        return pltpu.VMEM((number, width, columns), jnp.bfloat16)

    *sends, _ = pl.pallas_call(
        functools.partial(second_kernel, ways, outer, tile),
        out_shape=[blocks(outer)] * INNER + [pltpu.VMEM(part.shape, part.dtype)],
        in_specs=[whole(pltpu.VMEM)] * (ways + 2),
        out_specs=[whole(pltpu.VMEM)] * (INNER + 1),
        input_output_aliases={1: INNER},
        scratch_shapes=[
            pltpu.VMEM((lane_tiles, cycles * (width + 1 - width % 2), LANES), jnp.float32),
        ],
        compiler_params=params,
        cost_estimate=pl.CostEstimate(
            flops=4 * slots * rows * piece_rows * columns, bytes_accessed=8 * 1024 * 1024, transcendentals=0
        ),
        name="other_half",
    )(info, part, factors, *pieces)

    def send(array, number, step):
        perm = []
        for b in range(peers):
            for core in range(ways):
                over_outer = (step == 0) == bool(crossed(core, outer))
                distance = outer_distance(number, outer) * INNER if over_outer else inner_distance(number)
                perm.append((b * ways + core, (b ^ distance) * ways + core))
        return pltpu.with_memory_space_constraint(lax.ppermute(array, ("blk", "beamk"), perm), pltpu.VMEM)

    first = list(sends)
    for number in range(1, INNER):
        first[number] = send(first[number], number, 0)
    second = list(
        pl.pallas_call(
            functools.partial(regroup_kernel, outer),
            out_shape=[blocks(INNER)] * outer,
            in_specs=[whole(pltpu.VMEM)] * INNER,
            out_specs=[whole(pltpu.VMEM)] * outer,
            compiler_params=params,
            name="regroup",
        )(*first)
    )
    for number in range(1, outer):
        second[number] = send(second[number], number, 1)
    slot_count = slots * peers
    out = pl.pallas_call(
        functools.partial(place_kernel, outer),
        out_shape=pltpu.HBM((k_local, slot_count, columns), jnp.bfloat16),
        in_specs=[whole(pltpu.VMEM)] * outer,
        out_specs=whole(pltpu.HBM),
        scratch_shapes=[
            pltpu.VMEM((lane_tiles, k_local * (slot_count + 1), LANES), jnp.float32),
            pltpu.VMEM((lane_tiles, k_local, slot_count, LANES), jnp.bfloat16),
            pltpu.SemaphoreType.DMA((lane_tiles,)),
        ],
        compiler_params=params,
        name="place",
    )(*second)
    return out.transpose(1, 0, 2)[None]


def solution(mesh):
    in_specs = (
        P("blk", "beamk", None),
        P("beamk", None, None),
        P("blk", "beamk", None, None),
        P("blk"),
    )
    out_specs = P("blk", None, "beamk", None)
    body = functools.partial(local, ways=mesh.shape["beamk"], peers=mesh.shape["blk"])
    return jax.shard_map(body, mesh=mesh, in_specs=in_specs, out_specs=out_specs, check_vma=False)
```

```python
import functools

import jax
import jax.numpy as jnp
from jax import lax
from jax.experimental import pallas as pl
from jax.experimental.pallas import tpu as pltpu
from jax.sharding import PartitionSpec as P

KB = 40
LANES = 128
INNER = 4
VMEM_LIMIT = 24 * 1024 * 1024


def tile_of(rows):
    return max(t for t in range(LANES, min(rows, 512) + 1, LANES) if rows % t == 0)


def pitch_of(rows):
    return rows + 1 - rows % 2


def turning(lane_tiles, groups, rows):
    return pltpu.VMEM((lane_tiles, -(-groups // 8) * 8 * pitch_of(rows) + 8, LANES), jnp.float32)


def whole(memory):
    return pl.BlockSpec(memory_space=memory)


def turn_by_i(rows):
    half = rows.shape[1] // 2
    swapped = pltpu.roll(rows, half, 1)
    column = lax.broadcasted_iota(jnp.int32, swapped.shape, 1)
    return jnp.where(column < half, -swapped, swapped)


def owner_of(distance, ways):
    return lax.rem(lax.axis_index("beamk") - distance + ways, ways)


def first_tile(m_value, owner, piece_rows, tile):
    return jnp.minimum(jnp.maximum(m_value - owner * piece_rows, 0) // tile, piece_rows // tile)


def first_kernel(
    ways, tile, m_list, sky, wigner, beam, part, factors, info, m_ref, sky_in, wigner_in, beam_in, own, m_sem, sky_sem, wigner_sem, distant_sem, beam_sem
):
    slots, piece_rows, columns = sky.shape
    k_local, cycles = wigner.shape[1], wigner.shape[2]
    rows = k_local * cycles
    tiles = piece_rows // tile
    all_tiles = ways * tiles
    first_k = lax.axis_index("beamk") * k_local - KB // 2
    last = tiles - 1

    def m_copy():
        return pltpu.make_async_copy(m_list, m_ref, m_sem)

    def beam_copy(distance, half):
        span = pl.ds(pl.multiple_of(owner_of(distance, ways) * piece_rows, tile), piece_rows)
        return pltpu.make_async_copy(beam.at[:, half, span], beam_in.at[half, :, span], beam_sem.at[distance, half])

    def sky_copy(slot, step):
        span = pl.ds(pl.multiple_of(step * tile, tile), tile)
        return pltpu.make_async_copy(sky.at[slot, span], sky_in.at[slot, span], sky_sem.at[slot, step])

    def wigner_copy(slot, step):
        start = pl.multiple_of(owner_of(0, ways) * piece_rows + step * tile, tile)
        span = pl.ds(start, tile)
        return pltpu.make_async_copy(wigner.at[slot, :, :, span], wigner_in.at[slot, :, :, span], wigner_sem.at[slot, step])

    def distant_copy(distance, slot):
        span = pl.ds(pl.multiple_of(owner_of(distance, ways) * piece_rows, tile), piece_rows)
        return pltpu.make_async_copy(wigner.at[slot, :, :, span], wigner_in.at[slot, :, :, span], distant_sem.at[distance - 1, slot])

    def begin(distance, slot):
        return first_tile(m_ref[slot], owner_of(distance, ways), piece_rows, tile)

    def fill(target, distance, slot, step):
        index = owner_of(distance, ways) * tiles + step
        rows_of = pl.ds(pl.multiple_of(index * tile, tile), tile)
        index = jnp.where(index == m_ref[slot] // tile, all_tiles + slot, index)
        span = pl.ds(pl.multiple_of(index * tile, tile), tile)
        for k in range(k_local):
            values = wigner_in[slot, k, :, rows_of]
            for half in range(2):
                factor = jnp.broadcast_to(beam_in[half, k : k + 1, span], (cycles, tile)).astype(jnp.bfloat16)
                target[half * rows + k * cycles : half * rows + (k + 1) * cycles, :] = values * factor

    def cut(slot):
        index = m_ref[slot] // tile
        degrees = index * tile + lax.broadcasted_iota(jnp.int32, (k_local, tile), 1)
        k_values = first_k + lax.broadcasted_iota(jnp.int32, (k_local, tile), 0)
        inside = degrees >= jnp.maximum(m_ref[slot], jnp.abs(k_values))
        span = pl.ds(pl.multiple_of(index * tile, tile), tile)
        for half in range(2):
            beam_in[half, :, (all_tiles + slot) * tile : (all_tiles + slot + 1) * tile] = jnp.where(inside, beam_in[half, :, span], 0.0)

    def cut_in(distance, slot):
        return m_ref[slot] // piece_rows == owner_of(distance, ways)

    def upper(distance):
        return 2 * (owner_of(distance, ways) + 1) > ways

    def where_needed(distance, slot, do):
        if slot % 2 == 0:
            do()
        else:
            pl.when(upper(distance))(do)

    m_copy().start()
    for slot in range(slots):

        def fetch(slot=slot):
            for step in reversed(range(tiles)):
                wigner_copy(slot, step).start()
                if slot == 0 and step == last:
                    for half in range(2):
                        beam_copy(0, half).start()
                sky_copy(slot, step).start()

        where_needed(0, slot, fetch)
    for distance in range(1, ways):
        for half in range(2):
            beam_copy(distance, half).start()
        for slot in range(slots):
            where_needed(distance, slot, lambda distance=distance, slot=slot: distant_copy(distance, slot).start())
    m_copy().wait()
    for slot in range(slots):
        info[slot : slot + 1, :] = jnp.full((1, LANES), m_ref[slot].astype(jnp.float32))
    def beam_arrives(distance):
        for half in range(2):
            beam_copy(distance, half).wait()
        for slot in range(slots):
            pl.when(cut_in(distance, slot))(functools.partial(cut, slot))

    beam_arrives(0)

    @pl.loop(0, slots)
    def _(slot):
        begins = begin(0, slot)

        @pl.loop(begins, tiles)
        def _(later):
            step = tiles - 1 - later + begins
            wigner_copy(slot, step).wait()
            span = pl.ds(pl.multiple_of(step * tile, tile), tile)
            fill(own.at[:, span], 0, slot, step)
            sky_copy(slot, step).wait()

        for skipped in range(tiles):

            @pl.when(begins == skipped)
            def _():
                span = slice(skipped * tile, piece_rows)
                part[slot] = jnp.dot(own[:, span], sky_in[slot, span], preferred_element_type=jnp.float32)

        @pl.when(begins == tiles)
        def _():
            part[slot] = jnp.zeros(part.shape[1:], part.dtype)

    for distance in range(1, ways):
        beam_arrives(distance)
        for slot in range(slots):
            where_needed(distance, slot, lambda distance=distance, slot=slot: distant_copy(distance, slot).wait())

        @pl.loop(0, slots)
        def _(slot):
            @pl.loop(begin(distance, slot), tiles)
            def _(step):
                span = pl.ds(pl.multiple_of(step * tile, tile), tile)
                fill(factors.at[distance - 1, slot, :, span], distance, slot, step)

    for slot in range(slots):

        def drop(slot=slot):
            @pl.loop(0, begin(0, slot))
            def _(step):
                wigner_copy(slot, step).wait()
                sky_copy(slot, step).wait()

        where_needed(0, slot, drop)


def crossed(core, outer):
    return (core % 2) * (outer == INNER)


def distance_of(first, second, outer):
    straight = second * INNER + first
    return jnp.where(crossed(lax.axis_index("beamk"), outer) == 1, first * INNER + second, straight)


def second_kernel(ways, outer, tile, info, _, factors, *refs):
    pieces, refs = refs[: ways - 1], refs[ways - 1 :]
    outs, (acc, turned) = refs[:INNER], refs[INNER:]
    slots, rows, columns = acc.shape
    rows = rows // 2
    piece_rows = pieces[0].shape[1]
    tiles = piece_rows // tile
    width = outs[0].shape[1]
    cycles = outer * INNER
    k_local = width // slots
    pitch = pitch_of(width)

    m_values = [jnp.max(info[slot : slot + 1, :]).astype(jnp.int32) for slot in range(slots)]

    def finish(slot):
        for k in range(k_local):
            span = slice(k * cycles, (k + 1) * cycles)
            total = acc[slot, span] + turn_by_i(acc[slot, rows + k * cycles : rows + (k + 1) * cycles])
            for lane in range(columns // LANES):
                turned[lane, pl.ds(slot * k_local + k, cycles, stride=pitch), :] = total[:, lane * LANES : (lane + 1) * LANES]

    for slot in range(slots):
        for distance in range(1, ways):
            beside = slot > 0 and distance == ways - 1
            missing = first_tile(m_values[slot], owner_of(distance, ways), piece_rows, tile)
            for skipped in range(tiles + (1 if beside else 0)):

                @pl.when(missing == skipped)
                def _():
                    span = slice(skipped * tile, piece_rows)
                    if skipped < tiles:
                        acc[slot] += jnp.dot(
                            factors[distance - 1, slot, :, span],
                            pieces[distance - 1][slot, span],
                            preferred_element_type=jnp.float32,
                        )
                    if beside:
                        finish(slot - 1)

    finish(slots - 1)
    me = lax.axis_index("blk")
    for first in range(INNER):
        for second in range(outer):
            start = (me ^ distance_of(first, second, outer)) * pitch
            for lane in range(columns // LANES):
                block = turned[lane, pl.ds(start, width), :].astype(jnp.bfloat16)
                outs[first][second, :, lane * LANES : (lane + 1) * LANES] = block


def far_first(arrays):
    return [arrays[0], *reversed(arrays[1:])]


def regroup_kernel(outer, *refs):
    arrived, onward = far_first(refs[:INNER]), refs[INNER:]
    for second in range(outer):
        for first in range(INNER):
            onward[second][first] = arrived[first][second]


def place_kernel(outer, *refs):
    arrived, (out, turned, staged, sem) = far_first(refs[:outer]), refs[outer:]
    k_local, slot_count, columns = staged.shape
    width = arrived[0].shape[1]
    slots = width // k_local
    pitch = pitch_of(slot_count)
    me = lax.axis_index("blk")
    for lane in range(columns // LANES):
        span = slice(lane * LANES, (lane + 1) * LANES)
        for second in range(outer):
            for first in range(INNER):
                block = arrived[second][first, :, span].astype(jnp.float32)
                source = me ^ distance_of(first, second, outer)
                for slot in range(slots):
                    turned[lane, pl.ds(slots * source + slot, k_local, stride=pitch), :] = block[slot * k_local : (slot + 1) * k_local]
    copies = []
    step = -(-k_local // 4)
    for number, start in enumerate(range(0, k_local, step)):
        end = min(start + step, k_local)
        for k in range(start, end):
            for lane in range(columns // LANES):
                values = turned[lane, k * pitch : k * pitch + slot_count]
                staged[k, :, lane * LANES : (lane + 1) * LANES] = values.astype(staged.dtype)
        copies.append(pltpu.make_async_copy(staged.at[start:end], out.at[start:end], sem.at[number]))
        copies[-1].start()
    for copy in copies:
        copy.wait()


def local(sky, beam, wigner, m_list, *, ways, peers):
    slots, piece_rows, columns = sky.shape
    _, k_local, cycles, degrees = wigner.shape
    rows = k_local * cycles
    tile = tile_of(piece_rows)
    tiles = piece_rows // tile
    lane_tiles = columns // LANES
    width = slots * k_local
    params = pltpu.CompilerParams(vmem_limit_bytes=VMEM_LIMIT)

    pieces = []
    for shift in range(1, ways):
        perm = [(c, (c + shift) % ways) for c in range(ways)]
        pieces.append(pltpu.with_memory_space_constraint(lax.ppermute(sky, "beamk", perm), pltpu.VMEM))
    sky, beam, wigner, m_list = (pltpu.with_memory_space_constraint(x, pltpu.HBM) for x in (sky, beam, wigner, m_list))

    part, factors, info = pl.pallas_call(
        functools.partial(first_kernel, ways, tile),
        out_shape=(
            pltpu.VMEM((slots, 2 * rows, columns), jnp.float32),
            pltpu.VMEM((ways - 1, slots, 2 * rows, piece_rows), jnp.bfloat16),
            pltpu.VMEM((8, LANES), jnp.float32),
        ),
        in_specs=[whole(pltpu.HBM)] * 4,
        out_specs=(whole(pltpu.VMEM),) * 3,
        scratch_shapes=[
            pltpu.SMEM(m_list.shape, jnp.int32),
            pltpu.VMEM((slots, piece_rows, columns), jnp.bfloat16),
            pltpu.VMEM(wigner.shape, jnp.bfloat16),
            pltpu.VMEM((2, k_local, degrees + slots * tile), jnp.float32),
            pltpu.VMEM((2 * rows, piece_rows), jnp.bfloat16),
            pltpu.SemaphoreType.DMA,
            pltpu.SemaphoreType.DMA((slots, tiles)),
            pltpu.SemaphoreType.DMA((slots, tiles)),
            pltpu.SemaphoreType.DMA((ways - 1, slots)),
            pltpu.SemaphoreType.DMA((ways, 2)),
        ],
        compiler_params=params,
        cost_estimate=pl.CostEstimate(
            flops=4 * slots * rows * piece_rows * columns, bytes_accessed=8 * 1024 * 1024, transcendentals=0
        ),
        name="own_half",
    )(m_list, sky, wigner, beam)

    outer = peers // INNER

    def blocks(number):
        return pltpu.VMEM((number, width, columns), jnp.bfloat16)

    *sends, _ = pl.pallas_call(
        functools.partial(second_kernel, ways, outer, tile),
        out_shape=[blocks(outer)] * INNER + [pltpu.VMEM(part.shape, part.dtype)],
        in_specs=[whole(pltpu.VMEM)] * (ways + 2),
        out_specs=[whole(pltpu.VMEM)] * (INNER + 1),
        input_output_aliases={1: INNER},
        scratch_shapes=[
            turning(lane_tiles, cycles, width),
        ],
        compiler_params=params,
        cost_estimate=pl.CostEstimate(
            flops=4 * slots * rows * piece_rows * columns, bytes_accessed=8 * 1024 * 1024, transcendentals=0
        ),
        name="other_half",
    )(info, part, factors, *pieces)

    def send(array, number, step):
        perm = []
        for b in range(peers):
            for core in range(ways):
                over_outer = (step == 0) == bool(crossed(core, outer))
                perm.append((b * ways + core, (b ^ (number * INNER if over_outer else number)) * ways + core))
        return pltpu.with_memory_space_constraint(lax.ppermute(array, ("blk", "beamk"), perm), pltpu.VMEM)

    first = list(sends)
    for number in range(1, INNER):
        first[number] = send(first[number], number, 0)
    second = list(
        pl.pallas_call(
            functools.partial(regroup_kernel, outer),
            out_shape=[blocks(INNER)] * outer,
            in_specs=[whole(pltpu.VMEM)] * INNER,
            out_specs=[whole(pltpu.VMEM)] * outer,
            compiler_params=params,
            name="regroup",
        )(*far_first(first))
    )
    for number in range(1, outer):
        second[number] = send(second[number], number, 1)
    slot_count = slots * peers
    out = pl.pallas_call(
        functools.partial(place_kernel, outer),
        out_shape=pltpu.HBM((k_local, slot_count, columns), jnp.bfloat16),
        in_specs=[whole(pltpu.VMEM)] * outer,
        out_specs=whole(pltpu.HBM),
        scratch_shapes=[
            turning(lane_tiles, k_local, slot_count),
            pltpu.VMEM((k_local, slot_count, columns), jnp.bfloat16),
            pltpu.SemaphoreType.DMA((4,)),
        ],
        compiler_params=params,
        name="place",
    )(*far_first(second))
    return out.transpose(1, 0, 2)[None]


def solution(mesh):
    in_specs = (
        P("blk", "beamk", None),
        P("beamk", None, None),
        P("blk", "beamk", None, None),
        P("blk"),
    )
    out_specs = P("blk", None, "beamk", None)
    body = functools.partial(local, ways=mesh.shape["beamk"], peers=mesh.shape["blk"])
    return jax.shard_map(body, mesh=mesh, in_specs=in_specs, out_specs=out_specs, check_vma=False)
```

```python
import functools

import jax
import jax.numpy as jnp
from jax import lax
from jax.experimental import pallas as pl
from jax.experimental.pallas import tpu as pltpu
from jax.sharding import PartitionSpec as P

KB = 40
LANES = 128
INNER = 4
VMEM_LIMIT = 24 * 1024 * 1024


def tile_of(rows):
    return max(t for t in range(LANES, min(rows, 512) + 1, LANES) if rows % t == 0)


def pitch_of(rows):
    return rows + 1 - rows % 2


def turning(lane_tiles, groups, rows):
    return pltpu.VMEM((lane_tiles, -(-groups // 8) * 8 * pitch_of(rows) + 8, LANES), jnp.float32)


def whole(memory):
    return pl.BlockSpec(memory_space=memory)


def turn_by_i(rows):
    half = rows.shape[1] // 2
    swapped = pltpu.roll(rows, half, 1)
    column = lax.broadcasted_iota(jnp.int32, swapped.shape, 1)
    return jnp.where(column < half, -swapped, swapped)


def owner_of(distance, ways):
    return lax.rem(lax.axis_index("beamk") - distance + ways, ways)


def first_tile(m_value, owner, piece_rows, tile):
    return jnp.minimum(jnp.maximum(m_value - owner * piece_rows, 0) // tile, piece_rows // tile)


def first_kernel(
    ways, tile, m_list, sky, wigner, beam, part, factors, info, m_ref, sky_in, wigner_in, beam_in, own, m_sem, sky_sem, wigner_sem, distant_sem, beam_sem
):
    slots, piece_rows, columns = sky.shape
    k_local, cycles = wigner.shape[1], wigner.shape[2]
    rows = k_local * cycles
    tiles = piece_rows // tile
    all_tiles = ways * tiles
    first_k = lax.axis_index("beamk") * k_local - KB // 2
    last = tiles - 1

    def m_copy():
        return pltpu.make_async_copy(m_list, m_ref, m_sem)

    def beam_copy(distance, half):
        span = pl.ds(pl.multiple_of(owner_of(distance, ways) * piece_rows, tile), piece_rows)
        return pltpu.make_async_copy(beam.at[:, half, span], beam_in.at[half, :, span], beam_sem.at[distance, half])

    def sky_copy(slot, step):
        span = pl.ds(pl.multiple_of(step * tile, tile), tile)
        return pltpu.make_async_copy(sky.at[slot, span], sky_in.at[slot, span], sky_sem.at[slot, step])

    def wigner_copy(slot, step):
        start = pl.multiple_of(owner_of(0, ways) * piece_rows + step * tile, tile)
        span = pl.ds(start, tile)
        return pltpu.make_async_copy(wigner.at[slot, :, :, span], wigner_in.at[slot, :, :, span], wigner_sem.at[slot, step])

    def distant_copy(distance, slot):
        span = pl.ds(pl.multiple_of(owner_of(distance, ways) * piece_rows, tile), piece_rows)
        return pltpu.make_async_copy(wigner.at[slot, :, :, span], wigner_in.at[slot, :, :, span], distant_sem.at[distance - 1, slot])

    def begin(distance, slot):
        return first_tile(m_ref[slot], owner_of(distance, ways), piece_rows, tile)

    def fill(target, distance, slot, step):
        index = owner_of(distance, ways) * tiles + step
        rows_of = pl.ds(pl.multiple_of(index * tile, tile), tile)
        index = jnp.where(index == m_ref[slot] // tile, all_tiles + slot, index)
        span = pl.ds(pl.multiple_of(index * tile, tile), tile)
        for k in range(k_local):
            values = wigner_in[slot, k, :, rows_of]
            for half in range(2):
                factor = jnp.broadcast_to(beam_in[half, k : k + 1, span], (cycles, tile)).astype(jnp.bfloat16)
                target[half * rows + k * cycles : half * rows + (k + 1) * cycles, :] = values * factor

    def cut(slot):
        index = m_ref[slot] // tile
        degrees = index * tile + lax.broadcasted_iota(jnp.int32, (k_local, tile), 1)
        k_values = first_k + lax.broadcasted_iota(jnp.int32, (k_local, tile), 0)
        inside = degrees >= jnp.maximum(m_ref[slot], jnp.abs(k_values))
        span = pl.ds(pl.multiple_of(index * tile, tile), tile)
        for half in range(2):
            beam_in[half, :, (all_tiles + slot) * tile : (all_tiles + slot + 1) * tile] = jnp.where(inside, beam_in[half, :, span], 0.0)

    def cut_in(distance, slot):
        return m_ref[slot] // piece_rows == owner_of(distance, ways)

    def upper(distance):
        return 2 * (owner_of(distance, ways) + 1) > ways

    def where_needed(distance, slot, do):
        if slot % 2 == 0:
            do()
        else:
            pl.when(upper(distance))(do)

    m_copy().start()
    for slot in range(slots):

        def fetch(slot=slot):
            for step in reversed(range(tiles)):
                wigner_copy(slot, step).start()
                if slot == 0 and step == last:
                    for half in range(2):
                        beam_copy(0, half).start()
                sky_copy(slot, step).start()

        where_needed(0, slot, fetch)
    for distance in range(1, ways):
        for half in range(2):
            beam_copy(distance, half).start()
        for slot in range(slots):
            where_needed(distance, slot, lambda distance=distance, slot=slot: distant_copy(distance, slot).start())
    m_copy().wait()
    for slot in range(slots):
        info[slot : slot + 1, :] = jnp.full((1, LANES), m_ref[slot].astype(jnp.float32))
    def beam_arrives(distance):
        for half in range(2):
            beam_copy(distance, half).wait()
        for slot in range(slots):
            pl.when(cut_in(distance, slot))(functools.partial(cut, slot))

    beam_arrives(0)

    @pl.loop(0, slots)
    def _(slot):
        begins = begin(0, slot)

        @pl.loop(begins, tiles)
        def _(later):
            step = tiles - 1 - later + begins
            wigner_copy(slot, step).wait()
            span = pl.ds(pl.multiple_of(step * tile, tile), tile)
            fill(own.at[:, span], 0, slot, step)
            sky_copy(slot, step).wait()

        for skipped in range(tiles):

            @pl.when(begins == skipped)
            def _():
                span = slice(skipped * tile, piece_rows)
                part[slot] = jnp.dot(own[:, span], sky_in[slot, span], preferred_element_type=jnp.float32)

        @pl.when(begins == tiles)
        def _():
            part[slot] = jnp.zeros(part.shape[1:], part.dtype)

    for distance in range(1, ways):
        beam_arrives(distance)
        for slot in range(slots):
            where_needed(distance, slot, lambda distance=distance, slot=slot: distant_copy(distance, slot).wait())

        @pl.loop(0, slots)
        def _(slot):
            @pl.loop(begin(distance, slot), tiles)
            def _(step):
                span = pl.ds(pl.multiple_of(step * tile, tile), tile)
                fill(factors.at[distance - 1, slot, :, span], distance, slot, step)

    for slot in range(slots):

        def drop(slot=slot):
            @pl.loop(0, begin(0, slot))
            def _(step):
                wigner_copy(slot, step).wait()
                sky_copy(slot, step).wait()

        where_needed(0, slot, drop)


def crossed(core, outer):
    return (core % 2) * (outer == INNER)


def distance_of(first, second, outer):
    straight = second * INNER + first
    return jnp.where(crossed(lax.axis_index("beamk"), outer) == 1, first * INNER + second, straight)


def second_kernel(ways, outer, tile, info, _, factors, *refs):
    pieces, refs = refs[: ways - 1], refs[ways - 1 :]
    outs, (acc, turned) = refs[:INNER], refs[INNER:]
    slots, rows, columns = acc.shape
    rows = rows // 2
    piece_rows = pieces[0].shape[1]
    tiles = piece_rows // tile
    width = outs[0].shape[1]
    cycles = outer * INNER
    k_local = width // slots
    pitch = pitch_of(width)

    m_values = [jnp.max(info[slot : slot + 1, :]).astype(jnp.int32) for slot in range(slots)]

    def finish(slot):
        for k in range(k_local):
            span = slice(k * cycles, (k + 1) * cycles)
            total = acc[slot, span] + turn_by_i(acc[slot, rows + k * cycles : rows + (k + 1) * cycles])
            for lane in range(columns // LANES):
                turned[lane, pl.ds(slot * k_local + k, cycles, stride=pitch), :] = total[:, lane * LANES : (lane + 1) * LANES]

    for slot in range(slots):
        for distance in range(1, ways):
            beside = slot > 0 and distance == ways - 1
            missing = first_tile(m_values[slot], owner_of(distance, ways), piece_rows, tile)
            for skipped in range(tiles + (1 if beside else 0)):

                @pl.when(missing == skipped)
                def _():
                    span = slice(skipped * tile, piece_rows)
                    if skipped < tiles:
                        acc[slot] += jnp.dot(
                            factors[distance - 1, slot, :, span],
                            pieces[distance - 1][slot, span],
                            preferred_element_type=jnp.float32,
                        )
                    if beside:
                        finish(slot - 1)

    finish(slots - 1)
    me = lax.axis_index("blk")
    for first in range(INNER):
        for second in range(outer):
            start = (me ^ distance_of(first, second, outer)) * pitch
            for lane in range(columns // LANES):
                block = turned[lane, pl.ds(start, width), :].astype(jnp.bfloat16)
                outs[first][second, :, lane * LANES : (lane + 1) * LANES] = block


def far_first(arrays):
    return [arrays[0], *reversed(arrays[1:])]


def regroup_kernel(outer, *refs):
    arrived, onward = far_first(refs[:INNER]), refs[INNER:]
    for second in range(outer):
        for first in range(INNER):
            onward[second][first] = arrived[first][second]
            if second == 1:
                onward[outer][first] = arrived[first][second]


def place_kernel(outer, *refs):
    here, low, *others, high = refs[: outer + 1]
    out, turned, staged, sem = refs[outer + 1 :]
    arrived = far_first([here, *others, high])
    k_local, slot_count, columns = staged.shape
    width = arrived[0].shape[1]
    slots = width // k_local
    pitch = pitch_of(slot_count)
    me = lax.axis_index("blk")
    in_low = jnp.logical_or(crossed(lax.axis_index("beamk"), outer) == 1, me < outer // 2 * INNER)
    for lane in range(columns // LANES):
        span = slice(lane * LANES, (lane + 1) * LANES)
        for second in range(outer):
            for first in range(INNER):
                block = arrived[second][first, :, span].astype(jnp.float32)
                if second == 1:
                    block = jnp.where(in_low, low[first, :, span].astype(jnp.float32), block)
                source = me ^ distance_of(first, second, outer)
                for slot in range(slots):
                    turned[lane, pl.ds(slots * source + slot, k_local, stride=pitch), :] = block[slot * k_local : (slot + 1) * k_local]
    copies = []
    step = -(-k_local // 4)
    for number, start in enumerate(range(0, k_local, step)):
        end = min(start + step, k_local)
        for k in range(start, end):
            for lane in range(columns // LANES):
                values = turned[lane, k * pitch : k * pitch + slot_count]
                staged[k, :, lane * LANES : (lane + 1) * LANES] = values.astype(staged.dtype)
        copies.append(pltpu.make_async_copy(staged.at[start:end], out.at[start:end], sem.at[number]))
        copies[-1].start()
    for copy in copies:
        copy.wait()


def local(sky, beam, wigner, m_list, *, ways, peers):
    slots, piece_rows, columns = sky.shape
    _, k_local, cycles, degrees = wigner.shape
    rows = k_local * cycles
    tile = tile_of(piece_rows)
    tiles = piece_rows // tile
    lane_tiles = columns // LANES
    width = slots * k_local
    params = pltpu.CompilerParams(vmem_limit_bytes=VMEM_LIMIT)

    pieces = []
    for shift in range(1, ways):
        perm = [(c, (c + shift) % ways) for c in range(ways)]
        pieces.append(pltpu.with_memory_space_constraint(lax.ppermute(sky, "beamk", perm), pltpu.VMEM))
    sky, beam, wigner, m_list = (pltpu.with_memory_space_constraint(x, pltpu.HBM) for x in (sky, beam, wigner, m_list))

    part, factors, info = pl.pallas_call(
        functools.partial(first_kernel, ways, tile),
        out_shape=(
            pltpu.VMEM((slots, 2 * rows, columns), jnp.float32),
            pltpu.VMEM((ways - 1, slots, 2 * rows, piece_rows), jnp.bfloat16),
            pltpu.VMEM((8, LANES), jnp.float32),
        ),
        in_specs=[whole(pltpu.HBM)] * 4,
        out_specs=(whole(pltpu.VMEM),) * 3,
        scratch_shapes=[
            pltpu.SMEM(m_list.shape, jnp.int32),
            pltpu.VMEM((slots, piece_rows, columns), jnp.bfloat16),
            pltpu.VMEM(wigner.shape, jnp.bfloat16),
            pltpu.VMEM((2, k_local, degrees + slots * tile), jnp.float32),
            pltpu.VMEM((2 * rows, piece_rows), jnp.bfloat16),
            pltpu.SemaphoreType.DMA,
            pltpu.SemaphoreType.DMA((slots, tiles)),
            pltpu.SemaphoreType.DMA((slots, tiles)),
            pltpu.SemaphoreType.DMA((ways - 1, slots)),
            pltpu.SemaphoreType.DMA((ways, 2)),
        ],
        compiler_params=params,
        cost_estimate=pl.CostEstimate(
            flops=4 * slots * rows * piece_rows * columns, bytes_accessed=8 * 1024 * 1024, transcendentals=0
        ),
        name="own_half",
    )(m_list, sky, wigner, beam)

    outer = peers // INNER

    def blocks(number):
        return pltpu.VMEM((number, width, columns), jnp.bfloat16)

    *sends, _ = pl.pallas_call(
        functools.partial(second_kernel, ways, outer, tile),
        out_shape=[blocks(outer)] * INNER + [pltpu.VMEM(part.shape, part.dtype)],
        in_specs=[whole(pltpu.VMEM)] * (ways + 2),
        out_specs=[whole(pltpu.VMEM)] * (INNER + 1),
        input_output_aliases={1: INNER},
        scratch_shapes=[
            turning(lane_tiles, cycles, width),
        ],
        compiler_params=params,
        cost_estimate=pl.CostEstimate(
            flops=4 * slots * rows * piece_rows * columns, bytes_accessed=8 * 1024 * 1024, transcendentals=0
        ),
        name="other_half",
    )(info, part, factors, *pieces)

    def send(array, number, step, low=None):
        perm = []
        for b in range(peers):
            for core in range(ways):
                over_outer = (step == 0) == bool(crossed(core, outer))
                if low is None or low == (not over_outer or b < outer // 2 * INNER):
                    perm.append((b * ways + core, (b ^ (number * INNER if over_outer else number)) * ways + core))
        return pltpu.with_memory_space_constraint(lax.ppermute(array, ("blk", "beamk"), perm), pltpu.VMEM)

    first = list(sends)
    for number in range(1, INNER):
        first[number] = send(first[number], number, 0)
    second = list(
        pl.pallas_call(
            functools.partial(regroup_kernel, outer),
            out_shape=[blocks(INNER)] * (outer + 1),
            in_specs=[whole(pltpu.VMEM)] * INNER,
            out_specs=[whole(pltpu.VMEM)] * (outer + 1),
            compiler_params=params,
            name="regroup",
        )(*far_first(first))
    )
    low = send(second.pop(), 1, 1, True)
    second[1] = send(second[1], 1, 1, False)
    for number in range(2, outer):
        second[number] = send(second[number], number, 1)
    here, *others = far_first(second)
    slot_count = slots * peers
    out = pl.pallas_call(
        functools.partial(place_kernel, outer),
        out_shape=pltpu.HBM((k_local, slot_count, columns), jnp.bfloat16),
        in_specs=[whole(pltpu.VMEM)] * (outer + 1),
        out_specs=whole(pltpu.HBM),
        scratch_shapes=[
            turning(lane_tiles, k_local, slot_count),
            pltpu.VMEM((k_local, slot_count, columns), jnp.bfloat16),
            pltpu.SemaphoreType.DMA((4,)),
        ],
        compiler_params=params,
        name="place",
    )(here, low, *others)
    return out.transpose(1, 0, 2)[None]


def solution(mesh):
    in_specs = (
        P("blk", "beamk", None),
        P("beamk", None, None),
        P("blk", "beamk", None, None),
        P("blk"),
    )
    out_specs = P("blk", None, "beamk", None)
    body = functools.partial(local, ways=mesh.shape["beamk"], peers=mesh.shape["blk"])
    return jax.shard_map(body, mesh=mesh, in_specs=in_specs, out_specs=out_specs, check_vma=False)
```

```python
import functools

import jax
import jax.numpy as jnp
from jax import lax
from jax.experimental import pallas as pl
from jax.experimental.pallas import tpu as pltpu
from jax.sharding import PartitionSpec as P

KB = 40
LANES = 128
INNER = 4
VMEM_LIMIT = 24 * 1024 * 1024


def tile_of(rows):
    return max(t for t in range(LANES, min(rows, 512) + 1, LANES) if rows % t == 0)


def pitch_of(rows):
    return rows + 1 - rows % 2


def turning(lane_tiles, groups, rows):
    return pltpu.VMEM((lane_tiles, -(-groups // 8) * 8 * pitch_of(rows) + 8, LANES), jnp.float32)


def whole(memory):
    return pl.BlockSpec(memory_space=memory)


def turn_by_i(rows):
    half = rows.shape[1] // 2
    swapped = pltpu.roll(rows, half, 1)
    column = lax.broadcasted_iota(jnp.int32, swapped.shape, 1)
    return jnp.where(column < half, -swapped, swapped)


def owner_of(distance, ways):
    return lax.rem(lax.axis_index("beamk") - distance + ways, ways)


def first_tile(m_value, owner, piece_rows, tile):
    return jnp.minimum(jnp.maximum(m_value - owner * piece_rows, 0) // tile, piece_rows // tile)


def first_kernel(
    ways, tile, m_list, sky, wigner, beam, part, factors, info, m_ref, sky_in, wigner_in, beam_in, own, m_sem, sky_sem, wigner_sem, distant_sem, beam_sem
):
    slots, piece_rows, columns = sky.shape
    k_local, cycles = wigner.shape[1], wigner.shape[2]
    rows = k_local * cycles
    tiles = piece_rows // tile
    all_tiles = ways * tiles
    first_k = lax.axis_index("beamk") * k_local - KB // 2
    last = tiles - 1

    def m_copy():
        return pltpu.make_async_copy(m_list, m_ref, m_sem)

    def beam_copy(distance, half):
        span = pl.ds(pl.multiple_of(owner_of(distance, ways) * piece_rows, tile), piece_rows)
        return pltpu.make_async_copy(beam.at[:, half, span], beam_in.at[half, :, span], beam_sem.at[distance, half])

    def sky_copy(slot, step):
        span = pl.ds(pl.multiple_of(step * tile, tile), tile)
        return pltpu.make_async_copy(sky.at[slot, span], sky_in.at[slot, span], sky_sem.at[slot, step])

    def wigner_copy(slot, step):
        start = pl.multiple_of(owner_of(0, ways) * piece_rows + step * tile, tile)
        span = pl.ds(start, tile)
        return pltpu.make_async_copy(wigner.at[slot, :, :, span], wigner_in.at[slot, :, :, span], wigner_sem.at[slot, step])

    def distant_copy(distance, slot):
        span = pl.ds(pl.multiple_of(owner_of(distance, ways) * piece_rows, tile), piece_rows)
        return pltpu.make_async_copy(wigner.at[slot, :, :, span], wigner_in.at[slot, :, :, span], distant_sem.at[distance - 1, slot])

    def begin(distance, slot):
        return first_tile(m_ref[slot], owner_of(distance, ways), piece_rows, tile)

    def fill(target, distance, slot, step):
        index = owner_of(distance, ways) * tiles + step
        rows_of = pl.ds(pl.multiple_of(index * tile, tile), tile)
        index = jnp.where(index == m_ref[slot] // tile, all_tiles + slot, index)
        span = pl.ds(pl.multiple_of(index * tile, tile), tile)
        for k in range(k_local):
            values = wigner_in[slot, k, :, rows_of]
            for half in range(2):
                factor = jnp.broadcast_to(beam_in[half, k : k + 1, span], (cycles, tile)).astype(jnp.bfloat16)
                target[half * rows + k * cycles : half * rows + (k + 1) * cycles, :] = values * factor

    def cut(slot):
        index = m_ref[slot] // tile
        degrees = index * tile + lax.broadcasted_iota(jnp.int32, (k_local, tile), 1)
        k_values = first_k + lax.broadcasted_iota(jnp.int32, (k_local, tile), 0)
        inside = degrees >= jnp.maximum(m_ref[slot], jnp.abs(k_values))
        span = pl.ds(pl.multiple_of(index * tile, tile), tile)
        for half in range(2):
            beam_in[half, :, (all_tiles + slot) * tile : (all_tiles + slot + 1) * tile] = jnp.where(inside, beam_in[half, :, span], 0.0)

    def cut_in(distance, slot):
        return m_ref[slot] // piece_rows == owner_of(distance, ways)

    def upper(distance):
        return 2 * (owner_of(distance, ways) + 1) > ways

    def where_needed(distance, slot, do):
        if slot % 2 == 0:
            do()
        else:
            pl.when(upper(distance))(do)

    m_copy().start()
    for slot in range(slots):

        def fetch(slot=slot):
            for step in reversed(range(tiles)):
                wigner_copy(slot, step).start()
                if slot == 0 and step == last:
                    for half in range(2):
                        beam_copy(0, half).start()
                sky_copy(slot, step).start()

        where_needed(0, slot, fetch)
    for distance in range(1, ways):
        for half in range(2):
            beam_copy(distance, half).start()
        for slot in range(slots):
            where_needed(distance, slot, lambda distance=distance, slot=slot: distant_copy(distance, slot).start())
    m_copy().wait()
    for slot in range(slots):
        info[slot : slot + 1, :] = jnp.full((1, LANES), m_ref[slot].astype(jnp.float32))
    def beam_arrives(distance):
        for half in range(2):
            beam_copy(distance, half).wait()
        for slot in range(slots):
            pl.when(cut_in(distance, slot))(functools.partial(cut, slot))

    beam_arrives(0)

    @pl.loop(0, slots)
    def _(slot):
        begins = begin(0, slot)

        @pl.loop(begins, tiles)
        def _(later):
            step = tiles - 1 - later + begins
            wigner_copy(slot, step).wait()
            span = pl.ds(pl.multiple_of(step * tile, tile), tile)
            fill(own.at[:, span], 0, slot, step)
            sky_copy(slot, step).wait()

        for skipped in range(tiles):

            @pl.when(begins == skipped)
            def _():
                span = slice(skipped * tile, piece_rows)
                part[slot] = jnp.dot(own[:, span], sky_in[slot, span], preferred_element_type=jnp.float32)

        @pl.when(begins == tiles)
        def _():
            part[slot] = jnp.zeros(part.shape[1:], part.dtype)

    for distance in range(1, ways):
        beam_arrives(distance)
        for slot in range(slots):
            where_needed(distance, slot, lambda distance=distance, slot=slot: distant_copy(distance, slot).wait())

        @pl.loop(0, slots)
        def _(slot):
            @pl.loop(begin(distance, slot), tiles)
            def _(step):
                span = pl.ds(pl.multiple_of(step * tile, tile), tile)
                fill(factors.at[distance - 1, slot, :, span], distance, slot, step)

    for slot in range(slots):

        def drop(slot=slot):
            @pl.loop(0, begin(0, slot))
            def _(step):
                wigner_copy(slot, step).wait()
                sky_copy(slot, step).wait()

        where_needed(0, slot, drop)


def crossed(core, outer):
    return (core % 2) * (outer == INNER)


def distance_of(first, second, outer):
    straight = second * INNER + first
    return jnp.where(crossed(lax.axis_index("beamk"), outer) == 1, first * INNER + second, straight)


def second_kernel(ways, outer, tile, info, _, factors, *refs):
    pieces, refs = refs[: ways - 1], refs[ways - 1 :]
    outs, (acc, turned) = refs[:INNER], refs[INNER:]
    slots, rows, columns = acc.shape
    rows = rows // 2
    piece_rows = pieces[0].shape[1]
    tiles = piece_rows // tile
    width = outs[0].shape[1]
    cycles = outer * INNER
    k_local = width // slots
    pitch = pitch_of(width)

    m_values = [jnp.max(info[slot : slot + 1, :]).astype(jnp.int32) for slot in range(slots)]

    def finish(slot):
        for k in range(k_local):
            span = slice(k * cycles, (k + 1) * cycles)
            total = acc[slot, span] + turn_by_i(acc[slot, rows + k * cycles : rows + (k + 1) * cycles])
            for lane in range(columns // LANES):
                turned[lane, pl.ds(slot * k_local + k, cycles, stride=pitch), :] = total[:, lane * LANES : (lane + 1) * LANES]

    for slot in range(slots):
        for distance in range(1, ways):
            beside = slot > 0 and distance == ways - 1
            missing = first_tile(m_values[slot], owner_of(distance, ways), piece_rows, tile)
            for skipped in range(tiles + (1 if beside else 0)):

                @pl.when(missing == skipped)
                def _():
                    span = slice(skipped * tile, piece_rows)
                    if skipped < tiles:
                        acc[slot] += jnp.dot(
                            factors[distance - 1, slot, :, span],
                            pieces[distance - 1][slot, span],
                            preferred_element_type=jnp.float32,
                        )
                    if beside:
                        finish(slot - 1)

    finish(slots - 1)
    me = lax.axis_index("blk")
    for first in range(INNER):
        for second in range(outer):
            start = (me ^ distance_of(first, second, outer)) * pitch
            for lane in range(columns // LANES):
                block = turned[lane, pl.ds(start, width), :].astype(jnp.bfloat16)
                outs[first][second, :, lane * LANES : (lane + 1) * LANES] = block


def far_first(arrays):
    return [arrays[0], *reversed(arrays[1:])]


def middle_first(arrays):
    half = len(arrays) // 2
    return [arrays[0], arrays[half], *arrays[2:half], arrays[1], *arrays[half + 1 :]]


def regroup_kernel(outer, *refs):
    arrived, onward = far_first(refs[:INNER]), refs[INNER:]
    for second in range(outer):
        for first in range(INNER):
            onward[second][first] = arrived[first][second]


def place_kernel(outer, *refs):
    arrived, (out, turned, staged, sem) = middle_first(refs[:outer]), refs[outer:]
    k_local, slot_count, columns = staged.shape
    width = arrived[0].shape[1]
    slots = width // k_local
    pitch = pitch_of(slot_count)
    me = lax.axis_index("blk")
    for lane in range(columns // LANES):
        span = slice(lane * LANES, (lane + 1) * LANES)
        for second in range(outer):
            for first in range(INNER):
                block = arrived[second][first, :, span].astype(jnp.float32)
                source = me ^ distance_of(first, second, outer)
                for slot in range(slots):
                    turned[lane, pl.ds(slots * source + slot, k_local, stride=pitch), :] = block[slot * k_local : (slot + 1) * k_local]
    copies = []
    step = -(-k_local // 4)
    for number, start in enumerate(range(0, k_local, step)):
        end = min(start + step, k_local)
        for k in range(start, end):
            for lane in range(columns // LANES):
                values = turned[lane, k * pitch : k * pitch + slot_count]
                staged[k, :, lane * LANES : (lane + 1) * LANES] = values.astype(staged.dtype)
        copies.append(pltpu.make_async_copy(staged.at[start:end], out.at[start:end], sem.at[number]))
        copies[-1].start()
    for copy in copies:
        copy.wait()


def local(sky, beam, wigner, m_list, *, ways, peers):
    slots, piece_rows, columns = sky.shape
    _, k_local, cycles, degrees = wigner.shape
    rows = k_local * cycles
    tile = tile_of(piece_rows)
    tiles = piece_rows // tile
    lane_tiles = columns // LANES
    width = slots * k_local
    params = pltpu.CompilerParams(vmem_limit_bytes=VMEM_LIMIT)

    pieces = []
    for shift in range(1, ways):
        perm = [(c, (c + shift) % ways) for c in range(ways)]
        pieces.append(pltpu.with_memory_space_constraint(lax.ppermute(sky, "beamk", perm), pltpu.VMEM))
    sky, beam, wigner, m_list = (pltpu.with_memory_space_constraint(x, pltpu.HBM) for x in (sky, beam, wigner, m_list))

    part, factors, info = pl.pallas_call(
        functools.partial(first_kernel, ways, tile),
        out_shape=(
            pltpu.VMEM((slots, 2 * rows, columns), jnp.float32),
            pltpu.VMEM((ways - 1, slots, 2 * rows, piece_rows), jnp.bfloat16),
            pltpu.VMEM((8, LANES), jnp.float32),
        ),
        in_specs=[whole(pltpu.HBM)] * 4,
        out_specs=(whole(pltpu.VMEM),) * 3,
        scratch_shapes=[
            pltpu.SMEM(m_list.shape, jnp.int32),
            pltpu.VMEM((slots, piece_rows, columns), jnp.bfloat16),
            pltpu.VMEM(wigner.shape, jnp.bfloat16),
            pltpu.VMEM((2, k_local, degrees + slots * tile), jnp.float32),
            pltpu.VMEM((2 * rows, piece_rows), jnp.bfloat16),
            pltpu.SemaphoreType.DMA,
            pltpu.SemaphoreType.DMA((slots, tiles)),
            pltpu.SemaphoreType.DMA((slots, tiles)),
            pltpu.SemaphoreType.DMA((ways - 1, slots)),
            pltpu.SemaphoreType.DMA((ways, 2)),
        ],
        compiler_params=params,
        cost_estimate=pl.CostEstimate(
            flops=4 * slots * rows * piece_rows * columns, bytes_accessed=8 * 1024 * 1024, transcendentals=0
        ),
        name="own_half",
    )(m_list, sky, wigner, beam)

    outer = peers // INNER

    def blocks(number):
        return pltpu.VMEM((number, width, columns), jnp.bfloat16)

    *sends, _ = pl.pallas_call(
        functools.partial(second_kernel, ways, outer, tile),
        out_shape=[blocks(outer)] * INNER + [pltpu.VMEM(part.shape, part.dtype)],
        in_specs=[whole(pltpu.VMEM)] * (ways + 2),
        out_specs=[whole(pltpu.VMEM)] * (INNER + 1),
        input_output_aliases={1: INNER},
        scratch_shapes=[
            turning(lane_tiles, cycles, width),
        ],
        compiler_params=params,
        cost_estimate=pl.CostEstimate(
            flops=4 * slots * rows * piece_rows * columns, bytes_accessed=8 * 1024 * 1024, transcendentals=0
        ),
        name="other_half",
    )(info, part, factors, *pieces)

    def send(array, number, step):
        perm = []
        for b in range(peers):
            for core in range(ways):
                over_outer = (step == 0) == bool(crossed(core, outer))
                perm.append((b * ways + core, (b ^ (number * INNER if over_outer else number)) * ways + core))
        return pltpu.with_memory_space_constraint(lax.ppermute(array, ("blk", "beamk"), perm), pltpu.VMEM)

    first = list(sends)
    for number in range(1, INNER):
        first[number] = send(first[number], number, 0)
    second = list(
        pl.pallas_call(
            functools.partial(regroup_kernel, outer),
            out_shape=[blocks(INNER)] * outer,
            in_specs=[whole(pltpu.VMEM)] * INNER,
            out_specs=[whole(pltpu.VMEM)] * outer,
            compiler_params=params,
            name="regroup",
        )(*far_first(first))
    )
    for number in range(1, outer):
        second[number] = send(second[number], number, 1)
    slot_count = slots * peers
    out = pl.pallas_call(
        functools.partial(place_kernel, outer),
        out_shape=pltpu.HBM((k_local, slot_count, columns), jnp.bfloat16),
        in_specs=[whole(pltpu.VMEM)] * outer,
        out_specs=whole(pltpu.HBM),
        scratch_shapes=[
            turning(lane_tiles, k_local, slot_count),
            pltpu.VMEM((k_local, slot_count, columns), jnp.bfloat16),
            pltpu.SemaphoreType.DMA((4,)),
        ],
        compiler_params=params,
        name="place",
    )(*middle_first(second))
    return out.transpose(1, 0, 2)[None]


def solution(mesh):
    in_specs = (
        P("blk", "beamk", None),
        P("beamk", None, None),
        P("blk", "beamk", None, None),
        P("blk"),
    )
    out_specs = P("blk", None, "beamk", None)
    body = functools.partial(local, ways=mesh.shape["beamk"], peers=mesh.shape["blk"])
    return jax.shard_map(body, mesh=mesh, in_specs=in_specs, out_specs=out_specs, check_vma=False)
```

```python
import functools

import jax
import jax.numpy as jnp
from jax import lax
from jax.experimental import pallas as pl
from jax.experimental.pallas import tpu as pltpu
from jax.sharding import PartitionSpec as P

KB = 40
LANES = 128
INNER = 4
VMEM_LIMIT = 24 * 1024 * 1024


def tile_of(rows):
    return max(t for t in range(LANES, min(rows, 512) + 1, LANES) if rows % t == 0)


def pitch_of(rows):
    return rows + 1 - rows % 2


def turning(lane_tiles, groups, rows):
    return pltpu.VMEM((lane_tiles, -(-groups // 8) * 8 * pitch_of(rows) + 8, LANES), jnp.float32)


def whole(memory):
    return pl.BlockSpec(memory_space=memory)


def turn_by_i(rows):
    half = rows.shape[1] // 2
    swapped = pltpu.roll(rows, half, 1)
    column = lax.broadcasted_iota(jnp.int32, swapped.shape, 1)
    return jnp.where(column < half, -swapped, swapped)


def owner_of(distance, ways):
    return lax.rem(lax.axis_index("beamk") - distance + ways, ways)


def first_tile(m_value, owner, piece_rows, tile):
    return jnp.minimum(jnp.maximum(m_value - owner * piece_rows, 0) // tile, piece_rows // tile)


def first_kernel(
    ways, tile, m_list, sky, wigner, beam, part, factors, info, m_ref, sky_in, wigner_in, beam_in, own, m_sem, sky_sem, wigner_sem, distant_sem, beam_sem
):
    slots, piece_rows, columns = sky.shape
    k_local, cycles = wigner.shape[1], wigner.shape[2]
    rows = k_local * cycles
    tiles = piece_rows // tile
    all_tiles = ways * tiles
    first_k = lax.axis_index("beamk") * k_local - KB // 2
    last = tiles - 1

    def m_copy():
        return pltpu.make_async_copy(m_list, m_ref, m_sem)

    def beam_copy(distance, half):
        span = pl.ds(pl.multiple_of(owner_of(distance, ways) * piece_rows, tile), piece_rows)
        return pltpu.make_async_copy(beam.at[:, half, span], beam_in.at[half, :, span], beam_sem.at[distance, half])

    def sky_copy(slot, step):
        span = pl.ds(pl.multiple_of(step * tile, tile), tile)
        return pltpu.make_async_copy(sky.at[slot, span], sky_in.at[slot, span], sky_sem.at[slot, step])

    def wigner_copy(slot, step):
        start = pl.multiple_of(owner_of(0, ways) * piece_rows + step * tile, tile)
        span = pl.ds(start, tile)
        return pltpu.make_async_copy(wigner.at[slot, :, :, span], wigner_in.at[slot, :, :, span], wigner_sem.at[slot, step])

    def distant_copy(distance, slot):
        span = pl.ds(pl.multiple_of(owner_of(distance, ways) * piece_rows, tile), piece_rows)
        return pltpu.make_async_copy(wigner.at[slot, :, :, span], wigner_in.at[slot, :, :, span], distant_sem.at[distance - 1, slot])

    def begin(distance, slot):
        return first_tile(m_ref[slot], owner_of(distance, ways), piece_rows, tile)

    def fill(target, distance, slot, step):
        index = owner_of(distance, ways) * tiles + step
        rows_of = pl.ds(pl.multiple_of(index * tile, tile), tile)
        index = jnp.where(index == m_ref[slot] // tile, all_tiles + slot, index)
        span = pl.ds(pl.multiple_of(index * tile, tile), tile)
        for k in range(k_local):
            values = wigner_in[slot, k, :, rows_of]
            for half in range(2):
                factor = jnp.broadcast_to(beam_in[half, k : k + 1, span], (cycles, tile)).astype(jnp.bfloat16)
                target[half * rows + k * cycles : half * rows + (k + 1) * cycles, :] = values * factor

    def cut(slot):
        index = m_ref[slot] // tile
        degrees = index * tile + lax.broadcasted_iota(jnp.int32, (k_local, tile), 1)
        k_values = first_k + lax.broadcasted_iota(jnp.int32, (k_local, tile), 0)
        inside = degrees >= jnp.maximum(m_ref[slot], jnp.abs(k_values))
        span = pl.ds(pl.multiple_of(index * tile, tile), tile)
        for half in range(2):
            beam_in[half, :, (all_tiles + slot) * tile : (all_tiles + slot + 1) * tile] = jnp.where(inside, beam_in[half, :, span], 0.0)

    def cut_in(distance, slot):
        return m_ref[slot] // piece_rows == owner_of(distance, ways)

    def upper(distance):
        return 2 * (owner_of(distance, ways) + 1) > ways

    def where_needed(distance, slot, do):
        if slot % 2 == 0:
            do()
        else:
            pl.when(upper(distance))(do)

    m_copy().start()
    for slot in range(slots):

        def fetch(slot=slot):
            for step in reversed(range(tiles)):
                wigner_copy(slot, step).start()
                if slot == 0 and step == last:
                    for half in range(2):
                        beam_copy(0, half).start()
                sky_copy(slot, step).start()

        where_needed(0, slot, fetch)
    for distance in range(1, ways):
        for half in range(2):
            beam_copy(distance, half).start()
        for slot in range(slots):
            where_needed(distance, slot, lambda distance=distance, slot=slot: distant_copy(distance, slot).start())
    m_copy().wait()
    for slot in range(slots):
        info[slot : slot + 1, :] = jnp.full((1, LANES), m_ref[slot].astype(jnp.float32))
    def beam_arrives(distance):
        for half in range(2):
            beam_copy(distance, half).wait()
        for slot in range(slots):
            pl.when(cut_in(distance, slot))(functools.partial(cut, slot))

    beam_arrives(0)

    @pl.loop(0, slots)
    def _(slot):
        begins = begin(0, slot)

        @pl.loop(begins, tiles)
        def _(later):
            step = tiles - 1 - later + begins
            wigner_copy(slot, step).wait()
            span = pl.ds(pl.multiple_of(step * tile, tile), tile)
            fill(own.at[:, span], 0, slot, step)
            sky_copy(slot, step).wait()

        for skipped in range(tiles):

            @pl.when(begins == skipped)
            def _():
                span = slice(skipped * tile, piece_rows)
                part[slot] = jnp.dot(own[:, span], sky_in[slot, span], preferred_element_type=jnp.float32)

        @pl.when(begins == tiles)
        def _():
            part[slot] = jnp.zeros(part.shape[1:], part.dtype)

    for distance in range(1, ways):
        beam_arrives(distance)
        for slot in range(slots):
            where_needed(distance, slot, lambda distance=distance, slot=slot: distant_copy(distance, slot).wait())

        @pl.loop(0, slots)
        def _(slot):
            @pl.loop(begin(distance, slot), tiles)
            def _(step):
                span = pl.ds(pl.multiple_of(step * tile, tile), tile)
                fill(factors.at[distance - 1, slot, :, span], distance, slot, step)

    for slot in range(slots):

        def drop(slot=slot):
            @pl.loop(0, begin(0, slot))
            def _(step):
                wigner_copy(slot, step).wait()
                sky_copy(slot, step).wait()

        where_needed(0, slot, drop)


def crossed(core, outer):
    return (core % 2) * (outer == INNER)


def distance_of(first, second, outer):
    straight = second * INNER + first
    return jnp.where(crossed(lax.axis_index("beamk"), outer) == 1, first * INNER + second, straight)


def second_kernel(ways, outer, tile, info, _, factors, *refs):
    pieces, refs = refs[: ways - 1], refs[ways - 1 :]
    outs, (acc, turned) = refs[:INNER], refs[INNER:]
    slots, rows, columns = acc.shape
    rows = rows // 2
    piece_rows = pieces[0].shape[1]
    tiles = piece_rows // tile
    width = outs[0].shape[1]
    cycles = outer * INNER
    k_local = width // slots
    pitch = pitch_of(width)

    m_values = [jnp.max(info[slot : slot + 1, :]).astype(jnp.int32) for slot in range(slots)]

    def finish(slot):
        for k in range(k_local):
            span = slice(k * cycles, (k + 1) * cycles)
            total = acc[slot, span] + turn_by_i(acc[slot, rows + k * cycles : rows + (k + 1) * cycles])
            for lane in range(columns // LANES):
                turned[lane, pl.ds(slot * k_local + k, cycles, stride=pitch), :] = total[:, lane * LANES : (lane + 1) * LANES]

    for slot in range(slots):
        for distance in range(1, ways):
            beside = slot > 0 and distance == ways - 1
            missing = first_tile(m_values[slot], owner_of(distance, ways), piece_rows, tile)
            for skipped in range(tiles + (1 if beside else 0)):

                @pl.when(missing == skipped)
                def _():
                    span = slice(skipped * tile, piece_rows)
                    if skipped < tiles:
                        acc[slot] += jnp.dot(
                            factors[distance - 1, slot, :, span],
                            pieces[distance - 1][slot, span],
                            preferred_element_type=jnp.float32,
                        )
                    if beside:
                        finish(slot - 1)

    finish(slots - 1)
    me = lax.axis_index("blk")
    for first in range(INNER):
        for second in range(outer):
            start = (me ^ distance_of(first, second, outer)) * pitch
            for lane in range(columns // LANES):
                block = turned[lane, pl.ds(start, width), :].astype(jnp.bfloat16)
                outs[first][second, :, lane * LANES : (lane + 1) * LANES] = block


def far_first(arrays):
    return [arrays[0], *reversed(arrays[1:])]


def regroup_kernel(outer, *refs):
    arrived, onward = far_first(refs[:INNER]), refs[INNER:]
    for second in range(outer):
        for first in range(INNER):
            onward[second][first] = arrived[first][second]


def place_kernel(outer, *refs):
    arrived, (out, turned, staged, sem) = far_first(refs[:outer]), refs[outer:]
    k_local, slot_count, columns = staged.shape
    width = arrived[0].shape[1]
    slots = width // k_local
    pitch = pitch_of(slot_count)
    me = lax.axis_index("blk")
    origin = me // (outer * INNER)
    for lane in range(columns // LANES):
        span = slice(lane * LANES, (lane + 1) * LANES)
        for second in range(outer):
            for first in range(INNER):
                block = arrived[second][first, :, span].astype(jnp.float32)
                source = me ^ distance_of(first, second, outer)
                for slot in range(slots):
                    turned[lane, pl.ds(slots * source + slot, k_local, stride=pitch), :] = block[slot * k_local : (slot + 1) * k_local]
    copies = []
    step = -(-k_local // 4)
    for number, start in enumerate(range(0, k_local, step)):
        end = min(start + step, k_local)
        for k in range(start, end):
            for lane in range(columns // LANES):
                values = turned[lane, pl.ds(origin + k * pitch, slot_count)]
                staged[k, :, lane * LANES : (lane + 1) * LANES] = values.astype(staged.dtype)
        copies.append(pltpu.make_async_copy(staged.at[start:end], out.at[start:end], sem.at[number]))
        copies[-1].start()
    for copy in copies:
        copy.wait()


def local(sky, beam, wigner, m_list, *, ways, peers):
    slots, piece_rows, columns = sky.shape
    _, k_local, cycles, degrees = wigner.shape
    rows = k_local * cycles
    tile = tile_of(piece_rows)
    tiles = piece_rows // tile
    lane_tiles = columns // LANES
    width = slots * k_local
    params = pltpu.CompilerParams(vmem_limit_bytes=VMEM_LIMIT)

    pieces = []
    for shift in range(1, ways):
        perm = [(c, (c + shift) % ways) for c in range(ways)]
        pieces.append(pltpu.with_memory_space_constraint(lax.ppermute(sky, "beamk", perm), pltpu.VMEM))
    sky, beam, wigner, m_list = (pltpu.with_memory_space_constraint(x, pltpu.HBM) for x in (sky, beam, wigner, m_list))

    part, factors, info = pl.pallas_call(
        functools.partial(first_kernel, ways, tile),
        out_shape=(
            pltpu.VMEM((slots, 2 * rows, columns), jnp.float32),
            pltpu.VMEM((ways - 1, slots, 2 * rows, piece_rows), jnp.bfloat16),
            pltpu.VMEM((8, LANES), jnp.float32),
        ),
        in_specs=[whole(pltpu.HBM)] * 4,
        out_specs=(whole(pltpu.VMEM),) * 3,
        scratch_shapes=[
            pltpu.SMEM(m_list.shape, jnp.int32),
            pltpu.VMEM((slots, piece_rows, columns), jnp.bfloat16),
            pltpu.VMEM(wigner.shape, jnp.bfloat16),
            pltpu.VMEM((2, k_local, degrees + slots * tile), jnp.float32),
            pltpu.VMEM((2 * rows, piece_rows), jnp.bfloat16),
            pltpu.SemaphoreType.DMA,
            pltpu.SemaphoreType.DMA((slots, tiles)),
            pltpu.SemaphoreType.DMA((slots, tiles)),
            pltpu.SemaphoreType.DMA((ways - 1, slots)),
            pltpu.SemaphoreType.DMA((ways, 2)),
        ],
        compiler_params=params,
        cost_estimate=pl.CostEstimate(
            flops=4 * slots * rows * piece_rows * columns, bytes_accessed=8 * 1024 * 1024, transcendentals=0
        ),
        name="own_half",
    )(m_list, sky, wigner, beam)

    outer = peers // INNER

    def blocks(number):
        return pltpu.VMEM((number, width, columns), jnp.bfloat16)

    *sends, _ = pl.pallas_call(
        functools.partial(second_kernel, ways, outer, tile),
        out_shape=[blocks(outer)] * INNER + [pltpu.VMEM(part.shape, part.dtype)],
        in_specs=[whole(pltpu.VMEM)] * (ways + 2),
        out_specs=[whole(pltpu.VMEM)] * (INNER + 1),
        input_output_aliases={1: INNER},
        scratch_shapes=[
            turning(lane_tiles, cycles, width),
        ],
        compiler_params=params,
        cost_estimate=pl.CostEstimate(
            flops=4 * slots * rows * piece_rows * columns, bytes_accessed=8 * 1024 * 1024, transcendentals=0
        ),
        name="other_half",
    )(info, part, factors, *pieces)

    def send(array, number, step):
        perm = []
        for b in range(peers):
            for core in range(ways):
                over_outer = (step == 0) == bool(crossed(core, outer))
                perm.append((b * ways + core, (b ^ (number * INNER if over_outer else number)) * ways + core))
        return pltpu.with_memory_space_constraint(lax.ppermute(array, ("blk", "beamk"), perm), pltpu.VMEM)

    first = list(sends)
    for number in range(1, INNER):
        first[number] = send(first[number], number, 0)
    second = list(
        pl.pallas_call(
            functools.partial(regroup_kernel, outer),
            out_shape=[blocks(INNER)] * outer,
            in_specs=[whole(pltpu.VMEM)] * INNER,
            out_specs=[whole(pltpu.VMEM)] * outer,
            compiler_params=params,
            name="regroup",
        )(*far_first(first))
    )
    for number in range(1, outer):
        second[number] = send(second[number], number, 1)
    slot_count = slots * peers
    out = pl.pallas_call(
        functools.partial(place_kernel, outer),
        out_shape=pltpu.HBM((k_local, slot_count, columns), jnp.bfloat16),
        in_specs=[whole(pltpu.VMEM)] * outer,
        out_specs=whole(pltpu.HBM),
        scratch_shapes=[
            turning(lane_tiles, k_local, slot_count),
            pltpu.VMEM((k_local, slot_count, columns), jnp.bfloat16),
            pltpu.SemaphoreType.DMA((4,)),
        ],
        compiler_params=params,
        name="place",
    )(*far_first(second))
    return out.transpose(1, 0, 2)[None]


def solution(mesh):
    in_specs = (
        P("blk", "beamk", None),
        P("beamk", None, None),
        P("blk", "beamk", None, None),
        P("blk"),
    )
    out_specs = P("blk", None, "beamk", None)
    body = functools.partial(local, ways=mesh.shape["beamk"], peers=mesh.shape["blk"])
    return jax.shard_map(body, mesh=mesh, in_specs=in_specs, out_specs=out_specs, check_vma=False)
```

```python
import functools

import jax
import jax.numpy as jnp
from jax import lax
from jax.experimental import pallas as pl
from jax.experimental.pallas import tpu as pltpu
from jax.sharding import PartitionSpec as P

KB = 40
LANES = 128
INNER = 4
VMEM_LIMIT = 24 * 1024 * 1024


def tile_of(rows):
    return max(t for t in range(LANES, min(rows, 512) + 1, LANES) if rows % t == 0)


def pitch_of(rows):
    return rows + 1 - rows % 2


def turning(lane_tiles, groups, rows):
    return pltpu.VMEM((lane_tiles, -(-groups // 8) * 8 * pitch_of(rows) + 8, LANES), jnp.float32)


def whole(memory):
    return pl.BlockSpec(memory_space=memory)


def turn_by_i(rows):
    half = rows.shape[1] // 2
    swapped = pltpu.roll(rows, half, 1)
    column = lax.broadcasted_iota(jnp.int32, swapped.shape, 1)
    return jnp.where(column < half, -swapped, swapped)


def owner_of(distance, ways):
    return lax.rem(lax.axis_index("beamk") - distance + ways, ways)


def first_tile(m_value, owner, piece_rows, tile):
    return jnp.minimum(jnp.maximum(m_value - owner * piece_rows, 0) // tile, piece_rows // tile)


def first_kernel(
    ways, tile, m_list, sky, wigner, beam, part, factors, info, m_ref, sky_in, wigner_in, beam_in, own, m_sem, sky_sem, wigner_sem, distant_sem, beam_sem
):
    slots, piece_rows, columns = sky.shape
    k_local, cycles = wigner.shape[1], wigner.shape[2]
    rows = k_local * cycles
    tiles = piece_rows // tile
    all_tiles = ways * tiles
    first_k = lax.axis_index("beamk") * k_local - KB // 2
    last = tiles - 1

    def m_copy():
        return pltpu.make_async_copy(m_list, m_ref, m_sem)

    def beam_copy(distance, half):
        span = pl.ds(pl.multiple_of(owner_of(distance, ways) * piece_rows, tile), piece_rows)
        return pltpu.make_async_copy(beam.at[:, half, span], beam_in.at[half, :, span], beam_sem.at[distance, half])

    def sky_copy(slot, step):
        span = pl.ds(pl.multiple_of(step * tile, tile), tile)
        return pltpu.make_async_copy(sky.at[slot, span], sky_in.at[slot, span], sky_sem.at[slot, step])

    def wigner_copy(slot, step):
        start = pl.multiple_of(owner_of(0, ways) * piece_rows + step * tile, tile)
        span = pl.ds(start, tile)
        return pltpu.make_async_copy(wigner.at[slot, :, :, span], wigner_in.at[slot, :, :, span], wigner_sem.at[slot, step])

    def distant_copy(distance, slot):
        span = pl.ds(pl.multiple_of(owner_of(distance, ways) * piece_rows, tile), piece_rows)
        return pltpu.make_async_copy(wigner.at[slot, :, :, span], wigner_in.at[slot, :, :, span], distant_sem.at[distance - 1, slot])

    def begin(distance, slot):
        return first_tile(m_ref[slot], owner_of(distance, ways), piece_rows, tile)

    def fill(target, distance, slot, step):
        index = owner_of(distance, ways) * tiles + step
        rows_of = pl.ds(pl.multiple_of(index * tile, tile), tile)
        index = jnp.where(index == m_ref[slot] // tile, all_tiles + slot, index)
        span = pl.ds(pl.multiple_of(index * tile, tile), tile)
        for k in range(k_local):
            values = wigner_in[slot, k, :, rows_of]
            for half in range(2):
                factor = jnp.broadcast_to(beam_in[half, k : k + 1, span], (cycles, tile)).astype(jnp.bfloat16)
                target[half * rows + k * cycles : half * rows + (k + 1) * cycles, :] = values * factor

    def cut(slot):
        index = m_ref[slot] // tile
        degrees = index * tile + lax.broadcasted_iota(jnp.int32, (k_local, tile), 1)
        k_values = first_k + lax.broadcasted_iota(jnp.int32, (k_local, tile), 0)
        inside = degrees >= jnp.maximum(m_ref[slot], jnp.abs(k_values))
        span = pl.ds(pl.multiple_of(index * tile, tile), tile)
        for half in range(2):
            beam_in[half, :, (all_tiles + slot) * tile : (all_tiles + slot + 1) * tile] = jnp.where(inside, beam_in[half, :, span], 0.0)

    def cut_in(distance, slot):
        return m_ref[slot] // piece_rows == owner_of(distance, ways)

    def upper(distance):
        return 2 * (owner_of(distance, ways) + 1) > ways

    def where_needed(distance, slot, do):
        if slot % 2 == 0:
            do()
        else:
            pl.when(upper(distance))(do)

    m_copy().start()
    for slot in range(slots):

        def fetch(slot=slot):
            for step in reversed(range(tiles)):
                wigner_copy(slot, step).start()
                if slot == 0 and step == last:
                    for half in range(2):
                        beam_copy(0, half).start()
                sky_copy(slot, step).start()

        where_needed(0, slot, fetch)
    for distance in range(1, ways):
        for half in range(2):
            beam_copy(distance, half).start()
        for slot in range(slots):
            where_needed(distance, slot, lambda distance=distance, slot=slot: distant_copy(distance, slot).start())
    m_copy().wait()
    for slot in range(slots):
        info[slot : slot + 1, :] = jnp.full((1, LANES), m_ref[slot].astype(jnp.float32))
    def beam_arrives(distance):
        for half in range(2):
            beam_copy(distance, half).wait()
        for slot in range(slots):
            pl.when(cut_in(distance, slot))(functools.partial(cut, slot))

    beam_arrives(0)

    @pl.loop(0, slots)
    def _(slot):
        begins = begin(0, slot)

        @pl.loop(begins, tiles)
        def _(later):
            step = tiles - 1 - later + begins
            wigner_copy(slot, step).wait()
            span = pl.ds(pl.multiple_of(step * tile, tile), tile)
            fill(own.at[:, span], 0, slot, step)
            sky_copy(slot, step).wait()

        for skipped in range(tiles):

            @pl.when(begins == skipped)
            def _():
                span = slice(skipped * tile, piece_rows)
                part[slot] = jnp.dot(own[:, span], sky_in[slot, span], preferred_element_type=jnp.float32)

        @pl.when(begins == tiles)
        def _():
            part[slot] = jnp.zeros(part.shape[1:], part.dtype)

    for distance in range(1, ways):
        beam_arrives(distance)
        for slot in range(slots):
            where_needed(distance, slot, lambda distance=distance, slot=slot: distant_copy(distance, slot).wait())

        @pl.loop(0, slots)
        def _(slot):
            @pl.loop(begin(distance, slot), tiles)
            def _(step):
                span = pl.ds(pl.multiple_of(step * tile, tile), tile)
                fill(factors.at[distance - 1, slot, :, span], distance, slot, step)

    for slot in range(slots):

        def drop(slot=slot):
            @pl.loop(0, begin(0, slot))
            def _(step):
                wigner_copy(slot, step).wait()
                sky_copy(slot, step).wait()

        where_needed(0, slot, drop)


def crossed(core, outer):
    return (core % 2) * (outer == INNER)


def inner_distance(number):
    return (0, 3, 2, 1)[number]


def device_at(first, second, outer, sign):
    me = lax.axis_index("blk")

    def at(shift, distance):
        group = lax.rem(me // INNER + (sign * shift + outer), outer)
        return group * INNER + (me % INNER ^ distance)

    straight = at(second, inner_distance(first))
    if outer != INNER:
        return straight
    return jnp.where(crossed(lax.axis_index("beamk"), outer) == 1, at(first, inner_distance(second)), straight)


def second_kernel(ways, outer, tile, info, _, factors, *refs):
    pieces, refs = refs[: ways - 1], refs[ways - 1 :]
    outs, (acc, turned) = refs[:INNER], refs[INNER:]
    slots, rows, columns = acc.shape
    rows = rows // 2
    piece_rows = pieces[0].shape[1]
    tiles = piece_rows // tile
    width = outs[0].shape[1]
    cycles = outer * INNER
    k_local = width // slots
    pitch = pitch_of(width)

    m_values = [jnp.max(info[slot : slot + 1, :]).astype(jnp.int32) for slot in range(slots)]

    def finish(slot):
        for k in range(k_local):
            span = slice(k * cycles, (k + 1) * cycles)
            total = acc[slot, span] + turn_by_i(acc[slot, rows + k * cycles : rows + (k + 1) * cycles])
            for lane in range(columns // LANES):
                turned[lane, pl.ds(slot * k_local + k, cycles, stride=pitch), :] = total[:, lane * LANES : (lane + 1) * LANES]

    for slot in range(slots):
        for distance in range(1, ways):
            beside = slot > 0 and distance == ways - 1
            missing = first_tile(m_values[slot], owner_of(distance, ways), piece_rows, tile)
            for skipped in range(tiles + (1 if beside else 0)):

                @pl.when(missing == skipped)
                def _():
                    span = slice(skipped * tile, piece_rows)
                    if skipped < tiles:
                        acc[slot] += jnp.dot(
                            factors[distance - 1, slot, :, span],
                            pieces[distance - 1][slot, span],
                            preferred_element_type=jnp.float32,
                        )
                    if beside:
                        finish(slot - 1)

    finish(slots - 1)
    for first in range(INNER):
        for second in range(outer):
            start = device_at(first, second, outer, 1) * pitch
            for lane in range(columns // LANES):
                block = turned[lane, pl.ds(start, width), :].astype(jnp.bfloat16)
                outs[first][second, :, lane * LANES : (lane + 1) * LANES] = block


def regroup_kernel(outer, *refs):
    arrived, onward = refs[:INNER], refs[INNER:]
    for second in range(outer):
        for first in range(INNER):
            onward[second][first] = arrived[first][second]


def place_kernel(outer, *refs):
    arrived, (out, turned, staged, sem) = refs[:outer], refs[outer:]
    k_local, slot_count, columns = staged.shape
    width = arrived[0].shape[1]
    slots = width // k_local
    pitch = pitch_of(slot_count)
    for lane in range(columns // LANES):
        span = slice(lane * LANES, (lane + 1) * LANES)
        for second in range(outer):
            for first in range(INNER):
                block = arrived[second][first, :, span].astype(jnp.float32)
                source = device_at(first, second, outer, -1)
                for slot in range(slots):
                    turned[lane, pl.ds(slots * source + slot, k_local, stride=pitch), :] = block[slot * k_local : (slot + 1) * k_local]
    copies = []
    step = -(-k_local // 4)
    for number, start in enumerate(range(0, k_local, step)):
        end = min(start + step, k_local)
        for k in range(start, end):
            for lane in range(columns // LANES):
                values = turned[lane, k * pitch : k * pitch + slot_count]
                staged[k, :, lane * LANES : (lane + 1) * LANES] = values.astype(staged.dtype)
        copies.append(pltpu.make_async_copy(staged.at[start:end], out.at[start:end], sem.at[number]))
        copies[-1].start()
    for copy in copies:
        copy.wait()


def local(sky, beam, wigner, m_list, *, ways, peers):
    slots, piece_rows, columns = sky.shape
    _, k_local, cycles, degrees = wigner.shape
    rows = k_local * cycles
    tile = tile_of(piece_rows)
    tiles = piece_rows // tile
    lane_tiles = columns // LANES
    width = slots * k_local
    params = pltpu.CompilerParams(vmem_limit_bytes=VMEM_LIMIT)

    pieces = []
    for shift in range(1, ways):
        perm = [(c, (c + shift) % ways) for c in range(ways)]
        pieces.append(pltpu.with_memory_space_constraint(lax.ppermute(sky, "beamk", perm), pltpu.VMEM))
    sky, beam, wigner, m_list = (pltpu.with_memory_space_constraint(x, pltpu.HBM) for x in (sky, beam, wigner, m_list))

    part, factors, info = pl.pallas_call(
        functools.partial(first_kernel, ways, tile),
        out_shape=(
            pltpu.VMEM((slots, 2 * rows, columns), jnp.float32),
            pltpu.VMEM((ways - 1, slots, 2 * rows, piece_rows), jnp.bfloat16),
            pltpu.VMEM((8, LANES), jnp.float32),
        ),
        in_specs=[whole(pltpu.HBM)] * 4,
        out_specs=(whole(pltpu.VMEM),) * 3,
        scratch_shapes=[
            pltpu.SMEM(m_list.shape, jnp.int32),
            pltpu.VMEM((slots, piece_rows, columns), jnp.bfloat16),
            pltpu.VMEM(wigner.shape, jnp.bfloat16),
            pltpu.VMEM((2, k_local, degrees + slots * tile), jnp.float32),
            pltpu.VMEM((2 * rows, piece_rows), jnp.bfloat16),
            pltpu.SemaphoreType.DMA,
            pltpu.SemaphoreType.DMA((slots, tiles)),
            pltpu.SemaphoreType.DMA((slots, tiles)),
            pltpu.SemaphoreType.DMA((ways - 1, slots)),
            pltpu.SemaphoreType.DMA((ways, 2)),
        ],
        compiler_params=params,
        cost_estimate=pl.CostEstimate(
            flops=4 * slots * rows * piece_rows * columns, bytes_accessed=8 * 1024 * 1024, transcendentals=0
        ),
        name="own_half",
    )(m_list, sky, wigner, beam)

    outer = peers // INNER

    def blocks(number):
        return pltpu.VMEM((number, width, columns), jnp.bfloat16)

    *sends, _ = pl.pallas_call(
        functools.partial(second_kernel, ways, outer, tile),
        out_shape=[blocks(outer)] * INNER + [pltpu.VMEM(part.shape, part.dtype)],
        in_specs=[whole(pltpu.VMEM)] * (ways + 2),
        out_specs=[whole(pltpu.VMEM)] * (INNER + 1),
        input_output_aliases={1: INNER},
        scratch_shapes=[
            turning(lane_tiles, cycles, width),
        ],
        compiler_params=params,
        cost_estimate=pl.CostEstimate(
            flops=4 * slots * rows * piece_rows * columns, bytes_accessed=8 * 1024 * 1024, transcendentals=0
        ),
        name="other_half",
    )(info, part, factors, *pieces)

    def send(array, number, step):
        perm = []
        for b in range(peers):
            for core in range(ways):
                over_outer = (step == 0) == bool(crossed(core, outer))
                there = (b + number * INNER) % peers if over_outer else b ^ inner_distance(number)
                perm.append((b * ways + core, there * ways + core))
        return pltpu.with_memory_space_constraint(lax.ppermute(array, ("blk", "beamk"), perm), pltpu.VMEM)

    first = list(sends)
    for number in range(1, INNER):
        first[number] = send(first[number], number, 0)
    second = list(
        pl.pallas_call(
            functools.partial(regroup_kernel, outer),
            out_shape=[blocks(INNER)] * outer,
            in_specs=[whole(pltpu.VMEM)] * INNER,
            out_specs=[whole(pltpu.VMEM)] * outer,
            compiler_params=params,
            name="regroup",
        )(*first)
    )
    for number in range(1, outer):
        second[number] = send(second[number], number, 1)
    slot_count = slots * peers
    out = pl.pallas_call(
        functools.partial(place_kernel, outer),
        out_shape=pltpu.HBM((k_local, slot_count, columns), jnp.bfloat16),
        in_specs=[whole(pltpu.VMEM)] * outer,
        out_specs=whole(pltpu.HBM),
        scratch_shapes=[
            turning(lane_tiles, k_local, slot_count),
            pltpu.VMEM((k_local, slot_count, columns), jnp.bfloat16),
            pltpu.SemaphoreType.DMA((4,)),
        ],
        compiler_params=params,
        name="place",
    )(*second)
    return out.transpose(1, 0, 2)[None]


def solution(mesh):
    in_specs = (
        P("blk", "beamk", None),
        P("beamk", None, None),
        P("blk", "beamk", None, None),
        P("blk"),
    )
    out_specs = P("blk", None, "beamk", None)
    body = functools.partial(local, ways=mesh.shape["beamk"], peers=mesh.shape["blk"])
    return jax.shard_map(body, mesh=mesh, in_specs=in_specs, out_specs=out_specs, check_vma=False)
```

```python
import functools

import jax
import jax.numpy as jnp
from jax import lax
from jax.experimental import pallas as pl
from jax.experimental.pallas import tpu as pltpu
from jax.sharding import PartitionSpec as P

KB = 40
LANES = 128
INNER = 4
VMEM_LIMIT = 24 * 1024 * 1024


def tile_of(rows):
    return max(t for t in range(LANES, min(rows, 512) + 1, LANES) if rows % t == 0)


def pitch_of(rows):
    return rows + 1 - rows % 2


def turning(lane_tiles, groups, rows):
    return pltpu.VMEM((lane_tiles, -(-groups // 8) * 8 * pitch_of(rows) + 8, LANES), jnp.float32)


def whole(memory):
    return pl.BlockSpec(memory_space=memory)


def turn_by_i(rows):
    half = rows.shape[1] // 2
    swapped = pltpu.roll(rows, half, 1)
    column = lax.broadcasted_iota(jnp.int32, swapped.shape, 1)
    return jnp.where(column < half, -swapped, swapped)


def owner_of(distance, ways):
    return lax.rem(lax.axis_index("beamk") - distance + ways, ways)


def first_tile(m_value, owner, piece_rows, tile):
    return jnp.minimum(jnp.maximum(m_value - owner * piece_rows, 0) // tile, piece_rows // tile)


def first_kernel(
    ways, tile, m_list, sky, wigner, beam, part, factors, info, m_ref, sky_in, wigner_in, beam_in, own, m_sem, sky_sem, wigner_sem, distant_sem, beam_sem
):
    slots, piece_rows, columns = sky.shape
    k_local, cycles = wigner.shape[1], wigner.shape[2]
    rows = k_local * cycles
    tiles = piece_rows // tile
    all_tiles = ways * tiles
    first_k = lax.axis_index("beamk") * k_local - KB // 2
    last = tiles - 1

    def m_copy():
        return pltpu.make_async_copy(m_list, m_ref, m_sem)

    def beam_copy(distance, half):
        span = pl.ds(pl.multiple_of(owner_of(distance, ways) * piece_rows, tile), piece_rows)
        return pltpu.make_async_copy(beam.at[:, half, span], beam_in.at[half, :, span], beam_sem.at[distance, half])

    def sky_copy(slot, step):
        span = pl.ds(pl.multiple_of(step * tile, tile), tile)
        return pltpu.make_async_copy(sky.at[slot, span], sky_in.at[slot, span], sky_sem.at[slot, step])

    def wigner_copy(slot, step):
        start = pl.multiple_of(owner_of(0, ways) * piece_rows + step * tile, tile)
        span = pl.ds(start, tile)
        return pltpu.make_async_copy(wigner.at[slot, :, :, span], wigner_in.at[slot, :, :, span], wigner_sem.at[slot, step])

    def distant_copy(distance, slot):
        span = pl.ds(pl.multiple_of(owner_of(distance, ways) * piece_rows, tile), piece_rows)
        return pltpu.make_async_copy(wigner.at[slot, :, :, span], wigner_in.at[slot, :, :, span], distant_sem.at[distance - 1, slot])

    def begin(distance, slot):
        return first_tile(m_ref[slot], owner_of(distance, ways), piece_rows, tile)

    def fill(target, distance, slot, step):
        index = owner_of(distance, ways) * tiles + step
        rows_of = pl.ds(pl.multiple_of(index * tile, tile), tile)
        index = jnp.where(index == m_ref[slot] // tile, all_tiles + slot, index)
        span = pl.ds(pl.multiple_of(index * tile, tile), tile)
        for k in range(k_local):
            values = wigner_in[slot, k, :, rows_of]
            for half in range(2):
                factor = jnp.broadcast_to(beam_in[half, k : k + 1, span], (cycles, tile)).astype(jnp.bfloat16)
                target[half * rows + k * cycles : half * rows + (k + 1) * cycles, :] = values * factor

    def cut(slot):
        index = m_ref[slot] // tile
        degrees = index * tile + lax.broadcasted_iota(jnp.int32, (k_local, tile), 1)
        k_values = first_k + lax.broadcasted_iota(jnp.int32, (k_local, tile), 0)
        inside = degrees >= jnp.maximum(m_ref[slot], jnp.abs(k_values))
        span = pl.ds(pl.multiple_of(index * tile, tile), tile)
        for half in range(2):
            beam_in[half, :, (all_tiles + slot) * tile : (all_tiles + slot + 1) * tile] = jnp.where(inside, beam_in[half, :, span], 0.0)

    def cut_in(distance, slot):
        return m_ref[slot] // piece_rows == owner_of(distance, ways)

    def upper(distance):
        return 2 * (owner_of(distance, ways) + 1) > ways

    def where_needed(distance, slot, do):
        if slot % 2 == 0:
            do()
        else:
            pl.when(upper(distance))(do)

    m_copy().start()
    for slot in range(slots):

        def fetch(slot=slot):
            for step in reversed(range(tiles)):
                wigner_copy(slot, step).start()
                if slot == 0 and step == last:
                    for half in range(2):
                        beam_copy(0, half).start()
                sky_copy(slot, step).start()

        where_needed(0, slot, fetch)
    for distance in range(1, ways):
        for half in range(2):
            beam_copy(distance, half).start()
        for slot in range(slots):
            where_needed(distance, slot, lambda distance=distance, slot=slot: distant_copy(distance, slot).start())
    m_copy().wait()
    for slot in range(slots):
        info[slot : slot + 1, :] = jnp.full((1, LANES), m_ref[slot].astype(jnp.float32))
    def beam_arrives(distance):
        for half in range(2):
            beam_copy(distance, half).wait()
        for slot in range(slots):
            pl.when(cut_in(distance, slot))(functools.partial(cut, slot))

    beam_arrives(0)

    @pl.loop(0, slots)
    def _(slot):
        begins = begin(0, slot)

        @pl.loop(begins, tiles)
        def _(later):
            step = tiles - 1 - later + begins
            wigner_copy(slot, step).wait()
            span = pl.ds(pl.multiple_of(step * tile, tile), tile)
            fill(own.at[:, span], 0, slot, step)
            sky_copy(slot, step).wait()

        for skipped in range(tiles):

            @pl.when(begins == skipped)
            def _():
                span = slice(skipped * tile, piece_rows)
                part[slot] = jnp.dot(own[:, span], sky_in[slot, span], preferred_element_type=jnp.float32)

        @pl.when(begins == tiles)
        def _():
            part[slot] = jnp.zeros(part.shape[1:], part.dtype)

    for distance in range(1, ways):
        beam_arrives(distance)
        for slot in range(slots):
            where_needed(distance, slot, lambda distance=distance, slot=slot: distant_copy(distance, slot).wait())

        @pl.loop(0, slots)
        def _(slot):
            @pl.loop(begin(distance, slot), tiles)
            def _(step):
                span = pl.ds(pl.multiple_of(step * tile, tile), tile)
                fill(factors.at[distance - 1, slot, :, span], distance, slot, step)

    for slot in range(slots):

        def drop(slot=slot):
            @pl.loop(0, begin(0, slot))
            def _(step):
                wigner_copy(slot, step).wait()
                sky_copy(slot, step).wait()

        where_needed(0, slot, drop)


def crossed(core, outer):
    return (core % 2) * (outer == INNER)


def inner_shift(number):
    return (0, 2, 1, 3)[number]


def ring(place):
    return place ^ (place >> 1)


def device_at(first, second, outer, sign):
    me = lax.axis_index("blk")

    def at(shift, inner):
        group = lax.rem(me // INNER + (sign * shift + outer), outer)
        return group * INNER + ring(lax.rem(ring(lax.rem(me, INNER)) + (sign * inner + INNER), INNER))

    straight = at(second, inner_shift(first))
    if outer != INNER:
        return straight
    return jnp.where(crossed(lax.axis_index("beamk"), outer) == 1, at(first, inner_shift(second)), straight)


def second_kernel(ways, outer, tile, info, _, factors, *refs):
    pieces, refs = refs[: ways - 1], refs[ways - 1 :]
    outs, (acc, turned) = refs[:INNER], refs[INNER:]
    slots, rows, columns = acc.shape
    rows = rows // 2
    piece_rows = pieces[0].shape[1]
    tiles = piece_rows // tile
    width = outs[0].shape[1]
    cycles = outer * INNER
    k_local = width // slots
    pitch = pitch_of(width)

    m_values = [jnp.max(info[slot : slot + 1, :]).astype(jnp.int32) for slot in range(slots)]

    def finish(slot):
        for k in range(k_local):
            span = slice(k * cycles, (k + 1) * cycles)
            total = acc[slot, span] + turn_by_i(acc[slot, rows + k * cycles : rows + (k + 1) * cycles])
            for lane in range(columns // LANES):
                turned[lane, pl.ds(slot * k_local + k, cycles, stride=pitch), :] = total[:, lane * LANES : (lane + 1) * LANES]

    for slot in range(slots):
        for distance in range(1, ways):
            beside = slot > 0 and distance == ways - 1
            missing = first_tile(m_values[slot], owner_of(distance, ways), piece_rows, tile)
            for skipped in range(tiles + (1 if beside else 0)):

                @pl.when(missing == skipped)
                def _():
                    span = slice(skipped * tile, piece_rows)
                    if skipped < tiles:
                        acc[slot] += jnp.dot(
                            factors[distance - 1, slot, :, span],
                            pieces[distance - 1][slot, span],
                            preferred_element_type=jnp.float32,
                        )
                    if beside:
                        finish(slot - 1)

    finish(slots - 1)
    for first in range(INNER):
        for second in range(outer):
            start = device_at(first, second, outer, 1) * pitch
            for lane in range(columns // LANES):
                block = turned[lane, pl.ds(start, width), :].astype(jnp.bfloat16)
                outs[first][second, :, lane * LANES : (lane + 1) * LANES] = block


def regroup_kernel(outer, *refs):
    arrived, onward = refs[:INNER], refs[INNER:]
    for second in range(outer):
        for first in range(INNER):
            onward[second][first] = arrived[first][second]


def place_kernel(outer, *refs):
    arrived, (out, turned, staged, sem) = refs[:outer], refs[outer:]
    k_local, slot_count, columns = staged.shape
    width = arrived[0].shape[1]
    slots = width // k_local
    pitch = pitch_of(slot_count)
    for lane in range(columns // LANES):
        span = slice(lane * LANES, (lane + 1) * LANES)
        for second in range(outer):
            for first in range(INNER):
                block = arrived[second][first, :, span].astype(jnp.float32)
                source = device_at(first, second, outer, -1)
                for slot in range(slots):
                    turned[lane, pl.ds(slots * source + slot, k_local, stride=pitch), :] = block[slot * k_local : (slot + 1) * k_local]
    copies = []
    step = -(-k_local // 4)
    for number, start in enumerate(range(0, k_local, step)):
        end = min(start + step, k_local)
        for k in range(start, end):
            for lane in range(columns // LANES):
                values = turned[lane, k * pitch : k * pitch + slot_count]
                staged[k, :, lane * LANES : (lane + 1) * LANES] = values.astype(staged.dtype)
        copies.append(pltpu.make_async_copy(staged.at[start:end], out.at[start:end], sem.at[number]))
        copies[-1].start()
    for copy in copies:
        copy.wait()


def local(sky, beam, wigner, m_list, *, ways, peers):
    slots, piece_rows, columns = sky.shape
    _, k_local, cycles, degrees = wigner.shape
    rows = k_local * cycles
    tile = tile_of(piece_rows)
    tiles = piece_rows // tile
    lane_tiles = columns // LANES
    width = slots * k_local
    params = pltpu.CompilerParams(vmem_limit_bytes=VMEM_LIMIT)

    pieces = []
    for shift in range(1, ways):
        perm = [(c, (c + shift) % ways) for c in range(ways)]
        pieces.append(pltpu.with_memory_space_constraint(lax.ppermute(sky, "beamk", perm), pltpu.VMEM))
    sky, beam, wigner, m_list = (pltpu.with_memory_space_constraint(x, pltpu.HBM) for x in (sky, beam, wigner, m_list))

    part, factors, info = pl.pallas_call(
        functools.partial(first_kernel, ways, tile),
        out_shape=(
            pltpu.VMEM((slots, 2 * rows, columns), jnp.float32),
            pltpu.VMEM((ways - 1, slots, 2 * rows, piece_rows), jnp.bfloat16),
            pltpu.VMEM((8, LANES), jnp.float32),
        ),
        in_specs=[whole(pltpu.HBM)] * 4,
        out_specs=(whole(pltpu.VMEM),) * 3,
        scratch_shapes=[
            pltpu.SMEM(m_list.shape, jnp.int32),
            pltpu.VMEM((slots, piece_rows, columns), jnp.bfloat16),
            pltpu.VMEM(wigner.shape, jnp.bfloat16),
            pltpu.VMEM((2, k_local, degrees + slots * tile), jnp.float32),
            pltpu.VMEM((2 * rows, piece_rows), jnp.bfloat16),
            pltpu.SemaphoreType.DMA,
            pltpu.SemaphoreType.DMA((slots, tiles)),
            pltpu.SemaphoreType.DMA((slots, tiles)),
            pltpu.SemaphoreType.DMA((ways - 1, slots)),
            pltpu.SemaphoreType.DMA((ways, 2)),
        ],
        compiler_params=params,
        cost_estimate=pl.CostEstimate(
            flops=4 * slots * rows * piece_rows * columns, bytes_accessed=8 * 1024 * 1024, transcendentals=0
        ),
        name="own_half",
    )(m_list, sky, wigner, beam)

    outer = peers // INNER

    def blocks(number):
        return pltpu.VMEM((number, width, columns), jnp.bfloat16)

    *sends, _ = pl.pallas_call(
        functools.partial(second_kernel, ways, outer, tile),
        out_shape=[blocks(outer)] * INNER + [pltpu.VMEM(part.shape, part.dtype)],
        in_specs=[whole(pltpu.VMEM)] * (ways + 2),
        out_specs=[whole(pltpu.VMEM)] * (INNER + 1),
        input_output_aliases={1: INNER},
        scratch_shapes=[
            turning(lane_tiles, cycles, width),
        ],
        compiler_params=params,
        cost_estimate=pl.CostEstimate(
            flops=4 * slots * rows * piece_rows * columns, bytes_accessed=8 * 1024 * 1024, transcendentals=0
        ),
        name="other_half",
    )(info, part, factors, *pieces)

    def send(array, number, step):
        perm = []
        for b in range(peers):
            for core in range(ways):
                over_outer = (step == 0) == bool(crossed(core, outer))
                there = (b + number * INNER) % peers if over_outer else b // INNER * INNER + ring((ring(b % INNER) + inner_shift(number)) % INNER)
                perm.append((b * ways + core, there * ways + core))
        return pltpu.with_memory_space_constraint(lax.ppermute(array, ("blk", "beamk"), perm), pltpu.VMEM)

    first = list(sends)
    for number in range(1, INNER):
        first[number] = send(first[number], number, 0)
    second = list(
        pl.pallas_call(
            functools.partial(regroup_kernel, outer),
            out_shape=[blocks(INNER)] * outer,
            in_specs=[whole(pltpu.VMEM)] * INNER,
            out_specs=[whole(pltpu.VMEM)] * outer,
            compiler_params=params,
            name="regroup",
        )(*first)
    )
    for number in range(1, outer):
        second[number] = send(second[number], number, 1)
    slot_count = slots * peers
    out = pl.pallas_call(
        functools.partial(place_kernel, outer),
        out_shape=pltpu.HBM((k_local, slot_count, columns), jnp.bfloat16),
        in_specs=[whole(pltpu.VMEM)] * outer,
        out_specs=whole(pltpu.HBM),
        scratch_shapes=[
            turning(lane_tiles, k_local, slot_count),
            pltpu.VMEM((k_local, slot_count, columns), jnp.bfloat16),
            pltpu.SemaphoreType.DMA((4,)),
        ],
        compiler_params=params,
        name="place",
    )(*second)
    return out.transpose(1, 0, 2)[None]


def solution(mesh):
    in_specs = (
        P("blk", "beamk", None),
        P("beamk", None, None),
        P("blk", "beamk", None, None),
        P("blk"),
    )
    out_specs = P("blk", None, "beamk", None)
    body = functools.partial(local, ways=mesh.shape["beamk"], peers=mesh.shape["blk"])
    return jax.shard_map(body, mesh=mesh, in_specs=in_specs, out_specs=out_specs, check_vma=False)
```
